128 devices in a mesh: ctx: 16 (over x, z_lo, core), tp: 8 (over z_hi, y).
Axes of the slice: x: 4, y: 4, z: 4 (z_hi: 2, z_lo: 2; z = z_hi * 2 + z_lo), core: 2. Of those that a mesh axis runs over, the one named last changes fastest.
Arguments:
- tokens: bfloat16 [8192, 1024], P(('ctx', 'tp')), may hold values from -6 to 6
- positions: int32 [8192], replicated, may hold values from 0 to 8191, as said below
- sequence_ids: int32 [8192], replicated, may hold values from 0 to 2, as said below
- attn_gain: bfloat16 [1024], P('ctx'), may hold values from 0.099609375 to 1.8984375
- query_weight: bfloat16 [1024, 2048], P('ctx', 'tp'), may hold values from -0.1875 to 0.1875
- key_matrix: bfloat16 [1024, 1024], P('ctx', 'tp'), may hold values from -0.1875 to 0.1875
- value_matrix: bfloat16 [1024, 1024], P('ctx', 'tp'), may hold values from -0.1875 to 0.1875
- query_gain: bfloat16 [128], replicated, may hold values from 0.099609375 to 1.8984375
- key_gain: bfloat16 [128], replicated, may hold values from 0.099609375 to 1.8984375
- output_weight: bfloat16 [2048, 1024], P('tp', 'ctx'), may hold values from -0.5 to 0.5
- mlp_gain: bfloat16 [1024], P('ctx'), may hold values from 0.099609375 to 1.8984375
- gate_weight: bfloat16 [1024, 3072], P('ctx', 'tp'), may hold values from -0.1875 to 0.1875
- up_weight: bfloat16 [1024, 3072], P('ctx', 'tp'), may hold values from -0.1875 to 0.1875
- down_weight: bfloat16 [3072, 1024], P('tp', 'ctx'), may hold values from -0.109375 to 0.109375
- out_grad: bfloat16 [8192, 1024], P(('ctx', 'tp')), may hold values from -6 to 6
Outputs:
- output: bfloat16 [8192, 1024], P(('ctx', 'tp'))
- token_grad: float32 [8192, 1024], P(('ctx', 'tp'))
- attn_gain_grad: float32 [1024], P('ctx')
- query_weight_grad: float32 [1024, 2048], P('ctx', 'tp')
- key_weight_grad: float32 [1024, 1024], P('ctx', 'tp')
- value_weight_grad: float32 [1024, 1024], P('ctx', 'tp')
- query_gain_grad: float32 [128], replicated
- key_gain_grad: float32 [128], replicated
- output_weight_grad: float32 [2048, 1024], P('tp', 'ctx')
- mlp_gain_grad: float32 [1024], P('ctx')
- gate_weight_grad: float32 [1024, 3072], P('ctx', 'tp')
- up_weight_grad: float32 [1024, 3072], P('ctx', 'tp')
- down_weight_grad: float32 [3072, 1024], P('tp', 'ctx')
The draws below stay inside these ranges and needn't reach their ends.
Inputs may be any that keep to these rules, and one draw needn't show every extreme that they name: `positions`: along the tokens sequence_ids never fall, and where two neighbouring tokens have the same id the later position is one more than the earlier. Id 1 begins within the first 256 tokens and ends within the last 256; id 2 begins at position 0. `sequence_ids`: ids never fall along the tokens; all three occur.
All inputs are finite; a program needn't handle non-finite values.
Results may differ from the reference program's by a relative error of at most 0.025.
Values may be sent and summed in bfloat16 or wider, within the bound.
No kernel may reach another device: no remote copies, remote signals or barrier semaphores. Data moves between devices by JAX's collectives and lax.ppermute only.
A program may use at most 64 MiB of HBM per device.

```python
from functools import partial
import jax
import jax.numpy as jnp
from jax import lax

MODEL_WIDTH = 1024
QUERY_HEADS = 16
KEY_VALUE_HEADS = 8
HEAD_WIDTH = 128
FF = 3072
STRETCH = 512
STREAM_TOKENS = 8192
N_CTX = 16


def layout(key):
    all_rows = STRETCH * N_CTX
    head_len = jax.random.randint(jax.random.fold_in(key, 11), (), 1, STRETCH // 2 + 1)
    tail_len = jax.random.randint(jax.random.fold_in(key, 12), (), 1, STRETCH // 2 + 1)
    first_offset = jax.random.randint(jax.random.fold_in(key, 13), (), 0, STRETCH)
    places = jnp.arange(all_rows, dtype=jnp.int32)
    tail_start = all_rows - tail_len
    sequence_ids = (places >= head_len).astype(jnp.int32) + (places >= tail_start).astype(jnp.int32)
    begin = jnp.where(sequence_ids == 0, 0, jnp.where(sequence_ids == 1, head_len, tail_start))
    offset = jnp.where(sequence_ids == 0, first_offset, jnp.where(sequence_ids == 1, head_len + tail_len, 0))
    return (sequence_ids, (offset + places - begin).astype(jnp.int32))


def draw_positions(key, part):
    return layout(key)[1]


def draw_sequence_ids(key, part):
    return layout(key)[0]


def shard_levels(stream_key, dims, shards, least, high):
    loudness = 1.0
    for axis_at, blocks in shards:
        heights = jax.random.uniform(jax.random.fold_in(jax.random.fold_in(stream_key, 6), axis_at), (blocks,), jnp.float32, least / len(shards), high / len(shards))
        loudness = loudness * jnp.repeat(jnp.exp(heights), dims[axis_at] // blocks).reshape((-1,) + (1,) * (len(dims) - 1 - axis_at))
    return loudness


def scatter_about(own_key, shape, scale, reach, pieces=(), kind=jnp.bfloat16):
    drawn = jax.random.normal(own_key, shape, jnp.float32) * scale
    if len(pieces) > 0:
        drawn = shard_levels(own_key, shape, pieces, -0.22, 0.18) * drawn
    return jnp.clip(drawn, min=-reach, max=reach).astype(kind)


def setup_inputs(seed: int = 0) -> dict:
    streams_of = jax.random.split(jax.random.key(seed), 16)
    tokens = scatter_about(streams_of[0], (STREAM_TOKENS, MODEL_WIDTH), 1.0, 6.0, ((0, 128),))
    positions = draw_positions(jax.random.fold_in(streams_of[15], 71), 0)
    sequence_ids = draw_sequence_ids(jax.random.fold_in(streams_of[15], 71), 0)
    attn_gain = jnp.clip(1.0 + 0.18 * jax.random.normal(streams_of[3], (MODEL_WIDTH,), jnp.float32), 0.099609375, 1.8984375).astype(jnp.bfloat16)
    query_weight = scatter_about(streams_of[4], (MODEL_WIDTH, QUERY_HEADS * HEAD_WIDTH), MODEL_WIDTH ** -0.5, 0.1875, ((0, 16), (1, 8)))
    key_matrix = scatter_about(streams_of[5], (MODEL_WIDTH, KEY_VALUE_HEADS * HEAD_WIDTH), MODEL_WIDTH ** -0.5, 0.1875, ((0, 16), (1, 8)))
    value_matrix = scatter_about(streams_of[6], (MODEL_WIDTH, KEY_VALUE_HEADS * HEAD_WIDTH), MODEL_WIDTH ** -0.5, 0.1875, ((0, 16), (1, 8)))
    query_gain = jnp.clip(1.0 + 0.18 * jax.random.normal(streams_of[7], (HEAD_WIDTH,), jnp.float32), 0.099609375, 1.8984375).astype(jnp.bfloat16)
    key_gain = jnp.clip(1.0 + 0.18 * jax.random.normal(streams_of[8], (HEAD_WIDTH,), jnp.float32), 0.099609375, 1.8984375).astype(jnp.bfloat16)
    output_weight = scatter_about(streams_of[9], (QUERY_HEADS * HEAD_WIDTH, MODEL_WIDTH), (QUERY_HEADS * HEAD_WIDTH // 16) ** -0.5, 0.5, ((0, 8), (1, 16)))
    mlp_gain = jnp.clip(1.0 + 0.18 * jax.random.normal(streams_of[10], (MODEL_WIDTH,), jnp.float32), 0.099609375, 1.8984375).astype(jnp.bfloat16)
    gate_weight = scatter_about(streams_of[11], (MODEL_WIDTH, FF), MODEL_WIDTH ** -0.5, 0.1875, ((0, 16), (1, 8)))
    up_weight = scatter_about(streams_of[12], (MODEL_WIDTH, FF), MODEL_WIDTH ** -0.5, 0.1875, ((0, 16), (1, 8)))
    down_weight = scatter_about(streams_of[13], (FF, MODEL_WIDTH), FF ** -0.5, 0.109375, ((0, 8), (1, 16)))
    out_grad = scatter_about(streams_of[14], (STREAM_TOKENS, MODEL_WIDTH), 1.0, 6.0, ((0, 128),))
    return dict(tokens=tokens, positions=positions, sequence_ids=sequence_ids, attn_gain=attn_gain, query_weight=query_weight, key_matrix=key_matrix, value_matrix=value_matrix, query_gain=query_gain, key_gain=key_gain, output_weight=output_weight, mlp_gain=mlp_gain, gate_weight=gate_weight, up_weight=up_weight, down_weight=down_weight, out_grad=out_grad)


@jax.custom_vjp
def lower_precision(v):
    return lax.optimization_barrier(v.astype(jnp.bfloat16)).astype(jnp.float32)

@jax.custom_vjp
def lower_precision_back(v):
    return v

def low_keep(v):
    return (lower_precision(v), None)

def low_pass(kept, grad):
    return (grad,)

def back_keep(v):
    return (v, None)

def back_low(kept, grad):
    return (lower_precision(grad),)
lower_precision.defvjp(low_keep, low_pass)
lower_precision_back.defvjp(back_keep, back_low)
epsilon = 1e-06
rope_base = 1000000.0
masked_value = -1e+30

def matrix_product(left, right):
    return jnp.dot(left, right, precision=lax.Precision.HIGHEST)

def rms_scale(value_tensor, gain_vector):
    return value_tensor * lax.rsqrt(lax.optimization_barrier(jnp.mean(value_tensor * value_tensor, axis=-1, keepdims=True)) + epsilon) * gain_vector

def rope_tables(places, head_size):
    half_size = head_size // 2
    frequency = jnp.exp(-jnp.log(rope_base) * 2.0 * jnp.arange(half_size, dtype=jnp.float32) / head_size)
    angles = places.astype(jnp.float32)[:, None] * frequency[None, :]
    return (jnp.cos(angles)[:, None, :], jnp.sin(angles)[:, None, :])

def rotate(value_tensor, cosine_table, sine_table):
    half_size = value_tensor.shape[-1] // 2
    first_half = value_tensor[..., :half_size]
    second_half = value_tensor[..., half_size:]
    return jnp.concatenate([first_half * cosine_table - second_half * sine_table, second_half * cosine_table + first_half * sine_table], axis=-1)

def attention(query_rows, keys, value_tensor, places, sequence_ids):
    document_span_rows = min(512, STREAM_TOKENS)
    count_of_blocks = STREAM_TOKENS // document_span_rows
    grouped_heads = QUERY_HEADS // KEY_VALUE_HEADS
    score_scale = HEAD_WIDTH ** (-0.5)
    blocked_queries = query_rows.reshape(count_of_blocks, document_span_rows, KEY_VALUE_HEADS, grouped_heads, HEAD_WIDTH)
    place_blocks = places.reshape(count_of_blocks, document_span_rows)
    id_blocks = sequence_ids.reshape(count_of_blocks, document_span_rows)

    def one_block(inputs):
        query_block, query_places, query_ids = inputs
        scores = jnp.einsum('qhgd,khd->hgqk', query_block, keys, precision=lax.Precision.HIGHEST) * score_scale
        scores = lower_precision_back(scores)
        allowed = (sequence_ids[None, :] == query_ids[:, None]) & (places[None, :] <= query_places[:, None])
        masked = jnp.where(allowed, scores, masked_value)
        largest = lax.optimization_barrier(jnp.max(masked, axis=-1, keepdims=True))
        weights = jnp.where(allowed, jnp.exp(masked - largest), 0.0)
        probabilities = lower_precision(weights / lax.optimization_barrier(jnp.sum(weights, axis=-1, keepdims=True)))
        result = jnp.einsum('hgqk,khd->qhgd', probabilities, value_tensor, precision=lax.Precision.HIGHEST)
        return result.reshape(document_span_rows, QUERY_HEADS * HEAD_WIDTH)
    mapped = lax.map(jax.checkpoint(one_block), (blocked_queries, place_blocks, id_blocks))
    return mapped.reshape(STREAM_TOKENS, QUERY_HEADS * HEAD_WIDTH)

def layer(places, sequence_ids, tokens, attn_gain, query_weight, key_matrix, value_matrix, query_gain, key_gain, output_weight, mlp_gain, gate_weight, up_weight, down_weight):
    first_normed = lower_precision(rms_scale(tokens, attn_gain))
    query_raw = lower_precision_back(matrix_product(first_normed, query_weight)).reshape(STREAM_TOKENS, QUERY_HEADS, HEAD_WIDTH)
    unrotated_key = lower_precision_back(matrix_product(first_normed, key_matrix)).reshape(STREAM_TOKENS, KEY_VALUE_HEADS, HEAD_WIDTH)
    value_tensor = lower_precision(lower_precision_back(matrix_product(first_normed, value_matrix))).reshape(STREAM_TOKENS, KEY_VALUE_HEADS, HEAD_WIDTH)
    cosine_table, sine_table = rope_tables(places, HEAD_WIDTH)
    query_rows = lower_precision(rotate(rms_scale(query_raw, query_gain), cosine_table, sine_table))
    keys = lower_precision(rotate(rms_scale(unrotated_key, key_gain), cosine_table, sine_table))
    attended = lower_precision(lower_precision_back(attention(query_rows, keys, value_tensor, places, sequence_ids)))
    hidden = tokens + lower_precision_back(matrix_product(attended, output_weight))
    normed_two = lower_precision(rms_scale(hidden, mlp_gain))
    gate_proj = lower_precision_back(matrix_product(normed_two, gate_weight))
    up_proj = lower_precision_back(matrix_product(normed_two, up_weight))
    active = lower_precision(jax.nn.silu(gate_proj) * up_proj)
    return hidden + lower_precision_back(matrix_product(active, down_weight))

def reference(tokens, positions, sequence_ids, attn_gain, query_weight, key_matrix, value_matrix, query_gain, key_gain, output_weight, mlp_gain, gate_weight, up_weight, down_weight, out_grad):
    floats = [array.astype(jnp.float32) for array in (tokens, attn_gain, query_weight, key_matrix, value_matrix, query_gain, key_gain, output_weight, mlp_gain, gate_weight, up_weight, down_weight)]
    result, pullback = jax.vjp(partial(layer, positions, sequence_ids), *floats)
    grads = pullback(out_grad.astype(jnp.float32))
    return (result.astype(jnp.bfloat16), grads[0], grads[1], grads[2], grads[3], grads[4], grads[5], grads[6], grads[7], grads[8], grads[9], grads[10], grads[11])
```

```python
import jax
import jax.numpy as jnp
from jax import lax
from jax.experimental import pallas as pl
from jax.experimental.pallas import tpu as pltpu
from jax.sharding import Mesh, PartitionSpec as P

AXES = ("x", "zl", "core", "zh", "y")
EPS = 1e-06
ROPE_BASE = 1000000.0
HEAD = 128
RUN = 256
GROUP = 512
KEYS = 512
N_BLOCKS = 16
LOG2E = 1.4426950408889634
LN2 = 0.6931471805599453
Q_SCALE = LOG2E * HEAD ** (-0.5)
BF = jnp.bfloat16
F32 = jnp.float32
VMEM_LIMIT = 60 * 1024 * 1024


def swap_with(value, axis, mask):
    if axis == "z":
        return lax.ppermute(value, ("zl", "zh"), [(i, i ^ mask) for i in range(4)])
    size = 2 if axis == "core" else 4
    return lax.ppermute(value, axis, [(i, i ^ mask) for i in range(size)])


def transpose_core_zh(value):
    return lax.ppermute(value, ("core", "zh"), [(0, 0), (1, 2), (2, 1), (3, 3)])


def gather_axis(value, axis):
    return jnp.stack([value] + [swap_with(value, axis, m) for m in (1, 2, 3)])


def scatter_axis(parts, axis):
    total = parts[0].astype(F32)
    for m in (1, 2, 3):
        total = total + swap_with(parts[m].astype(BF), axis, m).astype(F32)
    return total


def gather_plane(block, cut):
    first = gather_axis(gather_axis(block[:, :cut], "x"), "z")
    second = gather_axis(gather_axis(block[:, cut:], "z"), "x")
    first = jnp.swapaxes(first, 0, 1).reshape(1024, cut)
    second = second.reshape(1024, block.shape[1] - cut)
    return jnp.concatenate([first, second], axis=1)


def scatter_plane(total, cut):
    columns = total.shape[1]
    first = total[:, :cut].reshape(4, 256, cut)
    second = total[:, cut:].reshape(4, 4, 64, columns - cut)
    first = scatter_axis([first[m] for m in range(4)], "x").reshape(4, 64, cut)
    second = scatter_axis([second[:, m] for m in range(4)], "z")
    first = scatter_axis([first[m] for m in range(4)], "z")
    second = scatter_axis([second[m] for m in range(4)], "x")
    return jnp.concatenate([first, second], axis=1)


def gather_rows(block):
    half = jnp.concatenate([block] + [swap_with(block, "y", m) for m in (1, 2, 3)], axis=0)
    return jnp.concatenate([half, swap_with(half, "core", 1)], axis=0)


def scatter_rows(partial):
    half = partial[:RUN].astype(F32) + swap_with(partial[RUN:], "core", 1).astype(F32)
    half = half.reshape(4, 64, partial.shape[1])
    return scatter_axis([half[m] for m in range(4)], "y")


def reorder(value, place):
    lanes = lax.broadcasted_iota(jnp.int32, value.shape, 1)
    for bit, width in enumerate((64, 128, 256, 512)):
        swapped = jnp.where(
            (lanes & width) != 0, jnp.roll(value, width, 1), jnp.roll(value, -width, 1)
        )
        value = jnp.where(((place >> bit) & 1) == 1, swapped, value)
    return value


def rms_parts(value):
    inverse = lax.rsqrt(jnp.mean(value * value, axis=-1, keepdims=True) + EPS)
    return value * inverse, inverse


def rms_back(scaled, normal, inverse):
    return inverse * (scaled - normal * jnp.mean(scaled * normal, axis=-1, keepdims=True))


def rotate(value, cosine, sine):
    first, second = value[:, : HEAD // 2], value[:, HEAD // 2 :]
    return jnp.concatenate(
        [first * cosine - second * sine, second * cosine + first * sine], axis=-1
    )


def dot(left, right, contract):
    return lax.dot_general(left, right, (contract, ((), ())), preferred_element_type=F32)


NN = ((1,), (0,))
NT = ((1,), (1,))
TN = ((0,), (0,))


def stream_index(spot, yi):
    return (((spot >> 6) ^ yi) << 6) | (spot & 63)


def load_keys(info, key_parts, value_parts, key_all, value_all, sems):
    xi, zl, zh, co = info[0], info[1], info[2], info[3]
    copies = []
    for turn in range(4):
        for sub in range(4):
            for kind in range(2):
                mx, mz = (sub, turn) if kind == 0 else (turn, sub)
                run = (((xi ^ mx) * 2 + (zl ^ (mz >> 1))) * 2 + co) * 2 + (zh ^ (mz & 1))
                source = (key_parts if kind == 0 else value_parts)[turn]
                target = key_all if kind == 0 else value_all
                for half in range(2):
                    row = (run ^ (2 * half)) * RUN
                    copies.append(
                        pltpu.make_async_copy(
                            source.at[pl.ds(sub * GROUP + half * RUN, RUN)],
                            target.at[pl.ds(pl.multiple_of(row, RUN), RUN)],
                            sems.at[(turn * 4 + sub) * 4 + kind * 2 + half],
                        )
                    )
    for copy in copies:
        copy.start()
    for copy in copies:
        copy.wait()


def first_of(token, start_one, start_two):
    return jnp.where(
        token >= start_two, start_two, jnp.where(token >= start_one, start_one, 0)
    )


def attention_kernel(
    info, query, k0, k1, k2, k3, v0, v1, v2, v3, out, sums, key_all, value_all, totals, sems
):
    load_keys(info, (k0, k1, k2, k3), (v0, v1, v2, v3), key_all, value_all, sems)
    xi, zl, zh, co, yi = (info[i] for i in range(5))
    start_one, start_two = info[5], info[6]
    group = xi * 2 + zl
    last_full = group * 2
    ones = jnp.ones((KEYS, HEAD), BF)
    row_iota = lax.broadcasted_iota(jnp.int32, (RUN, 1), 0)
    row_tokens = [
        ((group * 2 + (co ^ half)) * 2 + zh) * RUN + stream_index(row_iota, yi)
        for half in range(2)
    ]
    row_starts = [first_of(token, start_one, start_two) for token in row_tokens]
    totals[...] = jnp.zeros_like(totals)

    def block(index, masked):
        rows = pl.ds(pl.multiple_of(index * KEYS, KEYS), KEYS)
        keys = key_all[rows, :]
        values = jnp.concatenate([value_all[rows, :], ones], axis=1)
        spot = lax.broadcasted_iota(jnp.int32, (1, KEYS), 1)
        key_tokens = index * KEYS + (spot & ~(RUN - 1)) + stream_index(spot & (RUN - 1), yi)
        for half in range(2):
            for head in range(2):
                rows_here = slice(half * RUN, (half + 1) * RUN)
                scores = dot(query[rows_here, head * HEAD : (head + 1) * HEAD], keys, NT)
                weights = jnp.exp2(scores)
                if masked:
                    allowed = (key_tokens <= row_tokens[half]) & (key_tokens >= row_starts[half])
                    weights = jnp.where(allowed, weights, 0.0)
                totals[half * 2 + head] += dot(weights.astype(BF), values, NN)

    def full(index, carry):
        block(index, False)
        return carry

    lax.fori_loop(1, last_full, full, 0)
    for half in range(2):
        keep = row_starts[half] <= KEYS
        for head in range(2):
            totals[half * 2 + head] = jnp.where(keep, totals[half * 2 + head], 0.0)
    block(jnp.int32(0), True)

    @pl.when(last_full > 0)
    def _():
        block(last_full, True)

    block(last_full + 1, True)
    for half in range(2):
        for head in range(2):
            total = totals[half * 2 + head]
            weight_sum = total[:, HEAD:]
            out[half * RUN : (half + 1) * RUN, head * HEAD : (head + 1) * HEAD] = (
                total[:, :HEAD] / weight_sum
            ).astype(BF)
            sums[half * 2 + head] = jnp.log2(weight_sum).T[:8]


def attention_forward(info, query, key_parts, value_parts):
    any_space = pl.BlockSpec(memory_space=pl.ANY)
    vmem = pl.BlockSpec(memory_space=pltpu.VMEM)
    return pl.pallas_call(
        attention_kernel,
        out_shape=(
            jax.ShapeDtypeStruct((GROUP, 2 * HEAD), BF),
            jax.ShapeDtypeStruct((4, 8, RUN), F32),
        ),
        in_specs=[pl.BlockSpec(memory_space=pltpu.SMEM), vmem] + [any_space] * 8,
        out_specs=(vmem, vmem),
        scratch_shapes=[
            pltpu.VMEM((N_BLOCKS * KEYS, HEAD), BF),
            pltpu.VMEM((N_BLOCKS * KEYS, HEAD), BF),
            pltpu.VMEM((4, RUN, 2 * HEAD), F32),
            pltpu.SemaphoreType.DMA((64,)),
        ],
        compiler_params=pltpu.CompilerParams(vmem_limit_bytes=VMEM_LIMIT),
        name="attention_forward",
    )(info, query, *key_parts, *value_parts)


def attention_back_kernel(
    info,
    query,
    grad,
    sums,
    deltas,
    k0,
    k1,
    k2,
    k3,
    v0,
    v1,
    v2,
    v3,
    grad_query,
    grad_key,
    grad_value,
    key_all,
    value_all,
    totals,
    sems,
):
    load_keys(info, (k0, k1, k2, k3), (v0, v1, v2, v3), key_all, value_all, sems)
    xi, zl, zh, co, yi = (info[i] for i in range(5))
    start_one, start_two = info[5], info[6]
    group = xi * 2 + zl
    last_full = group * 2
    column_iota = lax.broadcasted_iota(jnp.int32, (1, RUN), 1)
    row_tokens = [
        ((group * 2 + (co ^ half)) * 2 + zh) * RUN + stream_index(column_iota, yi)
        for half in range(2)
    ]
    row_starts = [first_of(token, start_one, start_two) for token in row_tokens]
    totals[...] = jnp.zeros_like(totals)

    def places(index):
        owner, owner_core = index // 2, index % 2
        mx = (owner // 2) ^ xi
        half = owner_core ^ co
        spots = []
        for run in range(2):
            mz = ((owner % 2) ^ zl) * 2 + (run ^ zh)
            spots.append((mx, mz, half))
        return spots

    def store(index, key_grad, value_grad):
        for run, (mx, mz, half) in enumerate(places(index)):
            rows = slice(run * RUN, (run + 1) * RUN)
            key_row = (mz * 4 + mx) * GROUP + half * RUN
            value_row = (mx * 4 + mz) * GROUP + half * RUN
            grad_key[pl.ds(pl.multiple_of(key_row, RUN), RUN), :] = key_grad[rows]
            grad_value[pl.ds(pl.multiple_of(value_row, RUN), RUN), :] = value_grad[rows]

    def block(index, masked):
        rows = pl.ds(pl.multiple_of(index * KEYS, KEYS), KEYS)
        keys = key_all[rows, :]
        values = value_all[rows, :]
        spot = lax.broadcasted_iota(jnp.int32, (KEYS, 1), 0)
        key_tokens = index * KEYS + (spot & ~(RUN - 1)) + stream_index(spot & (RUN - 1), yi)
        key_grad = jnp.zeros((KEYS, HEAD), F32)
        value_grad = jnp.zeros((KEYS, HEAD), F32)
        for half in range(2):
            for head in range(2):
                rows_here = slice(half * RUN, (half + 1) * RUN)
                lanes = slice(head * HEAD, (head + 1) * HEAD)
                queries = query[rows_here, lanes]
                grads = grad[rows_here, lanes]
                level = sums[half * 2 + head, 0:1, :]
                if not masked:
                    level = jnp.where(row_starts[half] <= KEYS, level, 1e30)
                probs = jnp.exp2(dot(keys, queries, NT) - level)
                if masked:
                    allowed = (key_tokens <= row_tokens[half]) & (key_tokens >= row_starts[half])
                    probs = jnp.where(allowed, probs, 0.0)
                grad_probs = dot(values, grads, NT)
                grad_scores = (probs * (grad_probs - deltas[half * 2 + head, 0:1, :])).astype(BF)
                value_grad = value_grad + dot(probs.astype(BF), grads, NN)
                key_grad = key_grad + dot(grad_scores, queries, NN)
                totals[half * 2 + head] += dot(grad_scores, keys, TN)
        store(index, (key_grad * LN2).astype(BF), value_grad.astype(BF))

    def full(index, carry):
        block(index, False)
        return carry

    lax.fori_loop(1, last_full, full, 0)
    block(jnp.int32(0), True)

    @pl.when(last_full > 0)
    def _():
        block(last_full, True)

    block(last_full + 1, True)

    def empty(index, carry):
        nothing = jnp.zeros((KEYS, HEAD), BF)
        store(index, nothing, nothing)
        return carry

    lax.fori_loop(last_full + 2, N_BLOCKS, empty, 0)
    for half in range(2):
        for head in range(2):
            grad_query[half * RUN : (half + 1) * RUN, head * HEAD : (head + 1) * HEAD] = (
                totals[half * 2 + head] * HEAD ** (-0.5)
            )


def attention_back(info, query, grad, sums, deltas, key_parts, value_parts):
    any_space = pl.BlockSpec(memory_space=pl.ANY)
    vmem = pl.BlockSpec(memory_space=pltpu.VMEM)
    return pl.pallas_call(
        attention_back_kernel,
        out_shape=(
            jax.ShapeDtypeStruct((GROUP, 2 * HEAD), F32),
            jax.ShapeDtypeStruct((N_BLOCKS * KEYS, HEAD), BF),
            jax.ShapeDtypeStruct((N_BLOCKS * KEYS, HEAD), BF),
        ),
        in_specs=[pl.BlockSpec(memory_space=pltpu.SMEM)] + [vmem] * 4 + [any_space] * 8,
        out_specs=(vmem, vmem, vmem),
        scratch_shapes=[
            pltpu.VMEM((N_BLOCKS * KEYS, HEAD), BF),
            pltpu.VMEM((N_BLOCKS * KEYS, HEAD), BF),
            pltpu.VMEM((4, RUN, HEAD), F32),
            pltpu.SemaphoreType.DMA((64,)),
        ],
        compiler_params=pltpu.CompilerParams(vmem_limit_bytes=VMEM_LIMIT),
        name="attention_back",
    )(info, query, grad, sums, deltas, *key_parts, *value_parts)


def local(
    tokens,
    positions,
    sequence_ids,
    attn_gain,
    query_weight,
    key_matrix,
    value_matrix,
    query_gain,
    key_gain,
    output_weight,
    mlp_gain,
    gate_weight,
    up_weight,
    down_weight,
    out_grad,
):
    xi, zl, co, zh, yi = (lax.axis_index(name) for name in AXES)
    place = xi * 4 + zl * 2 + zh
    start_one = jnp.sum(sequence_ids < 1, dtype=jnp.int32)
    start_two = jnp.sum(sequence_ids < 2, dtype=jnp.int32)
    info = jnp.stack([xi, zl, zh, co, yi, start_one, start_two]).astype(jnp.int32)

    gain_one = attn_gain.astype(F32)[:, None]
    gain_two = mlp_gain.astype(F32)[:, None]

    def scaled(weight, gain):
        return (weight.astype(F32) * gain).astype(BF)

    weights_one = jnp.concatenate(
        [
            scaled(query_weight, gain_one),
            scaled(key_matrix, gain_one),
            scaled(value_matrix, gain_one),
            output_weight.T,
        ],
        axis=1,
    )
    weights_two = jnp.concatenate(
        [scaled(gate_weight, gain_two), scaled(up_weight, gain_two), down_weight.T], axis=1
    )
    full_one = gather_plane(transpose_core_zh(weights_one), 384)

    resid = reorder(tokens.astype(F32), place)
    cotangent = reorder(out_grad.astype(F32), place)
    normal_one, inverse_one = rms_parts(resid)
    rows_one = gather_rows(normal_one.astype(BF))
    grad_rows = gather_rows(cotangent.astype(BF))

    run_places = positions.reshape(8, 2, 2, 4, 64)
    run_places = lax.dynamic_index_in_dim(run_places, xi * 2 + zl, 0, False)
    run_places = lax.dynamic_index_in_dim(run_places, zh, 1, False)
    run_places = jnp.where(co == 1, run_places[::-1], run_places)
    run_places = jnp.where((yi & 1) == 1, run_places[:, jnp.array([1, 0, 3, 2])], run_places)
    run_places = jnp.where((yi & 2) == 2, run_places[:, jnp.array([2, 3, 0, 1])], run_places)
    half_size = HEAD // 2
    frequency = jnp.exp(
        -jnp.log(ROPE_BASE) * 2.0 * jnp.arange(half_size, dtype=F32) / HEAD
    )
    angles = run_places.reshape(GROUP).astype(F32)[:, None] * frequency[None, :]
    cosine, sine = jnp.cos(angles), jnp.sin(angles)
    gain_query = query_gain.astype(F32)
    gain_key = key_gain.astype(F32)
    query_key_value = dot(rows_one, full_one[:, :512], NN)
    normals = [rms_parts(query_key_value[:, i * HEAD : (i + 1) * HEAD]) for i in range(3)]
    query = jnp.concatenate(
        [rotate(normals[i][0] * gain_query, cosine, sine) * Q_SCALE for i in range(2)], axis=1
    ).astype(BF)
    key = rotate(normals[2][0] * gain_key, cosine, sine).astype(BF)
    value = query_key_value[:, 3 * HEAD :].astype(BF)

    key_own = gather_axis(key, "x").reshape(4 * GROUP, HEAD)
    value_own = gather_axis(value, "z").reshape(4 * GROUP, HEAD)
    key_parts = [key_own] + [swap_with(key_own, "z", m) for m in (1, 2, 3)]
    value_parts = [value_own] + [swap_with(value_own, "x", m) for m in (1, 2, 3)]
    weights_two, key_parts, value_parts = lax.optimization_barrier(
        (weights_two, key_parts, value_parts)
    )
    full_two = gather_plane(transpose_core_zh(weights_two), 576)

    attended, sums = attention_forward(info, query, key_parts, value_parts)
    output_full = full_one[:, 512:]
    hidden = resid + scatter_rows(dot(attended, output_full, NT).astype(BF))
    normal_two, inverse_two = rms_parts(hidden)
    rows_two = gather_rows(normal_two.astype(BF))

    gate_up_full, down_full = full_two[:, :768], full_two[:, 768:]
    gate_up = dot(rows_two, gate_up_full, NN)
    gate, up = gate_up[:, :384], gate_up[:, 384:]
    sigmoid = jax.nn.sigmoid(gate)
    swish = gate * sigmoid
    active = (swish * up).astype(BF)
    grad_active = dot(grad_rows, down_full, NN)
    grad_gate_up = jnp.concatenate(
        [
            (grad_active * up * sigmoid * (1.0 + gate * (1.0 - sigmoid))).astype(BF),
            (grad_active * swish).astype(BF),
        ],
        axis=1,
    )
    scaled_two = scatter_rows(dot(grad_gate_up, gate_up_full, NT).astype(BF))
    grad_hidden = cotangent + rms_back(scaled_two, normal_two, inverse_two)
    grad_rows_one = gather_rows(grad_hidden.astype(BF))
    output = hidden + scatter_rows(dot(active, down_full, NT).astype(BF))
    output = reorder(output, place).astype(BF)
    down_grad = dot(grad_rows, active, TN)
    gate_up_grad = dot(rows_two, grad_gate_up, TN)
    two_grad = jnp.concatenate([gate_up_grad.astype(BF), down_grad.astype(BF)], axis=1)
    two_own = scatter_plane(two_grad, 576)

    grad_attended = dot(grad_rows_one, output_full, NN).astype(BF)
    products = grad_attended.astype(F32) * attended.astype(F32)
    deltas = jnp.stack(
        [
            jnp.sum(products[half * RUN : (half + 1) * RUN, head * HEAD : (head + 1) * HEAD], axis=1)
            for half in range(2)
            for head in range(2)
        ]
    )
    deltas = jnp.broadcast_to(deltas[:, None, :], (4, 8, RUN))
    grad_query, grad_key, grad_value = attention_back(
        info, query, grad_attended, sums, deltas, key_parts, value_parts
    )
    output_grad = dot(grad_rows_one, attended, TN).astype(BF)
    grad_key = scatter_axis(
        [grad_key[m * 4 * GROUP : (m + 1) * 4 * GROUP] for m in range(4)], "z"
    )
    grad_value = scatter_axis(
        [grad_value[m * 4 * GROUP : (m + 1) * 4 * GROUP] for m in range(4)], "x"
    )
    grad_key = scatter_axis([grad_key[m * GROUP : (m + 1) * GROUP] for m in range(4)], "x")
    grad_value = scatter_axis([grad_value[m * GROUP : (m + 1) * GROUP] for m in range(4)], "z")

    def head_back(gradient, gain, normal, inverse):
        turned = rotate(gradient, cosine, -sine)
        part = jnp.sum(turned * normal, axis=0)
        return rms_back(turned * gain, normal, inverse).astype(BF), part

    grad_head_one, part_one = head_back(grad_query[:, :HEAD], gain_query, *normals[0])
    grad_head_two, part_two = head_back(grad_query[:, HEAD:], gain_query, *normals[1])
    grad_key_raw, part_key = head_back(grad_key, gain_key, *normals[2])
    grad_raw = jnp.concatenate(
        [grad_head_one, grad_head_two, grad_key_raw, grad_value.astype(BF)], axis=1
    )
    scaled_one = scatter_rows(dot(grad_raw, full_one[:, :512], NT).astype(BF))
    token_grad = grad_hidden + rms_back(scaled_one, normal_one, inverse_one)
    token_grad = reorder(token_grad, place)
    raw_grad = dot(rows_one, grad_raw, TN).astype(BF)
    one_own = scatter_plane(jnp.concatenate([raw_grad, output_grad], axis=1), 384)

    one_own = transpose_core_zh(one_own.astype(BF)).astype(F32)
    two_own = transpose_core_zh(two_own.astype(BF)).astype(F32)
    query_part, key_part, value_part = one_own[:, :256], one_own[:, 256:384], one_own[:, 384:512]
    gate_part, up_part = two_own[:, :384], two_own[:, 384:768]
    attn_part = (
        jnp.sum(query_part * query_weight.astype(F32), axis=1)
        + jnp.sum(key_part * key_matrix.astype(F32), axis=1)
        + jnp.sum(value_part * value_matrix.astype(F32), axis=1)
    )
    mlp_part = jnp.sum(
        gate_part * gate_weight.astype(F32) + up_part * up_weight.astype(F32), axis=1
    )
    gain_parts = jnp.concatenate([attn_part, mlp_part])
    head_parts = jnp.concatenate([part_one + part_two, part_key])

    def total_over(vector, axis, masks):
        received = [swap_with(vector, axis, m) for m in masks]
        for part in received:
            vector = vector + part
        return vector

    gain_parts = total_over(total_over(gain_parts, "y", (1, 2, 3)), "z", (1,))
    head_parts = total_over(head_parts, "core", (1,))
    head_parts = total_over(head_parts, "y", (1, 2, 3))
    head_parts = total_over(head_parts, "x", (1, 2, 3))
    head_parts = total_over(head_parts, "z", (1, 2, 3))
    return (
        output,
        token_grad,
        gain_parts[:64],
        query_part * gain_one,
        key_part * gain_one,
        value_part * gain_one,
        head_parts[:HEAD],
        head_parts[HEAD:],
        one_own[:, 512:].T,
        gain_parts[64:],
        gate_part * gain_two,
        up_part * gain_two,
        two_own[:, 768:].T,
    )


def solution(mesh):
    parts = Mesh(mesh.devices.reshape(4, 2, 2, 2, 4), AXES)
    ctx, tp = ("x", "zl", "core"), ("zh", "y")
    tokens, matrix, turned = P(AXES, None), P(ctx, tp), P(tp, ctx)
    return jax.shard_map(
        local,
        mesh=parts,
        in_specs=(
            tokens,
            P(),
            P(),
            P(ctx),
            matrix,
            matrix,
            matrix,
            P(),
            P(),
            turned,
            P(ctx),
            matrix,
            matrix,
            turned,
            tokens,
        ),
        out_specs=(
            tokens,
            tokens,
            P(ctx),
            matrix,
            matrix,
            matrix,
            P(),
            P(),
            turned,
            P(ctx),
            matrix,
            matrix,
            turned,
        ),
        check_vma=False,
    )
```

```python
import jax
import jax.numpy as jnp
from jax import lax
from jax.experimental import pallas as pl
from jax.experimental.pallas import tpu as pltpu
from jax.sharding import Mesh, PartitionSpec as P

AXES = ("x", "zl", "core", "zh", "y")
EPS = 1e-06
ROPE_BASE = 1000000.0
HEAD = 128
RUN = 256
GROUP = 512
KEYS = 512
N_BLOCKS = 16
LOG2E = 1.4426950408889634
LN2 = 0.6931471805599453
Q_SCALE = LOG2E * HEAD ** (-0.5)
BF = jnp.bfloat16
F32 = jnp.float32
VMEM_LIMIT = 60 * 1024 * 1024


def swap_with(value, axis, mask):
    if axis == "z":
        return lax.ppermute(value, ("zl", "zh"), [(i, i ^ mask) for i in range(4)])
    size = 2 if axis == "core" else 4
    return lax.ppermute(value, axis, [(i, i ^ mask) for i in range(size)])


def chunk_along_x(value, mask):
    moves = [
        ((x * 2 + core) * 2 + zh, ((x ^ mask) * 2 + zh) * 2 + core)
        for x in range(4)
        for core in range(2)
        for zh in range(2)
    ]
    return lax.ppermute(value, ("x", "core", "zh"), moves)


def chunk_along_z(value, mask):
    moves = [
        ((zl * 2 + core) * 2 + zh, ((zl ^ (mask >> 1)) * 2 + (zh ^ (mask & 1))) * 2 + core)
        for zl in range(2)
        for core in range(2)
        for zh in range(2)
    ]
    return lax.ppermute(value, ("zl", "core", "zh"), moves)


def exchange_runs(value):
    mirror = [(i, i ^ 14 if i % 2 else i) for i in range(16)]
    return lax.ppermute(value, ("x", "zl", "core"), mirror)


def gather_chunk(value):
    parts = [chunk_along_x(value, m) for m in range(4)]
    return [jnp.concatenate([p[:, c] for p in parts]) for c in (slice(0, 768), slice(768, 1920))]


def scatter_axis(parts, axis):
    total = parts[0].astype(F32)
    for m in (1, 2, 3):
        total = total + swap_with(parts[m].astype(BF), axis, m).astype(F32)
    return total


def gather_rows(block):
    half = jnp.concatenate([block] + [swap_with(block, "y", m) for m in (1, 2, 3)], axis=0)
    return half, swap_with(half, "core", 1)


def scatter_rows(mine, other):
    received = swap_with(other, "core", 1)
    parts = [
        mine[m * 64 : (m + 1) * 64].astype(F32) + received[m * 64 : (m + 1) * 64].astype(F32)
        for m in range(4)
    ]
    return scatter_axis(parts, "y")


def rms_parts(value):
    inverse = lax.rsqrt(jnp.mean(value * value, axis=-1, keepdims=True) + EPS)
    return value * inverse, inverse


def rms_back(scaled, normal, inverse):
    return inverse * (scaled - normal * jnp.mean(scaled * normal, axis=-1, keepdims=True))


def dot(left, right, contract):
    return lax.dot_general(left, right, (contract, ((), ())), preferred_element_type=F32)


NN = ((1,), (0,))
NT = ((1,), (1,))
TN = ((0,), (0,))


def stream_index(spot, yi):
    return (((spot >> 6) ^ yi) << 6) | (spot & 63)


def vmem():
    return pl.BlockSpec(memory_space=pltpu.VMEM)


def anywhere():
    return pl.BlockSpec(memory_space=pl.ANY)


def scalars():
    return pl.BlockSpec(memory_space=pltpu.SMEM)


def params():
    return pltpu.CompilerParams(vmem_limit_bytes=VMEM_LIMIT)


def cost(microseconds):
    return pl.CostEstimate(
        flops=int(microseconds * 1.15e9), transcendentals=0, bytes_accessed=1 << 20
    )


def shape(rows, columns, kind):
    return jax.ShapeDtypeStruct((rows, columns), kind)


def place_of(info):
    return info[0] * 4 + info[1] * 2 + info[2]


def rotate_lanes(value, cosine, sine):
    return value * cosine + pltpu.roll(value, HEAD // 2, 1) * sine


def normed(value):
    inverse = lax.rsqrt(jnp.mean(value * value, axis=-1, keepdims=True) + EPS)
    return value * inverse, inverse


def column_of(row):
    diagonal = lax.broadcasted_iota(jnp.int32, (64, 64), 0) == lax.broadcasted_iota(
        jnp.int32, (64, 64), 1
    )
    return jnp.sum(jnp.where(diagonal, row, 0.0), axis=1, keepdims=True)


def prepare_kernel(gain_one, gain_two, query, key, value, output, gate, up, down, out):
    first = column_of(gain_one[...].astype(F32))
    second = column_of(gain_two[...].astype(F32))
    out[:, :256] = (query[...].astype(F32) * first).astype(BF)
    out[:, 256:384] = (key[...].astype(F32) * first).astype(BF)
    out[:, 384:512] = (value[...].astype(F32) * first).astype(BF)
    out[:, 512:768] = output[...]
    out[:, 768:1152] = (gate[...].astype(F32) * second).astype(BF)
    out[:, 1152:1536] = (up[...].astype(F32) * second).astype(BF)
    out[:, 1536:] = down[...]


def prepare(*arrays):
    return pl.pallas_call(
        prepare_kernel,
        out_shape=shape(64, 1920, BF),
        in_specs=[vmem()] * 9,
        out_specs=vmem(),
        compiler_params=params(),
        name="prepare_weights",
        cost_estimate=cost(2),
    )(*arrays)


def weight_copies(info, parts, weight, sems):
    place = place_of(info)
    copies = []
    for mz, part in enumerate(parts):
        for mx in range(4):
            row = pl.multiple_of((place ^ (mx * 4 + mz)) * 64, 64)
            copies.append(
                pltpu.make_async_copy(
                    part.at[pl.ds(mx * 64, 64)], weight.at[pl.ds(row, 64)], sems.at[mz * 4 + mx]
                )
            )
    return copies


def project_kernel(
    info, mine, other, w0, w1, w2, w3, cosine, sine, gains, query, key, value, raw, weight, sems
):
    copies = weight_copies(info, (w0, w1, w2, w3), weight, sems)
    for copy in copies:
        copy.start()
    for copy in copies:
        copy.wait()
    for half, rows in enumerate((mine, other)):
        here = slice(half * RUN, (half + 1) * RUN)
        product = dot(rows[...], weight[:, : 4 * HEAD], NN)
        raw[here, :] = product[:, : 3 * HEAD]
        value[here, :] = product[:, 3 * HEAD :].astype(BF)
        for head in range(3):
            normal, _ = normed(product[:, head * HEAD : (head + 1) * HEAD])
            gain = gains[0:1, :] if head < 2 else gains[1:2, :]
            turned = rotate_lanes(normal * gain, cosine[here, :], sine[here, :])
            if head < 2:
                query[here, head * HEAD : (head + 1) * HEAD] = (turned * Q_SCALE).astype(BF)
            else:
                key[here, :] = turned.astype(BF)


def project(info, mine, other, parts, cosine, sine, gains):
    return pl.pallas_call(
        project_kernel,
        out_shape=(
            shape(GROUP, 2 * HEAD, BF),
            shape(GROUP, HEAD, BF),
            shape(GROUP, HEAD, BF),
            shape(GROUP, 3 * HEAD, F32),
            shape(1024, 6 * HEAD, BF),
        ),
        in_specs=[scalars(), vmem(), vmem()] + [anywhere()] * 4 + [vmem()] * 3,
        out_specs=(vmem(),) * 5,
        scratch_shapes=[pltpu.SemaphoreType.DMA((16,))],
        compiler_params=params(),
        name="project",
        cost_estimate=cost(5.5),
    )(info, mine, other, *parts, cosine, sine, gains)


def run_of(group, core, zh):
    return ((group ^ (7 * core)) * 2 + core) * 2 + zh


def key_copies(info, key_parts, value_parts, key_all, value_all, sems):
    xi, zl, zh, co = info[0], info[1], info[2], info[3]
    copies = []
    for turn in range(4):
        for sub in range(4):
            for kind in range(2):
                mx, mz = (sub, turn) if kind == 0 else (turn, sub)
                group = (xi ^ mx) * 2 + (zl ^ (mz >> 1))
                source = (key_parts if kind == 0 else value_parts)[turn]
                target = key_all if kind == 0 else value_all
                for half in range(2):
                    row = run_of(group, co ^ half, zh ^ (mz & 1)) * RUN
                    copies.append(
                        pltpu.make_async_copy(
                            source.at[pl.ds(sub * GROUP + half * RUN, RUN)],
                            target.at[pl.ds(pl.multiple_of(row, RUN), RUN)],
                            sems.at[(turn * 4 + sub) * 4 + kind * 2 + half],
                        )
                    )
    return copies


def first_of(token, start_one, start_two):
    return jnp.where(
        token >= start_two, start_two, jnp.where(token >= start_one, start_one, 0)
    )


def spans(group, core):
    mine = (group ^ (7 * core)) * 2 + core
    theirs = (group ^ (7 * (1 - core))) * 2 + 1 - core
    big = jnp.where(theirs > mine, 1, 0)
    return jnp.minimum(mine, theirs), jnp.maximum(mine, theirs), big


def attention_kernel(
    info,
    query,
    out_weight,
    k0,
    k1,
    k2,
    k3,
    v0,
    v1,
    v2,
    v3,
    out,
    sums,
    mine,
    other,
    key_all,
    value_all,
    totals,
    sems,
):
    copies = key_copies(info, (k0, k1, k2, k3), (v0, v1, v2, v3), key_all, value_all, sems)
    for copy in copies:
        copy.start()
    for copy in copies:
        copy.wait()
    xi, zl, zh, co, yi = (info[i] for i in range(5))
    start_one, start_two = info[5], info[6]
    group = xi * 2 + zl
    low, high, big = spans(group, co)
    ones = jnp.ones((KEYS, HEAD), BF)
    row_spot = stream_index(lax.broadcasted_iota(jnp.int32, (RUN, 1), 0), yi)
    totals[...] = jnp.zeros_like(totals)

    def tokens_of(half):
        token = run_of(group, co ^ half, zh) * RUN + row_spot
        return token, first_of(token, start_one, start_two)

    def block(index, masked, halves):
        rows = pl.ds(pl.multiple_of(index * KEYS, KEYS), KEYS)
        keys = key_all[rows, :]
        values = jnp.concatenate([value_all[rows, :], ones], axis=1)
        spot = lax.broadcasted_iota(jnp.int32, (1, KEYS), 1)
        key_tokens = index * KEYS + (spot & ~(RUN - 1)) + stream_index(spot & (RUN - 1), yi)
        for half in halves:
            rows_here = pl.ds(pl.multiple_of(half * RUN, RUN), RUN)
            if masked:
                token, start = tokens_of(half)
                allowed = (key_tokens <= token) & (key_tokens >= start)
            for head in range(2):
                scores = dot(query[rows_here, head * HEAD : (head + 1) * HEAD], keys, NT)
                weights = jnp.exp2(scores)
                if masked:
                    weights = jnp.where(allowed, weights, 0.0)
                totals[half * 2 + head] += dot(weights.astype(BF), values, NN)

    def full_both(index, carry):
        block(index, False, (0, 1))
        return carry

    def full_big(step, carry):
        block(low + 1 + 2 * step, False, (big,))
        block(low + 2 + 2 * step, False, (big,))
        return carry

    lax.fori_loop(1, low, full_both, 0)
    lax.fori_loop(0, (high - 1 - low) // 2, full_big, 0)
    for half in range(2):
        keep = tokens_of(half)[1] <= KEYS
        for head in range(2):
            totals[half * 2 + head] = jnp.where(keep, totals[half * 2 + head], 0.0)
    block(jnp.int32(0), True, (0, 1))

    @pl.when(low > 0)
    def _():
        block(low, True, (0, 1))

    block(high, True, (big,))
    for half in range(2):
        for head in range(2):
            total = totals[half * 2 + head]
            weight_sum = total[:, HEAD:]
            out[half * RUN : (half + 1) * RUN, head * HEAD : (head + 1) * HEAD] = (
                total[:, :HEAD] / weight_sum
            ).astype(BF)
            sums[half * 2 + head] = jnp.log2(weight_sum).T[:8]
    mine[...] = dot(out[:RUN, :], out_weight[:, 4 * HEAD :], NT).astype(BF)
    other[...] = dot(out[RUN:, :], out_weight[:, 4 * HEAD :], NT).astype(BF)


def attention_forward(info, query, out_weight, key_parts, value_parts):
    return pl.pallas_call(
        attention_kernel,
        out_shape=(
            shape(GROUP, 2 * HEAD, BF),
            jax.ShapeDtypeStruct((4, 8, RUN), F32),
            shape(RUN, 1024, BF),
            shape(RUN, 1024, BF),
        ),
        in_specs=[scalars(), vmem(), vmem()] + [anywhere()] * 8,
        out_specs=(vmem(),) * 4,
        scratch_shapes=[
            pltpu.VMEM((N_BLOCKS * KEYS, HEAD), BF),
            pltpu.VMEM((N_BLOCKS * KEYS, HEAD), BF),
            pltpu.VMEM((4, RUN, 2 * HEAD), F32),
            pltpu.SemaphoreType.DMA((64,)),
        ],
        compiler_params=params(),
        name="attention_forward",
        cost_estimate=cost(13),
    )(info, query, out_weight, *key_parts, *value_parts)


def feed_kernel(
    info,
    mine,
    other,
    mine_grad,
    other_grad,
    w0,
    w1,
    w2,
    w3,
    active,
    grads,
    mine_out,
    other_out,
    mine_down,
    other_down,
    weight,
    sems,
):
    copies = weight_copies(info, (w0, w1, w2, w3), weight, sems)
    for copy in copies:
        copy.start()
    for copy in copies:
        copy.wait()
    for half, (rows, rows_grad, out) in enumerate(
        ((mine, mine_grad, mine_out), (other, other_grad, other_out))
    ):
        here = slice(half * RUN, (half + 1) * RUN)
        gate_up = dot(rows[...], weight[:, :768], NN)
        gate, up = gate_up[:, :384], gate_up[:, 384:]
        sigmoid = 1.0 / (1.0 + jnp.exp(-gate))
        swish = gate * sigmoid
        active[here, :] = (swish * up).astype(BF)
        grad_active = dot(rows_grad[...], weight[:, 768:], NN)
        slope = sigmoid * (1.0 + gate * (1.0 - sigmoid))
        grads[here, :384] = (grad_active * up * slope).astype(BF)
        grads[here, 384:] = (grad_active * swish).astype(BF)
        out[...] = dot(grads[here, :], weight[:, :768], NT).astype(BF)
    mine_down[...] = dot(active[:RUN, :], weight[:, 768:], NT).astype(BF)
    other_down[...] = dot(active[RUN:, :], weight[:, 768:], NT).astype(BF)


def feed(info, mine, other, mine_grad, other_grad, parts):
    return pl.pallas_call(
        feed_kernel,
        out_shape=(shape(GROUP, 384, BF), shape(GROUP, 768, BF)) + (shape(RUN, 1024, BF),) * 4,
        in_specs=[scalars()] + [vmem()] * 4 + [anywhere()] * 4,
        out_specs=(vmem(),) * 6,
        scratch_shapes=[pltpu.VMEM((1024, 1152), BF), pltpu.SemaphoreType.DMA((16,))],
        compiler_params=params(),
        name="feed",
        cost_estimate=cost(7.5),
    )(info, mine, other, mine_grad, other_grad, *parts)


def head_back(gradient, raw, gain, cosine, sine):
    normal, inverse = normed(raw)
    turned = rotate_lanes(gradient, cosine, -sine)
    part = jnp.sum(turned * normal, axis=0, keepdims=True)
    scaled = turned * gain
    mean = jnp.mean(scaled * normal, axis=-1, keepdims=True)
    return (inverse * (scaled - normal * mean)).astype(BF), part


def attention_back_kernel(
    info,
    query,
    mine,
    other,
    out_weight,
    attended,
    sums,
    raw,
    cosine,
    sine,
    gains,
    k0,
    k1,
    k2,
    k3,
    v0,
    v1,
    v2,
    v3,
    grad_raw,
    gain_part,
    gk0,
    gk1,
    gk2,
    gk3,
    gv0,
    gv1,
    gv2,
    gv3,
    key_all,
    value_all,
    totals,
    grad,
    deltas,
    grad_key,
    grad_value,
    sems,
):
    copies = key_copies(info, (k0, k1, k2, k3), (v0, v1, v2, v3), key_all, value_all, sems)
    for copy in copies:
        copy.start()
    for half, rows_in in enumerate((mine, other)):
        here = slice(half * RUN, (half + 1) * RUN)
        rows_grad = dot(rows_in[...], out_weight[:, 4 * HEAD :], NN).astype(BF)
        grad[here, :] = rows_grad
        products = rows_grad.astype(F32) * attended[here, :].astype(F32)
        for head in range(2):
            turned = products[:, head * HEAD : (head + 1) * HEAD].T
            deltas[half * 2 + head] = jnp.broadcast_to(
                jnp.sum(turned, axis=0, keepdims=True), (8, RUN)
            )
    for copy in copies:
        copy.wait()
    xi, zl, zh, co, yi = (info[i] for i in range(5))
    start_one, start_two = info[5], info[6]
    group = xi * 2 + zl
    low, high, big = spans(group, co)
    column_spot = stream_index(lax.broadcasted_iota(jnp.int32, (1, RUN), 1), yi)

    def tokens_of(half):
        token = run_of(group, co ^ half, zh) * RUN + column_spot
        return token, first_of(token, start_one, start_two)

    totals[...] = jnp.zeros_like(totals)

    def places(index):
        owner_core = index % 2
        owner = (index // 2) ^ (7 * owner_core)
        mx = (owner // 2) ^ xi
        half = owner_core ^ co
        spots = []
        for run in range(2):
            mz = ((owner % 2) ^ zl) * 2 + (run ^ zh)
            spots.append((mx, mz, half))
        return spots

    def store(index, key_grad, value_grad):
        for run, (mx, mz, half) in enumerate(places(index)):
            rows = slice(run * RUN, (run + 1) * RUN)
            key_row = (mz * 4 + mx) * GROUP + half * RUN
            value_row = (mx * 4 + mz) * GROUP + half * RUN
            grad_key[pl.ds(pl.multiple_of(key_row, RUN), RUN), :] = key_grad[rows]
            grad_value[pl.ds(pl.multiple_of(value_row, RUN), RUN), :] = value_grad[rows]

    def block(index, masked, halves):
        rows = pl.ds(pl.multiple_of(index * KEYS, KEYS), KEYS)
        keys = key_all[rows, :]
        values = value_all[rows, :]
        spot = lax.broadcasted_iota(jnp.int32, (KEYS, 1), 0)
        key_tokens = index * KEYS + (spot & ~(RUN - 1)) + stream_index(spot & (RUN - 1), yi)
        key_grad = jnp.zeros((KEYS, HEAD), F32)
        value_grad = jnp.zeros((KEYS, HEAD), F32)
        for half in halves:
            rows_here = pl.ds(pl.multiple_of(half * RUN, RUN), RUN)
            token, start = tokens_of(half)
            if masked:
                allowed = (key_tokens <= token) & (key_tokens >= start)
            for head in range(2):
                lanes = slice(head * HEAD, (head + 1) * HEAD)
                queries = query[rows_here, lanes]
                grads = grad[rows_here, lanes]
                level = sums[half * 2 + head][0:1, :]
                if not masked:
                    level = jnp.where(start <= KEYS, level, 1e30)
                probs = jnp.exp2(dot(keys, queries, NT) - level)
                if masked:
                    probs = jnp.where(allowed, probs, 0.0)
                grad_probs = dot(values, grads, NT)
                grad_scores = (probs * (grad_probs - deltas[half * 2 + head][0:1, :])).astype(BF)
                value_grad = value_grad + dot(probs.astype(BF), grads, NN)
                key_grad = key_grad + dot(grad_scores, queries, NN)
                totals[half * 2 + head] += dot(grad_scores, keys, TN)
        store(index, (key_grad * LN2).astype(BF), value_grad.astype(BF))

    def full_both(index, carry):
        block(index, False, (0, 1))
        return carry

    def full_big(step, carry):
        block(low + 1 + 2 * step, False, (big,))
        block(low + 2 + 2 * step, False, (big,))
        return carry

    lax.fori_loop(1, low, full_both, 0)
    lax.fori_loop(0, (high - 1 - low) // 2, full_big, 0)
    block(jnp.int32(0), True, (0, 1))

    @pl.when(low > 0)
    def _():
        block(low, True, (0, 1))

    block(high, True, (big,))

    def empty(index, carry):
        nothing = jnp.zeros((KEYS, HEAD), BF)
        store(index, nothing, nothing)
        return carry

    lax.fori_loop(high + 1, N_BLOCKS, empty, 0)
    outs = []
    for m in range(4):
        for kind, (source, target) in enumerate(
            ((grad_key, (gk0, gk1, gk2, gk3)[m]), (grad_value, (gv0, gv1, gv2, gv3)[m]))
        ):
            outs.append(
                pltpu.make_async_copy(
                    source.at[pl.ds(m * 4 * GROUP, 4 * GROUP)], target, sems.at[m * 2 + kind]
                )
            )
    for copy in outs:
        copy.start()
    part = jnp.zeros((1, HEAD), F32)
    for half in range(2):
        here = slice(half * RUN, (half + 1) * RUN)
        for head in range(2):
            lanes = slice(head * HEAD, (head + 1) * HEAD)
            grad_raw[here, lanes], one = head_back(
                totals[half * 2 + head] * HEAD ** (-0.5),
                raw[here, lanes],
                gains[0:1, :],
                cosine[here, :],
                sine[here, :],
            )
            part = part + one
    gain_part[...] = jnp.broadcast_to(part, (8, HEAD))
    for copy in outs:
        copy.wait()


def attention_back(
    info, query, mine, other, out_weight, attended, sums, raw, cosine, sine, gains, keys, values
):
    return pl.pallas_call(
        attention_back_kernel,
        out_shape=(shape(GROUP, 2 * HEAD, BF), shape(8, HEAD, F32))
        + (shape(4 * GROUP, HEAD, BF),) * 8,
        in_specs=[scalars()] + [vmem()] * 10 + [anywhere()] * 8,
        out_specs=(vmem(), vmem()) + (anywhere(),) * 8,
        scratch_shapes=[
            pltpu.VMEM((N_BLOCKS * KEYS, HEAD), BF),
            pltpu.VMEM((N_BLOCKS * KEYS, HEAD), BF),
            pltpu.VMEM((4, RUN, HEAD), F32),
            pltpu.VMEM((GROUP, 2 * HEAD), BF),
            pltpu.VMEM((4, 8, RUN), F32),
            pltpu.VMEM((N_BLOCKS * KEYS, HEAD), BF),
            pltpu.VMEM((N_BLOCKS * KEYS, HEAD), BF),
            pltpu.SemaphoreType.DMA((64,)),
        ],
        compiler_params=params(),
        name="attention_back",
        cost_estimate=cost(24),
    )(
        info,
        query,
        mine,
        other,
        out_weight,
        attended,
        sums,
        raw,
        cosine,
        sine,
        gains,
        *keys,
        *values,
    )


def stack_kernel(k0, k1, k2, k3, v0, v1, v2, v3, keys, values):
    for m, (key, value) in enumerate(((k0, v0), (k1, v1), (k2, v2), (k3, v3))):
        rows = slice(m * GROUP, (m + 1) * GROUP)
        keys[rows, :] = key[...]
        values[rows, :] = value[...]


def stack(keys, values):
    return pl.pallas_call(
        stack_kernel,
        out_shape=(shape(4 * GROUP, HEAD, BF),) * 2,
        in_specs=[vmem()] * 8,
        out_specs=(vmem(),) * 2,
        compiler_params=params(),
        name="stack_keys_values",
        cost_estimate=cost(2.3),
    )(*keys, *values)


def sum_kernel(k0, k1, k2, k3, v0, v1, v2, v3, *outs):
    for kind, parts in enumerate(((k0, k1, k2, k3), (v0, v1, v2, v3))):
        for m in range(4):
            rows = slice(m * GROUP, (m + 1) * GROUP)
            total = sum(part[rows, :].astype(F32) for part in parts)
            outs[kind * 4 + m][...] = total.astype(BF)


def sum_parts(keys, values):
    return pl.pallas_call(
        sum_kernel,
        out_shape=(shape(GROUP, HEAD, BF),) * 8,
        in_specs=[vmem()] * 8,
        out_specs=(vmem(),) * 8,
        compiler_params=params(),
        name="sum_key_value_grads",
        cost_estimate=cost(3.3),
    )(*keys, *values)


def feed_grads_kernel(info, m1, o1, m2, o2, active, grads, f0, f1, f2, f3, total):
    place = place_of(info)
    top, low = slice(0, RUN), slice(RUN, GROUP)
    total[:, :768] = (
        dot(m2[...], grads[top, :], TN) + dot(o2[...], grads[low, :], TN)
    ).astype(BF)
    total[:, 768:] = (
        dot(m1[...], active[top, :], TN) + dot(o1[...], active[low, :], TN)
    ).astype(BF)
    for mx, out in enumerate((f0, f1, f2, f3)):
        for mz in range(4):
            row = pl.multiple_of((place ^ (mx * 4 + mz)) * 64, 64)
            out[mz * 64 : (mz + 1) * 64, :] = total[pl.ds(row, 64), :]


def feed_grads(info, rows, rows_two, active, grads):
    return pl.pallas_call(
        feed_grads_kernel,
        out_shape=(shape(256, 1152, BF),) * 4,
        in_specs=[scalars()] + [vmem()] * 6,
        out_specs=(vmem(),) * 4,
        scratch_shapes=[pltpu.VMEM((1024, 1152), BF)],
        compiler_params=params(),
        name="feed_grads",
        cost_estimate=cost(5),
    )(info, *rows, *rows_two, active, grads)


def early_kernel(info, m1, o1, mg, og, grad_raw, attended, e0, e1, e2, e3, total):
    place = place_of(info)
    top, low = slice(0, RUN), slice(RUN, GROUP)
    total[:, :256] = (
        dot(m1[...], grad_raw[top, :], TN) + dot(o1[...], grad_raw[low, :], TN)
    ).astype(BF)
    total[:, 256:] = (
        dot(mg[...], attended[top, :], TN) + dot(og[...], attended[low, :], TN)
    ).astype(BF)
    for mx, out in enumerate((e0, e1, e2, e3)):
        for mz in range(4):
            row = pl.multiple_of((place ^ (mx * 4 + mz)) * 64, 64)
            out[mz * 64 : (mz + 1) * 64, :] = total[pl.ds(row, 64), :]


def early_grads(info, rows, grad_rows, grad_raw, attended):
    return pl.pallas_call(
        early_kernel,
        out_shape=(shape(256, 512, BF),) * 4,
        in_specs=[scalars()] + [vmem()] * 6,
        out_specs=(vmem(),) * 4,
        scratch_shapes=[pltpu.VMEM((1024, 512), BF)],
        compiler_params=params(),
        name="early_grads",
        cost_estimate=cost(4),
    )(info, *rows, *grad_rows, grad_raw, attended)


def last_kernel(
    info,
    m1,
    o1,
    weight,
    grad_raw,
    query_part,
    raw,
    cosine,
    sine,
    gains,
    k0,
    k1,
    k2,
    k3,
    v0,
    v1,
    v2,
    v3,
    mine_down,
    other_down,
    mine,
    other,
    l0,
    l1,
    l2,
    l3,
    grads,
    total,
):
    place = place_of(info)
    part = jnp.zeros((1, HEAD), F32)
    for half, (out, down) in enumerate(((mine, mine_down), (other, other_down))):
        here = slice(half * RUN, (half + 1) * RUN)
        out[:, 1024:] = down[...]
        key_grad = sum(k[here, :].astype(F32) for k in (k0, k1, k2, k3))
        value_grad = sum(v[here, :].astype(F32) for v in (v0, v1, v2, v3))
        grads[here, :HEAD], one = head_back(
            key_grad, raw[here, 2 * HEAD :], gains[1:2, :], cosine[here, :], sine[here, :]
        )
        grads[here, HEAD:] = value_grad.astype(BF)
        part = part + one
        out[:, :1024] = (
            dot(grad_raw[here, :], weight[:, : 2 * HEAD], NT)
            + dot(grads[here, :], weight[:, 2 * HEAD : 4 * HEAD], NT)
        ).astype(BF)
    total[...] = (
        dot(m1[...], grads[:RUN, :], TN) + dot(o1[...], grads[RUN:, :], TN)
    ).astype(BF)
    row = lax.broadcasted_iota(jnp.int32, (64, 1), 0)
    heads = jnp.where(row == 0, query_part[0:1, :], jnp.where(row == 1, part, 0.0)).astype(BF)
    for mx, out in enumerate((l0, l1, l2, l3)):
        for mz in range(4):
            row = pl.multiple_of((place ^ (mx * 4 + mz)) * 64, 64)
            here = slice(mz * 64, (mz + 1) * 64)
            out[here, : 2 * HEAD] = total[pl.ds(row, 64), :]
            out[here, 2 * HEAD :] = heads


def last_step(info, rows, weight, grad_raw, query_part, raw, cosine, sine, gains, *parts):
    return pl.pallas_call(
        last_kernel,
        out_shape=(shape(RUN, 2048, BF),) * 2 + (shape(256, 3 * HEAD, BF),) * 4,
        in_specs=[scalars()] + [vmem()] * 19,
        out_specs=(vmem(),) * 6,
        scratch_shapes=[pltpu.VMEM((GROUP, 2 * HEAD), BF), pltpu.VMEM((1024, 2 * HEAD), BF)],
        compiler_params=params(),
        name="last_step",
        cost_estimate=cost(6),
    )(info, *rows, weight, grad_raw, query_part, raw, cosine, sine, gains, *parts)


def local(
    tokens,
    positions,
    sequence_ids,
    attn_gain,
    query_weight,
    key_matrix,
    value_matrix,
    query_gain,
    key_gain,
    output_weight,
    mlp_gain,
    gate_weight,
    up_weight,
    down_weight,
    out_grad,
):
    xi, zl, co, zh, yi = (lax.axis_index(name) for name in AXES)
    place = xi * 4 + zl * 2 + zh
    start_one = jnp.sum(sequence_ids < 1, dtype=jnp.int32)
    start_two = jnp.sum(sequence_ids < 2, dtype=jnp.int32)
    info = jnp.stack([xi, zl, zh, co, yi, start_one, start_two]).astype(jnp.int32)

    gain_one = attn_gain.astype(F32)[:, None]
    gain_two = mlp_gain.astype(F32)[:, None]
    weights = prepare(
        attn_gain.reshape(1, 64),
        mlp_gain.reshape(1, 64),
        query_weight,
        key_matrix,
        value_matrix,
        output_weight.T,
        gate_weight,
        up_weight,
        down_weight.T,
    )
    one_own, two_own = gather_chunk(weights)
    one_weights = [one_own] + [swap_with(one_own, "z", m) for m in (1, 2, 3)]

    resid = exchange_runs(tokens).astype(F32)
    normal_one, inverse_one = rms_parts(resid)
    rows_one = gather_rows(normal_one.astype(BF))

    run_places = positions.reshape(32, 4, 64)
    run_places = jnp.stack(
        [
            lax.dynamic_index_in_dim(run_places, run_of(xi * 2 + zl, co ^ half, zh), 0, False)
            for half in range(2)
        ]
    )
    run_places = jnp.where((yi & 1) == 1, run_places[:, jnp.array([1, 0, 3, 2])], run_places)
    run_places = jnp.where((yi & 2) == 2, run_places[:, jnp.array([2, 3, 0, 1])], run_places)
    half_size = HEAD // 2
    lane = jnp.arange(HEAD)
    frequency = jnp.exp(
        -jnp.log(ROPE_BASE) * 2.0 * (lane % half_size).astype(F32) / HEAD
    )
    angles = run_places.reshape(GROUP).astype(F32)[:, None] * frequency[None, :]
    cosine = jnp.cos(angles)
    sine = jnp.sin(angles) * jnp.where(lane < half_size, -1.0, 1.0)
    gains = jnp.stack([query_gain, key_gain]).astype(F32)
    query, key, value, raw, weight_full = project(
        info, *rows_one, one_weights, cosine, sine, gains
    )

    two_own, key = lax.optimization_barrier((two_own, key))
    two_weights = [two_own, None, swap_with(two_own, "z", 2), None]
    keys_x = [key] + [swap_with(key, "x", m) for m in (1, 2, 3)]
    values_z = [value] + [swap_with(value, "z", m) for m in (1, 2, 3)]
    keys_x, two_weights[2] = lax.optimization_barrier((keys_x, two_weights[2]))
    key_own, value_own = stack(keys_x, values_z)
    out_grad, key_own = lax.optimization_barrier((out_grad, key_own))
    out_grad = exchange_runs(out_grad)
    cotangent = out_grad.astype(F32)
    grad_rows = gather_rows(out_grad)
    key_parts = [key_own] + [swap_with(key_own, "z", m) for m in (1, 2, 3)]
    value_parts = [value_own] + [swap_with(value_own, "x", m) for m in (1, 2, 3)]

    two_own, key_parts, value_parts, grad_rows = lax.optimization_barrier(
        (two_own, key_parts, value_parts, grad_rows)
    )
    two_weights[1] = swap_with(two_own, "z", 1)
    two_weights[3] = swap_with(two_own, "z", 3)

    attended, sums, mine, other = attention_forward(
        info, query, weight_full, key_parts, value_parts
    )
    mine, other, two_weights[1] = lax.optimization_barrier((mine, other, two_weights[1]))
    hidden = resid + scatter_rows(mine, other)
    normal_two, inverse_two = rms_parts(hidden)
    normal_two, two_weights[3] = lax.optimization_barrier((normal_two, two_weights[3]))
    rows_two = gather_rows(normal_two.astype(BF))

    active, grad_gate_up, mine, other, mine_down, other_down = feed(
        info, *rows_two, *grad_rows, two_weights
    )
    scaled_two = scatter_rows(mine, other)
    grad_hidden = cotangent + rms_back(scaled_two, normal_two, inverse_two)
    grad_rows_one = gather_rows(grad_hidden.astype(BF))
    two_parts = feed_grads(info, grad_rows, rows_two, active, grad_gate_up)
    two_parts, grad_rows_one = lax.optimization_barrier((two_parts, grad_rows_one))
    two_parts = [two_parts[0]] + [swap_with(two_parts[m], "x", m) for m in (1, 2, 3)]

    grad_raw, query_part, *key_value_grads = attention_back(
        info,
        query,
        *grad_rows_one,
        weight_full,
        attended,
        sums,
        raw,
        cosine,
        sine,
        gains,
        key_parts,
        value_parts,
    )
    key_value_grads, two_parts = lax.optimization_barrier((key_value_grads, two_parts))
    key_grads, value_grads = key_value_grads[:4], key_value_grads[4:]
    early = early_grads(info, rows_one, grad_rows_one, grad_raw, attended)
    summed = sum_parts(
        [key_grads[0]] + [swap_with(key_grads[m], "z", m) for m in (1, 2, 3)],
        [value_grads[0]] + [swap_with(value_grads[m], "x", m) for m in (1, 2, 3)],
    )
    early, summed = lax.optimization_barrier((early, summed))
    key_grads = [summed[0]] + [swap_with(summed[m], "x", m) for m in (1, 2, 3)]
    value_grads = [summed[4]] + [swap_with(summed[4 + m], "z", m) for m in (1, 2, 3)]
    early = [early[0]] + [swap_with(early[m], "x", m) for m in (1, 2, 3)]
    key_grads, value_grads, early = lax.optimization_barrier((key_grads, value_grads, early))

    mine, other, *late = last_step(
        info,
        rows_one,
        weight_full,
        grad_raw,
        query_part,
        raw,
        cosine,
        sine,
        gains,
        *key_grads,
        *value_grads,
        mine_down,
        other_down,
    )
    late = [late[0]] + [swap_with(late[m], "x", m) for m in (1, 2, 3)]
    totals = [
        sum(part.astype(F32) for part in parts).astype(BF) for parts in (two_parts, early, late)
    ]
    received = swap_with(other, "core", 1)
    halves = [
        jnp.concatenate([v[m * 64 : (m + 1) * 64] for v in totals], axis=1) for m in range(4)
    ]
    parts = [
        mine[m * 64 : (m + 1) * 64].astype(F32) + received[m * 64 : (m + 1) * 64].astype(F32)
        for m in range(4)
    ]
    halves, parts = lax.optimization_barrier((halves, parts))
    own = sum(chunk_along_z(halves[m], m).astype(F32) for m in range(4))
    both = scatter_axis(parts, "y")
    output = hidden + both[:, 1024:]
    token_grad = grad_hidden + rms_back(both[:, :1024], normal_one, inverse_one)
    both = exchange_runs(jnp.concatenate([output.astype(BF), token_grad.astype(BF)], axis=1))
    output, token_grad = both[:, :1024], both[:, 1024:].astype(F32)

    gate_part, up_part, down_part = own[:, :384], own[:, 384:768], own[:, 768:1152]
    query_part, output_part = own[:, 1152:1408], own[:, 1408:1664]
    key_part, value_part = own[:, 1664:1792], own[:, 1792:1920]
    attn_part = (
        jnp.sum(query_part * query_weight.astype(F32), axis=1)
        + jnp.sum(key_part * key_matrix.astype(F32), axis=1)
        + jnp.sum(value_part * value_matrix.astype(F32), axis=1)
    )
    mlp_part = jnp.sum(
        gate_part * gate_weight.astype(F32) + up_part * up_weight.astype(F32), axis=1
    )
    sums_all = jnp.concatenate([attn_part, mlp_part, own[0, 1920:], own[1, 1920:]])
    received = [swap_with(sums_all, "y", m) for m in (1, 2, 3)]
    for part in received:
        sums_all = sums_all + part
    sums_all = sums_all + swap_with(sums_all, "z", 1)
    gain_parts, head_parts = sums_all[:128], sums_all[128:]
    return (
        output,
        token_grad,
        gain_parts[:64],
        query_part * gain_one,
        key_part * gain_one,
        value_part * gain_one,
        head_parts[:HEAD],
        head_parts[HEAD:],
        output_part.T,
        gain_parts[64:],
        gate_part * gain_two,
        up_part * gain_two,
        down_part.T,
    )


def solution(mesh):
    parts = Mesh(mesh.devices.reshape(4, 2, 2, 2, 4), AXES)
    ctx, tp = ("x", "zl", "core"), ("zh", "y")
    tokens, matrix, turned = P(AXES, None), P(ctx, tp), P(tp, ctx)
    return jax.shard_map(
        local,
        mesh=parts,
        in_specs=(
            tokens,
            P(),
            P(),
            P(ctx),
            matrix,
            matrix,
            matrix,
            P(),
            P(),
            turned,
            P(ctx),
            matrix,
            matrix,
            turned,
            tokens,
        ),
        out_specs=(
            tokens,
            tokens,
            P(ctx),
            matrix,
            matrix,
            matrix,
            P(),
            P(),
            turned,
            P(ctx),
            matrix,
            matrix,
            turned,
        ),
        check_vma=False,
    )
```

```python
import jax
import jax.numpy as jnp
from jax import lax
from jax.experimental import pallas as pl
from jax.experimental.pallas import tpu as pltpu
from jax.sharding import Mesh, PartitionSpec as P

AXES = ("x", "zl", "core", "zh", "y")
EPS = 1e-06
ROPE_BASE = 1000000.0
HEAD = 128
RUN = 256
GROUP = 512
KEYS = 512
N_BLOCKS = 16
LOG2E = 1.4426950408889634
LN2 = 0.6931471805599453
Q_SCALE = LOG2E * HEAD ** (-0.5)
BF = jnp.bfloat16
F32 = jnp.float32
VMEM_LIMIT = 60 * 1024 * 1024


NEIGHBOURS = {"x": (1, 3), "z": (2, 3)}


def swap_with(value, axis, mask):
    if axis == "z":
        return lax.ppermute(value, ("zl", "zh"), [(i, i ^ mask) for i in range(4)])
    size = 2 if axis == "core" else 4
    return lax.ppermute(value, axis, [(i, i ^ mask) for i in range(size)])


def chunk_along_x(value, mask):
    moves = [
        ((x * 2 + core) * 2 + zh, ((x ^ mask) * 2 + zh) * 2 + core)
        for x in range(4)
        for core in range(2)
        for zh in range(2)
    ]
    return lax.ppermute(value, ("x", "core", "zh"), moves)


def chunk_along_z(value, mask):
    moves = [
        ((zl * 2 + core) * 2 + zh, ((zl ^ (mask >> 1)) * 2 + (zh ^ (mask & 1))) * 2 + core)
        for zl in range(2)
        for core in range(2)
        for zh in range(2)
    ]
    return lax.ppermute(value, ("zl", "core", "zh"), moves)


def exchange_runs(value):
    mirror = [(i, i ^ 14 if i % 2 else i) for i in range(16)]
    return lax.ppermute(value, ("x", "zl", "core"), mirror)


def gather_chunk(value):
    parts = [chunk_along_x(value, m) for m in range(4)]
    return [jnp.concatenate([p[:, c] for p in parts]) for c in (slice(0, 768), slice(768, 1920))]


def scatter_axis(parts, axis):
    total = parts[0].astype(F32)
    for m in (1, 2, 3):
        total = total + swap_with(parts[m].astype(BF), axis, m).astype(F32)
    return total


def gather_steps(value, axis):
    near, far = NEIGHBOURS[axis]
    half = value.shape[0] // 2
    one, two = swap_with(value, axis, near), swap_with(value, axis, far)
    return [value, one, two, swap_with(two[:half], axis, near), swap_with(one[half:], axis, far)]


def gather_along_y(block):
    return jnp.concatenate([block] + [swap_with(block, "y", m) for m in (1, 2, 3)], axis=0)


def gather_rows(block):
    half = gather_along_y(block)
    return half, swap_with(half, "core", 1)


def scatter_rows(mine, other):
    received = swap_with(other, "core", 1)
    parts = [
        mine[m * 64 : (m + 1) * 64].astype(F32) + received[m * 64 : (m + 1) * 64].astype(F32)
        for m in range(4)
    ]
    return scatter_axis(parts, "y")


def rms_parts(value):
    inverse = lax.rsqrt(jnp.mean(value * value, axis=-1, keepdims=True) + EPS)
    return value * inverse, inverse


def rms_back(scaled, normal, inverse):
    return inverse * (scaled - normal * jnp.mean(scaled * normal, axis=-1, keepdims=True))


def dot(left, right, contract):
    return lax.dot_general(left, right, (contract, ((), ())), preferred_element_type=F32)


NN = ((1,), (0,))
NT = ((1,), (1,))
TN = ((0,), (0,))


def stream_index(spot, yi):
    return (((spot >> 6) ^ yi) << 6) | (spot & 63)


def vmem():
    return pl.BlockSpec(memory_space=pltpu.VMEM)


def anywhere():
    return pl.BlockSpec(memory_space=pl.ANY)


def scalars():
    return pl.BlockSpec(memory_space=pltpu.SMEM)


def params():
    return pltpu.CompilerParams(vmem_limit_bytes=VMEM_LIMIT)


def cost(microseconds):
    return pl.CostEstimate(
        flops=int(microseconds * 1.15e9), transcendentals=0, bytes_accessed=1 << 20
    )


def shape(rows, columns, kind):
    return jax.ShapeDtypeStruct((rows, columns), kind)


def place_of(info):
    return info[0] * 4 + info[1] * 2 + info[2]


def rotate_lanes(value, cosine, sine):
    return value * cosine + pltpu.roll(value, HEAD // 2, 1) * sine


def normed(value):
    inverse = lax.rsqrt(jnp.mean(value * value, axis=-1, keepdims=True) + EPS)
    return value * inverse, inverse


def column_of(row):
    diagonal = lax.broadcasted_iota(jnp.int32, (64, 64), 0) == lax.broadcasted_iota(
        jnp.int32, (64, 64), 1
    )
    return jnp.sum(jnp.where(diagonal, row, 0.0), axis=1, keepdims=True)


def prepare_kernel(gain_one, gain_two, query, key, value, output, gate, up, down, out):
    first = column_of(gain_one[...].astype(F32))
    second = column_of(gain_two[...].astype(F32))
    out[:, :256] = (query[...].astype(F32) * first).astype(BF)
    out[:, 256:384] = (key[...].astype(F32) * first).astype(BF)
    out[:, 384:512] = (value[...].astype(F32) * first).astype(BF)
    out[:, 512:768] = output[...]
    out[:, 768:1152] = (gate[...].astype(F32) * second).astype(BF)
    out[:, 1152:1536] = (up[...].astype(F32) * second).astype(BF)
    out[:, 1536:] = down[...]


def prepare(*arrays):
    return pl.pallas_call(
        prepare_kernel,
        out_shape=shape(64, 1920, BF),
        in_specs=[vmem()] * 9,
        out_specs=vmem(),
        compiler_params=params(),
        name="prepare_weights",
        cost_estimate=cost(2),
    )(*arrays)


def weight_copies(info, parts, weight, sems):
    place = place_of(info)
    copies = []
    for mz, part in enumerate(parts):
        for mx in range(4):
            row = pl.multiple_of((place ^ (mx * 4 + mz)) * 64, 64)
            copies.append(
                pltpu.make_async_copy(
                    part.at[pl.ds(mx * 64, 64)], weight.at[pl.ds(row, 64)], sems.at[mz * 4 + mx]
                )
            )
    return copies


def project_kernel(
    info, mine, other, w0, w1, w2, w3, cosine, sine, gains, query, key, value, raw, weight, sems
):
    copies = weight_copies(info, (w0, w1, w2, w3), weight, sems)
    for copy in copies:
        copy.start()
    for copy in copies:
        copy.wait()
    for half, rows in enumerate((mine, other)):
        here = slice(half * RUN, (half + 1) * RUN)
        product = dot(rows[...], weight[:, : 4 * HEAD], NN)
        raw[here, :] = product[:, : 3 * HEAD]
        value[here, :] = product[:, 3 * HEAD :].astype(BF)
        for head in range(3):
            normal, _ = normed(product[:, head * HEAD : (head + 1) * HEAD])
            gain = gains[0:1, :] if head < 2 else gains[1:2, :]
            turned = rotate_lanes(normal * gain, cosine[here, :], sine[here, :])
            if head < 2:
                query[here, head * HEAD : (head + 1) * HEAD] = (turned * Q_SCALE).astype(BF)
            else:
                key[here, :] = turned.astype(BF)


def project(info, mine, other, parts, cosine, sine, gains):
    return pl.pallas_call(
        project_kernel,
        out_shape=(
            shape(GROUP, 2 * HEAD, BF),
            shape(GROUP, HEAD, BF),
            shape(GROUP, HEAD, BF),
            shape(GROUP, 3 * HEAD, F32),
            shape(1024, 6 * HEAD, BF),
        ),
        in_specs=[scalars(), vmem(), vmem()] + [anywhere()] * 4 + [vmem()] * 3,
        out_specs=(vmem(),) * 5,
        scratch_shapes=[pltpu.SemaphoreType.DMA((16,))],
        compiler_params=params(),
        name="project",
        cost_estimate=cost(5.5),
    )(info, mine, other, *parts, cosine, sine, gains)


def run_of(group, core, zh):
    return ((group ^ (7 * core)) * 2 + core) * 2 + zh


def key_copies(info, key_parts, value_parts, key_all, value_all, sems):
    xi, zl, zh, co = info[0], info[1], info[2], info[3]
    copies = []
    for kind, (parts, target, axis) in enumerate(
        ((key_parts, key_all, "z"), (value_parts, value_all, "x"))
    ):
        near, far = NEIGHBOURS[axis]
        pieces = [(0, parts[0], 0), (near, parts[1], 0), (far, parts[2], 0)]
        pieces += [(near ^ far, parts[3], 0), (near ^ far, parts[4], 2)]
        for turn, source, first in pieces:
            for sub in range(first, min(first + source.shape[0] // GROUP, 4)):
                mx, mz = (sub, turn) if kind == 0 else (turn, sub)
                group = (xi ^ mx) * 2 + (zl ^ (mz >> 1))
                for half in range(2):
                    row = run_of(group, co ^ half, zh ^ (mz & 1)) * RUN
                    copies.append(
                        pltpu.make_async_copy(
                            source.at[pl.ds((sub - first) * GROUP + half * RUN, RUN)],
                            target.at[pl.ds(pl.multiple_of(row, RUN), RUN)],
                            sems.at[len(copies)],
                        )
                    )
    return copies


def first_of(token, start_one, start_two):
    return jnp.where(
        token >= start_two, start_two, jnp.where(token >= start_one, start_one, 0)
    )


def spans(group, core):
    mine = (group ^ (7 * core)) * 2 + core
    theirs = (group ^ (7 * (1 - core))) * 2 + 1 - core
    big = jnp.where(theirs > mine, 1, 0)
    return jnp.minimum(mine, theirs), jnp.maximum(mine, theirs), big


def attention_kernel(
    info,
    query,
    out_weight,
    k0,
    k1,
    k2,
    k3,
    k4,
    v0,
    v1,
    v2,
    v3,
    v4,
    out,
    sums,
    mine,
    other,
    key_all,
    value_all,
    totals,
    sems,
):
    copies = key_copies(info, (k0, k1, k2, k3, k4), (v0, v1, v2, v3, v4), key_all, value_all, sems)
    for copy in copies:
        copy.start()
    for copy in copies:
        copy.wait()
    xi, zl, zh, co, yi = (info[i] for i in range(5))
    start_one, start_two = info[5], info[6]
    group = xi * 2 + zl
    low, high, big = spans(group, co)
    ones = jnp.ones((KEYS, HEAD), BF)
    row_spot = stream_index(lax.broadcasted_iota(jnp.int32, (RUN, 1), 0), yi)
    totals[...] = jnp.zeros_like(totals)

    def tokens_of(half):
        token = run_of(group, co ^ half, zh) * RUN + row_spot
        return token, first_of(token, start_one, start_two)

    def block(index, masked, halves):
        rows = pl.ds(pl.multiple_of(index * KEYS, KEYS), KEYS)
        keys = key_all[rows, :]
        values = jnp.concatenate([value_all[rows, :], ones], axis=1)
        spot = lax.broadcasted_iota(jnp.int32, (1, KEYS), 1)
        key_tokens = index * KEYS + (spot & ~(RUN - 1)) + stream_index(spot & (RUN - 1), yi)
        for half in halves:
            rows_here = pl.ds(pl.multiple_of(half * RUN, RUN), RUN)
            if masked:
                token, start = tokens_of(half)
                allowed = (key_tokens <= token) & (key_tokens >= start)
            for head in range(2):
                scores = dot(query[rows_here, head * HEAD : (head + 1) * HEAD], keys, NT)
                weights = jnp.exp2(scores)
                if masked:
                    weights = jnp.where(allowed, weights, 0.0)
                totals[half * 2 + head] += dot(weights.astype(BF), values, NN)

    def full_both(index, carry):
        block(index, False, (0, 1))
        return carry

    def full_big(step, carry):
        block(low + 1 + 2 * step, False, (big,))
        block(low + 2 + 2 * step, False, (big,))
        return carry

    lax.fori_loop(1, low, full_both, 0)
    lax.fori_loop(0, (high - 1 - low) // 2, full_big, 0)
    for half in range(2):
        keep = tokens_of(half)[1] <= KEYS
        for head in range(2):
            totals[half * 2 + head] = jnp.where(keep, totals[half * 2 + head], 0.0)
    block(jnp.int32(0), True, (0, 1))

    @pl.when(low > 0)
    def _():
        block(low, True, (0, 1))

    block(high, True, (big,))
    for half in range(2):
        for head in range(2):
            total = totals[half * 2 + head]
            weight_sum = total[:, HEAD:]
            out[half * RUN : (half + 1) * RUN, head * HEAD : (head + 1) * HEAD] = (
                total[:, :HEAD] / weight_sum
            ).astype(BF)
            sums[half * 2 + head] = jnp.log2(weight_sum).T[:8]
    mine[...] = dot(out[:RUN, :], out_weight[:, 4 * HEAD :], NT).astype(BF)
    other[...] = dot(out[RUN:, :], out_weight[:, 4 * HEAD :], NT).astype(BF)


def attention_forward(info, query, out_weight, key_parts, value_parts):
    return pl.pallas_call(
        attention_kernel,
        out_shape=(
            shape(GROUP, 2 * HEAD, BF),
            jax.ShapeDtypeStruct((4, 8, RUN), F32),
            shape(RUN, 1024, BF),
            shape(RUN, 1024, BF),
        ),
        in_specs=[scalars(), vmem(), vmem()] + [anywhere()] * 10,
        out_specs=(vmem(),) * 4,
        scratch_shapes=[
            pltpu.VMEM((N_BLOCKS * KEYS, HEAD), BF),
            pltpu.VMEM((N_BLOCKS * KEYS, HEAD), BF),
            pltpu.VMEM((4, RUN, 2 * HEAD), F32),
            pltpu.SemaphoreType.DMA((64,)),
        ],
        compiler_params=params(),
        name="attention_forward",
        cost_estimate=cost(13),
    )(info, query, out_weight, *key_parts, *value_parts)


def feed_kernel(
    info,
    mine,
    other,
    mine_grad,
    other_grad,
    w0,
    w1,
    w2,
    w3,
    active,
    grads,
    mine_out,
    other_out,
    mine_down,
    other_down,
    weight,
    sems,
):
    copies = weight_copies(info, (w0, w1, w2, w3), weight, sems)
    for copy in copies:
        copy.start()
    for copy in copies:
        copy.wait()
    for half, (rows, rows_grad, out) in enumerate(
        ((mine, mine_grad, mine_out), (other, other_grad, other_out))
    ):
        here = slice(half * RUN, (half + 1) * RUN)
        gate_up = dot(rows[...], weight[:, :768], NN)
        gate, up = gate_up[:, :384], gate_up[:, 384:]
        sigmoid = 1.0 / (1.0 + jnp.exp(-gate))
        swish = gate * sigmoid
        active[here, :] = (swish * up).astype(BF)
        grad_active = dot(rows_grad[...], weight[:, 768:], NN)
        slope = sigmoid * (1.0 + gate * (1.0 - sigmoid))
        grads[here, :384] = (grad_active * up * slope).astype(BF)
        grads[here, 384:] = (grad_active * swish).astype(BF)
        out[...] = dot(grads[here, :], weight[:, :768], NT).astype(BF)
    mine_down[...] = dot(active[:RUN, :], weight[:, 768:], NT).astype(BF)
    other_down[...] = dot(active[RUN:, :], weight[:, 768:], NT).astype(BF)


def feed(info, mine, other, mine_grad, other_grad, parts):
    return pl.pallas_call(
        feed_kernel,
        out_shape=(shape(GROUP, 384, BF), shape(GROUP, 768, BF)) + (shape(RUN, 1024, BF),) * 4,
        in_specs=[scalars()] + [vmem()] * 4 + [anywhere()] * 4,
        out_specs=(vmem(),) * 6,
        scratch_shapes=[pltpu.VMEM((1024, 1152), BF), pltpu.SemaphoreType.DMA((16,))],
        compiler_params=params(),
        name="feed",
        cost_estimate=cost(7.5),
    )(info, mine, other, mine_grad, other_grad, *parts)


def head_back(gradient, raw, gain, cosine, sine):
    normal, inverse = normed(raw)
    turned = rotate_lanes(gradient, cosine, -sine)
    part = jnp.sum(turned * normal, axis=0, keepdims=True)
    scaled = turned * gain
    mean = jnp.mean(scaled * normal, axis=-1, keepdims=True)
    return (inverse * (scaled - normal * mean)).astype(BF), part


def attention_back_kernel(
    info,
    query,
    mine,
    other,
    out_weight,
    attended,
    sums,
    raw,
    cosine,
    sine,
    gains,
    k0,
    k1,
    k2,
    k3,
    k4,
    v0,
    v1,
    v2,
    v3,
    v4,
    grad_raw,
    gain_part,
    gk0,
    gk1,
    gk2,
    gk3,
    gk4,
    gv0,
    gv1,
    gv2,
    gv3,
    gv4,
    key_all,
    value_all,
    totals,
    grad,
    deltas,
    grad_key,
    grad_value,
    sems,
):
    copies = key_copies(info, (k0, k1, k2, k3, k4), (v0, v1, v2, v3, v4), key_all, value_all, sems)
    for copy in copies:
        copy.start()
    for half, rows_in in enumerate((mine, other)):
        here = slice(half * RUN, (half + 1) * RUN)
        rows_grad = dot(rows_in[...], out_weight[:, 4 * HEAD :], NN).astype(BF)
        grad[here, :] = rows_grad
        products = rows_grad.astype(F32) * attended[here, :].astype(F32)
        for head in range(2):
            turned = products[:, head * HEAD : (head + 1) * HEAD].T
            deltas[half * 2 + head] = jnp.broadcast_to(
                jnp.sum(turned, axis=0, keepdims=True), (8, RUN)
            )
    for copy in copies:
        copy.wait()
    xi, zl, zh, co, yi = (info[i] for i in range(5))
    start_one, start_two = info[5], info[6]
    group = xi * 2 + zl
    low, high, big = spans(group, co)
    column_spot = stream_index(lax.broadcasted_iota(jnp.int32, (1, RUN), 1), yi)

    def tokens_of(half):
        token = run_of(group, co ^ half, zh) * RUN + column_spot
        return token, first_of(token, start_one, start_two)

    totals[...] = jnp.zeros_like(totals)

    def places(index):
        owner_core = index % 2
        owner = (index // 2) ^ (7 * owner_core)
        mx = (owner // 2) ^ xi
        half = owner_core ^ co
        spots = []
        for run in range(2):
            mz = ((owner % 2) ^ zl) * 2 + (run ^ zh)
            spots.append((mx, mz, half))
        return spots

    def store(index, key_grad, value_grad):
        for run, (mx, mz, half) in enumerate(places(index)):
            rows = slice(run * RUN, (run + 1) * RUN)
            key_row = (mz * 4 + mx) * GROUP + half * RUN
            value_row = (mx * 4 + mz) * GROUP + half * RUN
            grad_key[pl.ds(pl.multiple_of(key_row, RUN), RUN), :] = key_grad[rows]
            grad_value[pl.ds(pl.multiple_of(value_row, RUN), RUN), :] = value_grad[rows]

    def block(index, masked, halves):
        rows = pl.ds(pl.multiple_of(index * KEYS, KEYS), KEYS)
        keys = key_all[rows, :]
        values = value_all[rows, :]
        spot = lax.broadcasted_iota(jnp.int32, (KEYS, 1), 0)
        key_tokens = index * KEYS + (spot & ~(RUN - 1)) + stream_index(spot & (RUN - 1), yi)
        key_grad = jnp.zeros((KEYS, HEAD), F32)
        value_grad = jnp.zeros((KEYS, HEAD), F32)
        for half in halves:
            rows_here = pl.ds(pl.multiple_of(half * RUN, RUN), RUN)
            token, start = tokens_of(half)
            if masked:
                allowed = (key_tokens <= token) & (key_tokens >= start)
            for head in range(2):
                lanes = slice(head * HEAD, (head + 1) * HEAD)
                queries = query[rows_here, lanes]
                grads = grad[rows_here, lanes]
                level = sums[half * 2 + head][0:1, :]
                if not masked:
                    level = jnp.where(start <= KEYS, level, 1e30)
                probs = jnp.exp2(dot(keys, queries, NT) - level)
                if masked:
                    probs = jnp.where(allowed, probs, 0.0)
                grad_probs = dot(values, grads, NT)
                grad_scores = (probs * (grad_probs - deltas[half * 2 + head][0:1, :])).astype(BF)
                value_grad = value_grad + dot(probs.astype(BF), grads, NN)
                key_grad = key_grad + dot(grad_scores, queries, NN)
                totals[half * 2 + head] += dot(grad_scores, keys, TN)
        store(index, (key_grad * LN2).astype(BF), value_grad.astype(BF))

    def full_both(index, carry):
        block(index, False, (0, 1))
        return carry

    def full_big(step, carry):
        block(low + 1 + 2 * step, False, (big,))
        block(low + 2 + 2 * step, False, (big,))
        return carry

    lax.fori_loop(1, low, full_both, 0)
    lax.fori_loop(0, (high - 1 - low) // 2, full_big, 0)
    block(jnp.int32(0), True, (0, 1))

    @pl.when(low > 0)
    def _():
        block(low, True, (0, 1))

    block(high, True, (big,))

    def empty(index, carry):
        nothing = jnp.zeros((KEYS, HEAD), BF)
        store(index, nothing, nothing)
        return carry

    lax.fori_loop(high + 1, N_BLOCKS, empty, 0)
    outs = []
    for source, targets, axis in (
        (grad_key, (gk0, gk1, gk2, gk3, gk4), "z"),
        (grad_value, (gv0, gv1, gv2, gv3, gv4), "x"),
    ):
        near, far = NEIGHBOURS[axis]
        block = 4 * GROUP
        starts = (0, near * block, far * block, (near ^ far) * block, (near ^ far) * block + block // 2)
        for start, target in zip(starts, targets):
            outs.append(
                pltpu.make_async_copy(
                    source.at[pl.ds(start, target.shape[0])], target, sems.at[len(outs)]
                )
            )
    for copy in outs:
        copy.start()
    part = jnp.zeros((1, HEAD), F32)
    for half in range(2):
        here = slice(half * RUN, (half + 1) * RUN)
        for head in range(2):
            lanes = slice(head * HEAD, (head + 1) * HEAD)
            grad_raw[here, lanes], one = head_back(
                totals[half * 2 + head] * HEAD ** (-0.5),
                raw[here, lanes],
                gains[0:1, :],
                cosine[here, :],
                sine[here, :],
            )
            part = part + one
    gain_part[...] = jnp.broadcast_to(part, (8, HEAD))
    for copy in outs:
        copy.wait()


def attention_back(
    info, query, mine, other, out_weight, attended, sums, raw, cosine, sine, gains, keys, values
):
    return pl.pallas_call(
        attention_back_kernel,
        out_shape=(shape(GROUP, 2 * HEAD, BF), shape(8, HEAD, F32))
        + ((shape(4 * GROUP, HEAD, BF),) * 3 + (shape(2 * GROUP, HEAD, BF),) * 2) * 2,
        in_specs=[scalars()] + [vmem()] * 10 + [anywhere()] * 10,
        out_specs=(vmem(), vmem()) + (anywhere(),) * 10,
        scratch_shapes=[
            pltpu.VMEM((N_BLOCKS * KEYS, HEAD), BF),
            pltpu.VMEM((N_BLOCKS * KEYS, HEAD), BF),
            pltpu.VMEM((4, RUN, HEAD), F32),
            pltpu.VMEM((GROUP, 2 * HEAD), BF),
            pltpu.VMEM((4, 8, RUN), F32),
            pltpu.VMEM((N_BLOCKS * KEYS, HEAD), BF),
            pltpu.VMEM((N_BLOCKS * KEYS, HEAD), BF),
            pltpu.SemaphoreType.DMA((64,)),
        ],
        compiler_params=params(),
        name="attention_back",
        cost_estimate=cost(24),
    )(
        info,
        query,
        mine,
        other,
        out_weight,
        attended,
        sums,
        raw,
        cosine,
        sine,
        gains,
        *keys,
        *values,
    )


def stack_kernel(k0, k1, k2, k3, v0, v1, v2, v3, keys, values):
    for m, (key, value) in enumerate(((k0, v0), (k1, v1), (k2, v2), (k3, v3))):
        rows = slice(m * GROUP, (m + 1) * GROUP)
        keys[rows, :] = key[...]
        values[rows, :] = value[...]


def stack(keys, values):
    return pl.pallas_call(
        stack_kernel,
        out_shape=(shape(4 * GROUP, HEAD, BF),) * 2,
        in_specs=[vmem()] * 8,
        out_specs=(vmem(),) * 2,
        compiler_params=params(),
        name="stack_keys_values",
        cost_estimate=cost(2.3),
    )(*keys, *values)


def forward_kernel(*refs):
    half = 2 * GROUP
    for kind in range(2):
        near, far, for_far, for_near = refs[kind * 4 : kind * 4 + 4]
        out_near, out_far = refs[8 + kind * 2 : 10 + kind * 2]
        out_near[:half, :] = near[:half, :]
        out_near[half:, :] = (near[half:, :].astype(F32) + for_near[...].astype(F32)).astype(BF)
        out_far[:half, :] = (far[:half, :].astype(F32) + for_far[...].astype(F32)).astype(BF)
        out_far[half:, :] = far[half:, :]


def forward_parts(*arrays):
    return pl.pallas_call(
        forward_kernel,
        out_shape=(shape(4 * GROUP, HEAD, BF),) * 4,
        in_specs=[vmem()] * 8,
        out_specs=(vmem(),) * 4,
        compiler_params=params(),
        name="forward_key_value_grads",
        cost_estimate=cost(2),
    )(*arrays)


def sum_kernel(k0, k1, k2, v0, v1, v2, *outs):
    for kind, parts in enumerate(((k0, k1, k2), (v0, v1, v2))):
        for m in range(4):
            rows = slice(m * GROUP, (m + 1) * GROUP)
            total = sum(part[rows, :].astype(F32) for part in parts)
            outs[kind * 4 + m][...] = total.astype(BF)


def sum_parts(*arrays):
    return pl.pallas_call(
        sum_kernel,
        out_shape=(shape(GROUP, HEAD, BF),) * 8,
        in_specs=[vmem()] * 6,
        out_specs=(vmem(),) * 8,
        compiler_params=params(),
        name="sum_key_value_grads",
        cost_estimate=cost(3),
    )(*arrays)


def feed_grads_kernel(info, m1, o1, m2, o2, active, grads, f0, f1, f2, f3, total):
    place = place_of(info)
    top, low = slice(0, RUN), slice(RUN, GROUP)
    total[:, :768] = (
        dot(m2[...], grads[top, :], TN) + dot(o2[...], grads[low, :], TN)
    ).astype(BF)
    total[:, 768:] = (
        dot(m1[...], active[top, :], TN) + dot(o1[...], active[low, :], TN)
    ).astype(BF)
    for mx, out in enumerate((f0, f1, f2, f3)):
        for mz in range(4):
            row = pl.multiple_of((place ^ (mx * 4 + mz)) * 64, 64)
            out[mz * 64 : (mz + 1) * 64, :] = total[pl.ds(row, 64), :]


def feed_grads(info, rows, rows_two, active, grads):
    return pl.pallas_call(
        feed_grads_kernel,
        out_shape=(shape(256, 1152, BF),) * 4,
        in_specs=[scalars()] + [vmem()] * 6,
        out_specs=(vmem(),) * 4,
        scratch_shapes=[pltpu.VMEM((1024, 1152), BF)],
        compiler_params=params(),
        name="feed_grads",
        cost_estimate=cost(5),
    )(info, *rows, *rows_two, active, grads)


def early_kernel(info, m1, o1, mg, og, grad_raw, attended, e0, e1, e2, e3, total):
    place = place_of(info)
    top, low = slice(0, RUN), slice(RUN, GROUP)
    total[:, :256] = (
        dot(m1[...], grad_raw[top, :], TN) + dot(o1[...], grad_raw[low, :], TN)
    ).astype(BF)
    total[:, 256:] = (
        dot(mg[...], attended[top, :], TN) + dot(og[...], attended[low, :], TN)
    ).astype(BF)
    for mx, out in enumerate((e0, e1, e2, e3)):
        for mz in range(4):
            row = pl.multiple_of((place ^ (mx * 4 + mz)) * 64, 64)
            out[mz * 64 : (mz + 1) * 64, :] = total[pl.ds(row, 64), :]


def early_grads(info, rows, grad_rows, grad_raw, attended):
    return pl.pallas_call(
        early_kernel,
        out_shape=(shape(256, 512, BF),) * 4,
        in_specs=[scalars()] + [vmem()] * 6,
        out_specs=(vmem(),) * 4,
        scratch_shapes=[pltpu.VMEM((1024, 512), BF)],
        compiler_params=params(),
        name="early_grads",
        cost_estimate=cost(4),
    )(info, *rows, *grad_rows, grad_raw, attended)


def last_kernel(
    info,
    m1,
    o1,
    weight,
    grad_raw,
    query_part,
    raw,
    cosine,
    sine,
    gains,
    k0,
    k1,
    k2,
    k3,
    v0,
    v1,
    v2,
    v3,
    mine_down,
    other_down,
    mine,
    other,
    l0,
    l1,
    l2,
    l3,
    grads,
    total,
):
    place = place_of(info)
    part = jnp.zeros((1, HEAD), F32)
    for half, (out, down) in enumerate(((mine, mine_down), (other, other_down))):
        here = slice(half * RUN, (half + 1) * RUN)
        out[:, 1024:] = down[...]
        key_grad = sum(k[here, :].astype(F32) for k in (k0, k1, k2, k3))
        value_grad = sum(v[here, :].astype(F32) for v in (v0, v1, v2, v3))
        grads[here, :HEAD], one = head_back(
            key_grad, raw[here, 2 * HEAD :], gains[1:2, :], cosine[here, :], sine[here, :]
        )
        grads[here, HEAD:] = value_grad.astype(BF)
        part = part + one
        out[:, :1024] = (
            dot(grad_raw[here, :], weight[:, : 2 * HEAD], NT)
            + dot(grads[here, :], weight[:, 2 * HEAD : 4 * HEAD], NT)
        ).astype(BF)
    total[...] = (
        dot(m1[...], grads[:RUN, :], TN) + dot(o1[...], grads[RUN:, :], TN)
    ).astype(BF)
    row = lax.broadcasted_iota(jnp.int32, (64, 1), 0)
    heads = jnp.where(row == 0, query_part[0:1, :], jnp.where(row == 1, part, 0.0)).astype(BF)
    for mx, out in enumerate((l0, l1, l2, l3)):
        for mz in range(4):
            row = pl.multiple_of((place ^ (mx * 4 + mz)) * 64, 64)
            here = slice(mz * 64, (mz + 1) * 64)
            out[here, : 2 * HEAD] = total[pl.ds(row, 64), :]
            out[here, 2 * HEAD :] = heads


def last_step(info, rows, weight, grad_raw, query_part, raw, cosine, sine, gains, *parts):
    return pl.pallas_call(
        last_kernel,
        out_shape=(shape(RUN, 2048, BF),) * 2 + (shape(256, 3 * HEAD, BF),) * 4,
        in_specs=[scalars()] + [vmem()] * 19,
        out_specs=(vmem(),) * 6,
        scratch_shapes=[pltpu.VMEM((GROUP, 2 * HEAD), BF), pltpu.VMEM((1024, 2 * HEAD), BF)],
        compiler_params=params(),
        name="last_step",
        cost_estimate=cost(6),
    )(info, *rows, weight, grad_raw, query_part, raw, cosine, sine, gains, *parts)


def local(
    tokens,
    positions,
    sequence_ids,
    attn_gain,
    query_weight,
    key_matrix,
    value_matrix,
    query_gain,
    key_gain,
    output_weight,
    mlp_gain,
    gate_weight,
    up_weight,
    down_weight,
    out_grad,
):
    xi, zl, co, zh, yi = (lax.axis_index(name) for name in AXES)
    place = xi * 4 + zl * 2 + zh
    start_one = jnp.sum(sequence_ids < 1, dtype=jnp.int32)
    start_two = jnp.sum(sequence_ids < 2, dtype=jnp.int32)
    info = jnp.stack([xi, zl, zh, co, yi, start_one, start_two]).astype(jnp.int32)

    gain_one = attn_gain.astype(F32)[:, None]
    gain_two = mlp_gain.astype(F32)[:, None]
    weights = prepare(
        attn_gain.reshape(1, 64),
        mlp_gain.reshape(1, 64),
        query_weight,
        key_matrix,
        value_matrix,
        output_weight.T,
        gate_weight,
        up_weight,
        down_weight.T,
    )
    one_own, two_own = gather_chunk(weights)
    one_weights = [one_own] + [swap_with(one_own, "z", m) for m in (1, 2, 3)]

    both = exchange_runs(jnp.concatenate([tokens, out_grad], axis=1))
    resid, out_grad = both[:, :1024].astype(F32), both[:, 1024:]
    normal_one, inverse_one = rms_parts(resid)
    rows_mine, rows_other = gather_rows(normal_one.astype(BF))
    out_grad, rows_other = lax.optimization_barrier((out_grad, rows_other))
    rows_one = (rows_mine, rows_other)
    cotangent = out_grad.astype(F32)
    grad_mine, grad_other = gather_rows(out_grad)

    run_places = positions.reshape(32, 4, 64)
    run_places = jnp.stack(
        [
            lax.dynamic_index_in_dim(run_places, run_of(xi * 2 + zl, co ^ half, zh), 0, False)
            for half in range(2)
        ]
    )
    run_places = jnp.where((yi & 1) == 1, run_places[:, jnp.array([1, 0, 3, 2])], run_places)
    run_places = jnp.where((yi & 2) == 2, run_places[:, jnp.array([2, 3, 0, 1])], run_places)
    half_size = HEAD // 2
    lane = jnp.arange(HEAD)
    frequency = jnp.exp(
        -jnp.log(ROPE_BASE) * 2.0 * (lane % half_size).astype(F32) / HEAD
    )
    angles = run_places.reshape(GROUP).astype(F32)[:, None] * frequency[None, :]
    cosine = jnp.cos(angles)
    sine = jnp.sin(angles) * jnp.where(lane < half_size, -1.0, 1.0)
    gains = jnp.stack([query_gain, key_gain]).astype(F32)
    query, key, value, raw, weight_full = project(
        info, *rows_one, one_weights, cosine, sine, gains
    )

    two_own, grad_mine, key = lax.optimization_barrier((two_own, grad_mine, key))
    two_weights = [two_own, None, swap_with(two_own, "z", 2), None]
    keys_x = [key] + [swap_with(key, "x", m) for m in (1, 2, 3)]
    values_z = [value] + [swap_with(value, "z", m) for m in (1, 2, 3)]
    keys_x, two_weights[2] = lax.optimization_barrier((keys_x, two_weights[2]))
    key_own, value_own = stack(keys_x, values_z)
    key_parts = gather_steps(key_own, "z")
    value_parts = gather_steps(value_own, "x")
    two_own, key_parts, value_parts, grad_other = lax.optimization_barrier(
        (two_own, key_parts, value_parts, grad_other)
    )
    grad_rows = (grad_mine, grad_other)
    two_weights[1] = swap_with(two_own, "z", 1)
    two_weights[3] = swap_with(two_own, "z", 3)

    attended, sums, mine, other = attention_forward(
        info, query, weight_full, key_parts, value_parts
    )
    mine, other, two_weights[1] = lax.optimization_barrier((mine, other, two_weights[1]))
    hidden = resid + scatter_rows(mine, other)
    normal_two, inverse_two = rms_parts(hidden)
    rows_mine = gather_along_y(normal_two.astype(BF))
    rows_mine, two_weights[3] = lax.optimization_barrier((rows_mine, two_weights[3]))
    rows_two = (rows_mine, swap_with(rows_mine, "core", 1))

    active, grad_gate_up, mine, other, mine_down, other_down = feed(
        info, *rows_two, *grad_rows, two_weights
    )
    scaled_two = scatter_rows(mine, other)
    grad_hidden = cotangent + rms_back(scaled_two, normal_two, inverse_two)
    grad_rows_one = gather_rows(grad_hidden.astype(BF))
    two_parts = feed_grads(info, grad_rows, rows_two, active, grad_gate_up)
    two_parts, grad_rows_one = lax.optimization_barrier((two_parts, grad_rows_one))
    two_parts = [two_parts[0]] + [swap_with(two_parts[m], "x", m) for m in (1, 2, 3)]

    grad_raw, query_part, *key_value_grads = attention_back(
        info,
        query,
        *grad_rows_one,
        weight_full,
        attended,
        sums,
        raw,
        cosine,
        sine,
        gains,
        key_parts,
        value_parts,
    )
    key_value_grads, two_parts = lax.optimization_barrier((key_value_grads, two_parts))
    key_grads, value_grads = key_value_grads[:5], key_value_grads[5:]
    forwarded = forward_parts(
        key_grads[1],
        key_grads[2],
        swap_with(key_grads[3], "z", NEIGHBOURS["z"][0]),
        swap_with(key_grads[4], "z", NEIGHBOURS["z"][1]),
        value_grads[1],
        value_grads[2],
        swap_with(value_grads[3], "x", NEIGHBOURS["x"][0]),
        swap_with(value_grads[4], "x", NEIGHBOURS["x"][1]),
    )
    early = early_grads(info, rows_one, grad_rows_one, grad_raw, attended)
    summed = sum_parts(
        key_grads[0],
        swap_with(forwarded[0], "z", NEIGHBOURS["z"][0]),
        swap_with(forwarded[1], "z", NEIGHBOURS["z"][1]),
        value_grads[0],
        swap_with(forwarded[2], "x", NEIGHBOURS["x"][0]),
        swap_with(forwarded[3], "x", NEIGHBOURS["x"][1]),
    )
    early, summed = lax.optimization_barrier((early, summed))
    key_grads = [summed[0]] + [swap_with(summed[m], "x", m) for m in (1, 2, 3)]
    value_grads = [summed[4]] + [swap_with(summed[4 + m], "z", m) for m in (1, 2, 3)]
    early = [early[0]] + [swap_with(early[m], "x", m) for m in (1, 2, 3)]
    key_grads, value_grads, early = lax.optimization_barrier((key_grads, value_grads, early))

    mine, other, *late = last_step(
        info,
        rows_one,
        weight_full,
        grad_raw,
        query_part,
        raw,
        cosine,
        sine,
        gains,
        *key_grads,
        *value_grads,
        mine_down,
        other_down,
    )
    late = [late[0]] + [swap_with(late[m], "x", m) for m in (1, 2, 3)]
    totals = [
        sum(part.astype(F32) for part in parts).astype(BF) for parts in (two_parts, early, late)
    ]
    received = swap_with(other, "core", 1)
    halves = [
        jnp.concatenate([v[m * 64 : (m + 1) * 64] for v in totals], axis=1) for m in range(4)
    ]
    parts = [
        mine[m * 64 : (m + 1) * 64].astype(F32) + received[m * 64 : (m + 1) * 64].astype(F32)
        for m in range(4)
    ]
    halves, parts = lax.optimization_barrier((halves, parts))
    own = sum(chunk_along_z(halves[m], m).astype(F32) for m in range(4))
    both = scatter_axis(parts, "y")
    output = hidden + both[:, 1024:]
    token_grad = grad_hidden + rms_back(both[:, :1024], normal_one, inverse_one)
    both = exchange_runs(jnp.concatenate([output.astype(BF), token_grad.astype(BF)], axis=1))
    output, token_grad = both[:, :1024], both[:, 1024:].astype(F32)

    gate_part, up_part, down_part = own[:, :384], own[:, 384:768], own[:, 768:1152]
    query_part, output_part = own[:, 1152:1408], own[:, 1408:1664]
    key_part, value_part = own[:, 1664:1792], own[:, 1792:1920]
    attn_part = (
        jnp.sum(query_part * query_weight.astype(F32), axis=1)
        + jnp.sum(key_part * key_matrix.astype(F32), axis=1)
        + jnp.sum(value_part * value_matrix.astype(F32), axis=1)
    )
    mlp_part = jnp.sum(
        gate_part * gate_weight.astype(F32) + up_part * up_weight.astype(F32), axis=1
    )
    sums_all = jnp.concatenate([attn_part, mlp_part, own[0, 1920:], own[1, 1920:]])
    received = [swap_with(sums_all, "y", m) for m in (1, 2, 3)]
    for part in received:
        sums_all = sums_all + part
    sums_all = sums_all + swap_with(sums_all, "z", 1)
    gain_parts, head_parts = sums_all[:128], sums_all[128:]
    return (
        output,
        token_grad,
        gain_parts[:64],
        query_part * gain_one,
        key_part * gain_one,
        value_part * gain_one,
        head_parts[:HEAD],
        head_parts[HEAD:],
        output_part.T,
        gain_parts[64:],
        gate_part * gain_two,
        up_part * gain_two,
        down_part.T,
    )


def solution(mesh):
    parts = Mesh(mesh.devices.reshape(4, 2, 2, 2, 4), AXES)
    ctx, tp = ("x", "zl", "core"), ("zh", "y")
    tokens, matrix, turned = P(AXES, None), P(ctx, tp), P(tp, ctx)
    return jax.shard_map(
        local,
        mesh=parts,
        in_specs=(
            tokens,
            P(),
            P(),
            P(ctx),
            matrix,
            matrix,
            matrix,
            P(),
            P(),
            turned,
            P(ctx),
            matrix,
            matrix,
            turned,
            tokens,
        ),
        out_specs=(
            tokens,
            tokens,
            P(ctx),
            matrix,
            matrix,
            matrix,
            P(),
            P(),
            turned,
            P(ctx),
            matrix,
            matrix,
            turned,
        ),
        check_vma=False,
    )
```

```python
import jax
import jax.numpy as jnp
from jax import lax
from jax.experimental import pallas as pl
from jax.experimental.pallas import tpu as pltpu
from jax.sharding import Mesh, PartitionSpec as P

AXES = ("x", "zl", "core", "zh", "y")
EPS = 1e-06
ROPE_BASE = 1000000.0
HEAD = 128
RUN = 256
GROUP = 512
KEYS = 512
N_BLOCKS = 16
LOG2E = 1.4426950408889634
LN2 = 0.6931471805599453
Q_SCALE = LOG2E * HEAD ** (-0.5)
BF = jnp.bfloat16
F32 = jnp.float32
VMEM_LIMIT = 60 * 1024 * 1024


NEIGHBOURS = {"x": (1, 3), "z": (2, 3)}


def swap_with(value, axis, mask):
    if axis == "z":
        return lax.ppermute(value, ("zl", "zh"), [(i, i ^ mask) for i in range(4)])
    size = 2 if axis == "core" else 4
    return lax.ppermute(value, axis, [(i, i ^ mask) for i in range(size)])


def chunk_along_x(value, mask):
    moves = [
        ((x * 2 + core) * 2 + zh, ((x ^ mask) * 2 + zh) * 2 + core)
        for x in range(4)
        for core in range(2)
        for zh in range(2)
    ]
    return lax.ppermute(value, ("x", "core", "zh"), moves)


def chunk_along_z(value, mask):
    moves = [
        ((zl * 2 + core) * 2 + zh, ((zl ^ (mask >> 1)) * 2 + (zh ^ (mask & 1))) * 2 + core)
        for zl in range(2)
        for core in range(2)
        for zh in range(2)
    ]
    return lax.ppermute(value, ("zl", "core", "zh"), moves)


def exchange_runs(value):
    mirror = [(i, i ^ 14 if i % 2 else i) for i in range(16)]
    return lax.ppermute(value, ("x", "zl", "core"), mirror)


def gather_chunk(value):
    parts = [chunk_along_x(value, m) for m in range(4)]
    return [jnp.concatenate([p[:, c] for p in parts]) for c in (slice(0, 768), slice(768, 1920))]


def scatter_axis(parts, axis):
    total = parts[0].astype(F32)
    for m in (1, 2, 3):
        total = total + swap_with(parts[m].astype(BF), axis, m).astype(F32)
    return total


def gather_steps(value, axis):
    near, far = NEIGHBOURS[axis]
    half = value.shape[0] // 2
    one, two = swap_with(value, axis, near), swap_with(value, axis, far)
    return [value, one, two, swap_with(two[:half], axis, near), swap_with(one[half:], axis, far)]


def gather_along_y(block):
    return jnp.concatenate([block] + [swap_with(block, "y", m) for m in (1, 2, 3)], axis=0)


def gather_rows(block):
    half = gather_along_y(block)
    return half, swap_with(half, "core", 1)


def scatter_rows(mine, other):
    received = swap_with(other, "core", 1)
    parts = [
        mine[m * 64 : (m + 1) * 64].astype(F32) + received[m * 64 : (m + 1) * 64].astype(F32)
        for m in range(4)
    ]
    return scatter_axis(parts, "y")


def rms_parts(value):
    inverse = lax.rsqrt(jnp.mean(value * value, axis=-1, keepdims=True) + EPS)
    return value * inverse, inverse


def rms_back(scaled, normal, inverse):
    return inverse * (scaled - normal * jnp.mean(scaled * normal, axis=-1, keepdims=True))


def dot(left, right, contract):
    return lax.dot_general(left, right, (contract, ((), ())), preferred_element_type=F32)


NN = ((1,), (0,))
NT = ((1,), (1,))
TN = ((0,), (0,))


def stream_index(spot, yi):
    return (((spot >> 6) ^ yi) << 6) | (spot & 63)


def vmem():
    return pl.BlockSpec(memory_space=pltpu.VMEM)


def anywhere():
    return pl.BlockSpec(memory_space=pl.ANY)


def scalars():
    return pl.BlockSpec(memory_space=pltpu.SMEM)


def params():
    return pltpu.CompilerParams(vmem_limit_bytes=VMEM_LIMIT)


def cost(microseconds):
    return pl.CostEstimate(
        flops=int(microseconds * 1.15e9), transcendentals=0, bytes_accessed=1 << 20
    )


def shape(rows, columns, kind):
    return jax.ShapeDtypeStruct((rows, columns), kind)


def place_of(info):
    return info[0] * 4 + info[1] * 2 + info[2]


def rotate_lanes(value, cosine, sine):
    return value * cosine + pltpu.roll(value, HEAD // 2, 1) * sine


def normed(value):
    inverse = lax.rsqrt(jnp.mean(value * value, axis=-1, keepdims=True) + EPS)
    return value * inverse, inverse


def column_of(row):
    diagonal = lax.broadcasted_iota(jnp.int32, (64, 64), 0) == lax.broadcasted_iota(
        jnp.int32, (64, 64), 1
    )
    return jnp.sum(jnp.where(diagonal, row, 0.0), axis=1, keepdims=True)


def prepare_kernel(gain_one, gain_two, query, key, value, output, gate, up, down, out):
    first = column_of(gain_one[...].astype(F32))
    second = column_of(gain_two[...].astype(F32))
    out[:, :256] = (query[...].astype(F32) * first).astype(BF)
    out[:, 256:384] = (key[...].astype(F32) * first).astype(BF)
    out[:, 384:512] = (value[...].astype(F32) * first).astype(BF)
    out[:, 512:768] = output[...]
    out[:, 768:1152] = (gate[...].astype(F32) * second).astype(BF)
    out[:, 1152:1536] = (up[...].astype(F32) * second).astype(BF)
    out[:, 1536:] = down[...]


def prepare(*arrays):
    return pl.pallas_call(
        prepare_kernel,
        out_shape=shape(64, 1920, BF),
        in_specs=[vmem()] * 9,
        out_specs=vmem(),
        compiler_params=params(),
        name="prepare_weights",
        cost_estimate=cost(2),
    )(*arrays)


def weight_copies(info, parts, weight, sems):
    place = place_of(info)
    copies = []
    for mz, part in enumerate(parts):
        for mx in range(4):
            row = pl.multiple_of((place ^ (mx * 4 + mz)) * 64, 64)
            copies.append(
                pltpu.make_async_copy(
                    part.at[pl.ds(mx * 64, 64)], weight.at[pl.ds(row, 64)], sems.at[mz * 4 + mx]
                )
            )
    return copies


def project_kernel(
    info, mine, other, w0, w1, w2, w3, cosine, sine, gains, query, key, value, raw, weight, sems
):
    copies = weight_copies(info, (w0, w1, w2, w3), weight, sems)
    for copy in copies:
        copy.start()
    for copy in copies:
        copy.wait()
    for half, rows in enumerate((mine, other)):
        here = slice(half * RUN, (half + 1) * RUN)
        product = dot(rows[...], weight[:, : 4 * HEAD], NN)
        raw[here, :] = product[:, : 3 * HEAD]
        value[here, :] = product[:, 3 * HEAD :].astype(BF)
        for head in range(3):
            normal, _ = normed(product[:, head * HEAD : (head + 1) * HEAD])
            gain = gains[0:1, :] if head < 2 else gains[1:2, :]
            turned = rotate_lanes(normal * gain, cosine[here, :], sine[here, :])
            if head < 2:
                query[here, head * HEAD : (head + 1) * HEAD] = (turned * Q_SCALE).astype(BF)
            else:
                key[here, :] = turned.astype(BF)


def project(info, mine, other, parts, cosine, sine, gains):
    return pl.pallas_call(
        project_kernel,
        out_shape=(
            shape(GROUP, 2 * HEAD, BF),
            shape(GROUP, HEAD, BF),
            shape(GROUP, HEAD, BF),
            shape(GROUP, 3 * HEAD, F32),
            shape(1024, 6 * HEAD, BF),
        ),
        in_specs=[scalars(), vmem(), vmem()] + [anywhere()] * 4 + [vmem()] * 3,
        out_specs=(vmem(),) * 5,
        scratch_shapes=[pltpu.SemaphoreType.DMA((16,))],
        compiler_params=params(),
        name="project",
        cost_estimate=cost(5.5),
    )(info, mine, other, *parts, cosine, sine, gains)


def run_of(group, core, zh):
    return ((group ^ (7 * core)) * 2 + core) * 2 + zh


def key_copies(info, key_parts, value_parts, key_all, value_all, sems):
    xi, zl, zh, co = info[0], info[1], info[2], info[3]
    copies = []
    for kind, (parts, target, axis) in enumerate(
        ((key_parts, key_all, "z"), (value_parts, value_all, "x"))
    ):
        near, far = NEIGHBOURS[axis]
        pieces = [(0, parts[0], 0), (near, parts[1], 0), (far, parts[2], 0)]
        pieces += [(near ^ far, parts[3], 0), (near ^ far, parts[4], 2)]
        for turn, source, first in pieces:
            for sub in range(first, min(first + source.shape[0] // GROUP, 4)):
                mx, mz = (sub, turn) if kind == 0 else (turn, sub)
                group = (xi ^ mx) * 2 + (zl ^ (mz >> 1))
                for half in range(2):
                    row = run_of(group, co ^ half, zh ^ (mz & 1)) * RUN
                    copies.append(
                        pltpu.make_async_copy(
                            source.at[pl.ds((sub - first) * GROUP + half * RUN, RUN)],
                            target.at[pl.ds(pl.multiple_of(row, RUN), RUN)],
                            sems.at[len(copies)],
                        )
                    )
    return copies


def first_of(token, start_one, start_two):
    return jnp.where(
        token >= start_two, start_two, jnp.where(token >= start_one, start_one, 0)
    )


def spans(group, core):
    mine = (group ^ (7 * core)) * 2 + core
    theirs = (group ^ (7 * (1 - core))) * 2 + 1 - core
    big = jnp.where(theirs > mine, 1, 0)
    return jnp.minimum(mine, theirs), jnp.maximum(mine, theirs), big


def attention_kernel(
    info,
    query,
    out_weight,
    k0,
    k1,
    k2,
    k3,
    k4,
    v0,
    v1,
    v2,
    v3,
    v4,
    out,
    sums,
    mine,
    other,
    key_all,
    value_all,
    totals,
    sems,
):
    copies = key_copies(info, (k0, k1, k2, k3, k4), (v0, v1, v2, v3, v4), key_all, value_all, sems)
    for copy in copies:
        copy.start()
    for copy in copies:
        copy.wait()
    xi, zl, zh, co, yi = (info[i] for i in range(5))
    start_one, start_two = info[5], info[6]
    group = xi * 2 + zl
    low, high, big = spans(group, co)
    ones = jnp.ones((KEYS, HEAD), BF)
    row_spot = stream_index(lax.broadcasted_iota(jnp.int32, (RUN, 1), 0), yi)
    totals[...] = jnp.zeros_like(totals)

    def tokens_of(half):
        token = run_of(group, co ^ half, zh) * RUN + row_spot
        return token, first_of(token, start_one, start_two)

    def block(index, masked, halves):
        rows = pl.ds(pl.multiple_of(index * KEYS, KEYS), KEYS)
        keys = key_all[rows, :]
        values = jnp.concatenate([value_all[rows, :], ones], axis=1)
        spot = lax.broadcasted_iota(jnp.int32, (1, KEYS), 1)
        key_tokens = index * KEYS + (spot & ~(RUN - 1)) + stream_index(spot & (RUN - 1), yi)
        for half in halves:
            rows_here = pl.ds(pl.multiple_of(half * RUN, RUN), RUN)
            if masked:
                token, start = tokens_of(half)
                allowed = (key_tokens <= token) & (key_tokens >= start)
            for head in range(2):
                scores = dot(query[rows_here, head * HEAD : (head + 1) * HEAD], keys, NT)
                weights = jnp.exp2(scores)
                if masked:
                    weights = jnp.where(allowed, weights, 0.0)
                totals[half * 2 + head] += dot(weights.astype(BF), values, NN)

    def full_both(index, carry):
        block(index, False, (0, 1))
        return carry

    def full_big(step, carry):
        block(low + 1 + 2 * step, False, (big,))
        block(low + 2 + 2 * step, False, (big,))
        return carry

    lax.fori_loop(1, low, full_both, 0)
    lax.fori_loop(0, (high - 1 - low) // 2, full_big, 0)
    for half in range(2):
        keep = tokens_of(half)[1] <= KEYS
        for head in range(2):
            totals[half * 2 + head] = jnp.where(keep, totals[half * 2 + head], 0.0)
    block(jnp.int32(0), True, (0, 1))

    @pl.when(low > 0)
    def _():
        block(low, True, (0, 1))

    block(high, True, (big,))
    for half in range(2):
        for head in range(2):
            total = totals[half * 2 + head]
            weight_sum = total[:, HEAD:]
            out[half * RUN : (half + 1) * RUN, head * HEAD : (head + 1) * HEAD] = (
                total[:, :HEAD] / weight_sum
            ).astype(BF)
            sums[half * 2 + head] = jnp.log2(weight_sum).T[:8]
    mine[...] = dot(out[:RUN, :], out_weight[:, 4 * HEAD :], NT).astype(BF)
    other[...] = dot(out[RUN:, :], out_weight[:, 4 * HEAD :], NT).astype(BF)


def attention_forward(info, query, out_weight, key_parts, value_parts):
    return pl.pallas_call(
        attention_kernel,
        out_shape=(
            shape(GROUP, 2 * HEAD, BF),
            jax.ShapeDtypeStruct((4, 8, RUN), F32),
            shape(RUN, 1024, BF),
            shape(RUN, 1024, BF),
        ),
        in_specs=[scalars(), vmem(), vmem()] + [anywhere()] * 10,
        out_specs=(vmem(),) * 4,
        scratch_shapes=[
            pltpu.VMEM((N_BLOCKS * KEYS, HEAD), BF),
            pltpu.VMEM((N_BLOCKS * KEYS, HEAD), BF),
            pltpu.VMEM((4, RUN, 2 * HEAD), F32),
            pltpu.SemaphoreType.DMA((64,)),
        ],
        compiler_params=params(),
        name="attention_forward",
        cost_estimate=cost(13),
    )(info, query, out_weight, *key_parts, *value_parts)


def feed_kernel(
    info,
    mine,
    other,
    mine_grad,
    other_grad,
    w0,
    w1,
    w2,
    w3,
    active,
    grads,
    mine_out,
    other_out,
    mine_down,
    other_down,
    weight,
    sems,
):
    copies = weight_copies(info, (w0, w1, w2, w3), weight, sems)
    for copy in copies:
        copy.start()
    for copy in copies:
        copy.wait()
    for half, (rows, rows_grad, out) in enumerate(
        ((mine, mine_grad, mine_out), (other, other_grad, other_out))
    ):
        here = slice(half * RUN, (half + 1) * RUN)
        gate_up = dot(rows[...], weight[:, :768], NN)
        gate, up = gate_up[:, :384], gate_up[:, 384:]
        sigmoid = 1.0 / (1.0 + jnp.exp(-gate))
        swish = gate * sigmoid
        active[here, :] = (swish * up).astype(BF)
        grad_active = dot(rows_grad[...], weight[:, 768:], NN)
        slope = sigmoid * (1.0 + gate * (1.0 - sigmoid))
        grads[here, :384] = (grad_active * up * slope).astype(BF)
        grads[here, 384:] = (grad_active * swish).astype(BF)
        out[...] = dot(grads[here, :], weight[:, :768], NT).astype(BF)
    mine_down[...] = dot(active[:RUN, :], weight[:, 768:], NT).astype(BF)
    other_down[...] = dot(active[RUN:, :], weight[:, 768:], NT).astype(BF)


def feed(info, mine, other, mine_grad, other_grad, parts):
    return pl.pallas_call(
        feed_kernel,
        out_shape=(shape(GROUP, 384, BF), shape(GROUP, 768, BF)) + (shape(RUN, 1024, BF),) * 4,
        in_specs=[scalars()] + [vmem()] * 4 + [anywhere()] * 4,
        out_specs=(vmem(),) * 6,
        scratch_shapes=[pltpu.VMEM((1024, 1152), BF), pltpu.SemaphoreType.DMA((16,))],
        compiler_params=params(),
        name="feed",
        cost_estimate=cost(7.5),
    )(info, mine, other, mine_grad, other_grad, *parts)


def head_back(gradient, raw, gain, cosine, sine):
    normal, inverse = normed(raw)
    turned = rotate_lanes(gradient, cosine, -sine)
    part = jnp.sum(turned * normal, axis=0, keepdims=True)
    scaled = turned * gain
    mean = jnp.mean(scaled * normal, axis=-1, keepdims=True)
    return (inverse * (scaled - normal * mean)).astype(BF), part


def attention_back_kernel(
    info,
    query,
    mine,
    other,
    out_weight,
    attended,
    sums,
    raw,
    cosine,
    sine,
    gains,
    k0,
    k1,
    k2,
    k3,
    k4,
    v0,
    v1,
    v2,
    v3,
    v4,
    grad_raw,
    gain_part,
    gk0,
    gk1,
    gk2,
    gk3,
    gk4,
    gv0,
    gv1,
    gv2,
    gv3,
    gv4,
    key_all,
    value_all,
    totals,
    grad,
    deltas,
    grad_key,
    grad_value,
    sems,
):
    copies = key_copies(info, (k0, k1, k2, k3, k4), (v0, v1, v2, v3, v4), key_all, value_all, sems)
    for copy in copies:
        copy.start()
    for half, rows_in in enumerate((mine, other)):
        here = slice(half * RUN, (half + 1) * RUN)
        rows_grad = dot(rows_in[...], out_weight[:, 4 * HEAD :], NN).astype(BF)
        grad[here, :] = rows_grad
        products = rows_grad.astype(F32) * attended[here, :].astype(F32)
        for head in range(2):
            turned = products[:, head * HEAD : (head + 1) * HEAD].T
            deltas[half * 2 + head] = jnp.broadcast_to(
                jnp.sum(turned, axis=0, keepdims=True), (8, RUN)
            )
    for copy in copies:
        copy.wait()
    xi, zl, zh, co, yi = (info[i] for i in range(5))
    start_one, start_two = info[5], info[6]
    group = xi * 2 + zl
    low, high, big = spans(group, co)
    column_spot = stream_index(lax.broadcasted_iota(jnp.int32, (1, RUN), 1), yi)

    def tokens_of(half):
        token = run_of(group, co ^ half, zh) * RUN + column_spot
        return token, first_of(token, start_one, start_two)

    totals[...] = jnp.zeros_like(totals)

    def places(index):
        owner_core = index % 2
        owner = (index // 2) ^ (7 * owner_core)
        mx = (owner // 2) ^ xi
        half = owner_core ^ co
        spots = []
        for run in range(2):
            mz = ((owner % 2) ^ zl) * 2 + (run ^ zh)
            spots.append((mx, mz, half))
        return spots

    def store(index, key_grad, value_grad):
        for run, (mx, mz, half) in enumerate(places(index)):
            rows = slice(run * RUN, (run + 1) * RUN)
            key_row = (mz * 4 + mx) * GROUP + half * RUN
            value_row = (mx * 4 + mz) * GROUP + half * RUN
            grad_key[pl.ds(pl.multiple_of(key_row, RUN), RUN), :] = key_grad[rows]
            grad_value[pl.ds(pl.multiple_of(value_row, RUN), RUN), :] = value_grad[rows]

    def block(index, masked, halves):
        rows = pl.ds(pl.multiple_of(index * KEYS, KEYS), KEYS)
        keys = key_all[rows, :]
        values = value_all[rows, :]
        spot = lax.broadcasted_iota(jnp.int32, (KEYS, 1), 0)
        key_tokens = index * KEYS + (spot & ~(RUN - 1)) + stream_index(spot & (RUN - 1), yi)
        key_grad = jnp.zeros((KEYS, HEAD), F32)
        value_grad = jnp.zeros((KEYS, HEAD), F32)
        for half in halves:
            rows_here = pl.ds(pl.multiple_of(half * RUN, RUN), RUN)
            token, start = tokens_of(half)
            if masked:
                allowed = (key_tokens <= token) & (key_tokens >= start)
            for head in range(2):
                lanes = slice(head * HEAD, (head + 1) * HEAD)
                queries = query[rows_here, lanes]
                grads = grad[rows_here, lanes]
                level = sums[half * 2 + head][0:1, :]
                if not masked:
                    level = jnp.where(start <= KEYS, level, 1e30)
                probs = jnp.exp2(dot(keys, queries, NT) - level)
                if masked:
                    probs = jnp.where(allowed, probs, 0.0)
                grad_probs = dot(values, grads, NT)
                grad_scores = (probs * (grad_probs - deltas[half * 2 + head][0:1, :])).astype(BF)
                value_grad = value_grad + dot(probs.astype(BF), grads, NN)
                key_grad = key_grad + dot(grad_scores, queries, NN)
                totals[half * 2 + head] += dot(grad_scores, keys, TN)
        store(index, (key_grad * LN2).astype(BF), value_grad.astype(BF))

    def full_both(index, carry):
        block(index, False, (0, 1))
        return carry

    def full_big(step, carry):
        block(low + 1 + 2 * step, False, (big,))
        block(low + 2 + 2 * step, False, (big,))
        return carry

    lax.fori_loop(1, low, full_both, 0)
    lax.fori_loop(0, (high - 1 - low) // 2, full_big, 0)
    block(jnp.int32(0), True, (0, 1))

    @pl.when(low > 0)
    def _():
        block(low, True, (0, 1))

    block(high, True, (big,))

    def empty(index, carry):
        nothing = jnp.zeros((KEYS, HEAD), BF)
        store(index, nothing, nothing)
        return carry

    lax.fori_loop(high + 1, N_BLOCKS, empty, 0)
    outs = []
    for source, targets, axis in (
        (grad_key, (gk0, gk1, gk2, gk3, gk4), "z"),
        (grad_value, (gv0, gv1, gv2, gv3, gv4), "x"),
    ):
        near, far = NEIGHBOURS[axis]
        block = 4 * GROUP
        starts = (0, near * block, far * block, (near ^ far) * block, (near ^ far) * block + block // 2)
        for start, target in zip(starts, targets):
            outs.append(
                pltpu.make_async_copy(
                    source.at[pl.ds(start, target.shape[0])], target, sems.at[len(outs)]
                )
            )
    for copy in outs:
        copy.start()
    part = jnp.zeros((1, HEAD), F32)
    for half in range(2):
        here = slice(half * RUN, (half + 1) * RUN)
        for head in range(2):
            lanes = slice(head * HEAD, (head + 1) * HEAD)
            grad_raw[here, lanes], one = head_back(
                totals[half * 2 + head] * HEAD ** (-0.5),
                raw[here, lanes],
                gains[0:1, :],
                cosine[here, :],
                sine[here, :],
            )
            part = part + one
    gain_part[...] = jnp.broadcast_to(part, (8, HEAD))
    for copy in outs:
        copy.wait()


def attention_back(
    info, query, mine, other, out_weight, attended, sums, raw, cosine, sine, gains, keys, values
):
    return pl.pallas_call(
        attention_back_kernel,
        out_shape=(shape(GROUP, 2 * HEAD, BF), shape(8, HEAD, F32))
        + ((shape(4 * GROUP, HEAD, BF),) * 3 + (shape(2 * GROUP, HEAD, BF),) * 2) * 2,
        in_specs=[scalars()] + [vmem()] * 10 + [anywhere()] * 10,
        out_specs=(vmem(), vmem()) + (anywhere(),) * 10,
        scratch_shapes=[
            pltpu.VMEM((N_BLOCKS * KEYS, HEAD), BF),
            pltpu.VMEM((N_BLOCKS * KEYS, HEAD), BF),
            pltpu.VMEM((4, RUN, HEAD), F32),
            pltpu.VMEM((GROUP, 2 * HEAD), BF),
            pltpu.VMEM((4, 8, RUN), F32),
            pltpu.VMEM((N_BLOCKS * KEYS, HEAD), BF),
            pltpu.VMEM((N_BLOCKS * KEYS, HEAD), BF),
            pltpu.SemaphoreType.DMA((64,)),
        ],
        compiler_params=params(),
        name="attention_back",
        cost_estimate=cost(24),
    )(
        info,
        query,
        mine,
        other,
        out_weight,
        attended,
        sums,
        raw,
        cosine,
        sine,
        gains,
        *keys,
        *values,
    )


def stack_kernel(k0, k1, k2, k3, v0, v1, v2, v3, keys, values):
    for m, (key, value) in enumerate(((k0, v0), (k1, v1), (k2, v2), (k3, v3))):
        rows = slice(m * GROUP, (m + 1) * GROUP)
        keys[rows, :] = key[...]
        values[rows, :] = value[...]


def stack(keys, values):
    return pl.pallas_call(
        stack_kernel,
        out_shape=(shape(4 * GROUP, HEAD, BF),) * 2,
        in_specs=[vmem()] * 8,
        out_specs=(vmem(),) * 2,
        compiler_params=params(),
        name="stack_keys_values",
        cost_estimate=cost(2.3),
    )(*keys, *values)


def forward_kernel(*refs):
    half = 2 * GROUP
    for kind in range(2):
        near, far, for_far, for_near = refs[kind * 4 : kind * 4 + 4]
        out_near, out_far = refs[8 + kind * 2 : 10 + kind * 2]
        out_near[:half, :] = near[:half, :]
        out_near[half:, :] = (near[half:, :].astype(F32) + for_near[...].astype(F32)).astype(BF)
        out_far[:half, :] = (far[:half, :].astype(F32) + for_far[...].astype(F32)).astype(BF)
        out_far[half:, :] = far[half:, :]


def forward_parts(*arrays):
    return pl.pallas_call(
        forward_kernel,
        out_shape=(shape(4 * GROUP, HEAD, BF),) * 4,
        in_specs=[vmem()] * 8,
        out_specs=(vmem(),) * 4,
        compiler_params=params(),
        name="forward_key_value_grads",
        cost_estimate=cost(2),
    )(*arrays)


def sum_kernel(k0, k1, k2, v0, v1, v2, *outs):
    for kind, parts in enumerate(((k0, k1, k2), (v0, v1, v2))):
        for m in range(4):
            rows = slice(m * GROUP, (m + 1) * GROUP)
            total = sum(part[rows, :].astype(F32) for part in parts)
            outs[kind * 4 + m][...] = total.astype(BF)


def sum_parts(*arrays):
    return pl.pallas_call(
        sum_kernel,
        out_shape=(shape(GROUP, HEAD, BF),) * 8,
        in_specs=[vmem()] * 6,
        out_specs=(vmem(),) * 8,
        compiler_params=params(),
        name="sum_key_value_grads",
        cost_estimate=cost(3),
    )(*arrays)


def feed_grads_kernel(info, m1, o1, m2, o2, active, grads, f0, f1, f2, f3, total):
    place = place_of(info)
    top, low = slice(0, RUN), slice(RUN, GROUP)
    total[:, :768] = (
        dot(m2[...], grads[top, :], TN) + dot(o2[...], grads[low, :], TN)
    ).astype(BF)
    total[:, 768:] = (
        dot(m1[...], active[top, :], TN) + dot(o1[...], active[low, :], TN)
    ).astype(BF)
    for mx, out in enumerate((f0, f1, f2, f3)):
        for mz in range(4):
            row = pl.multiple_of((place ^ (mx * 4 + mz)) * 64, 64)
            out[mz * 64 : (mz + 1) * 64, :] = total[pl.ds(row, 64), :]


def feed_grads(info, rows, rows_two, active, grads):
    return pl.pallas_call(
        feed_grads_kernel,
        out_shape=(shape(256, 1152, BF),) * 4,
        in_specs=[scalars()] + [vmem()] * 6,
        out_specs=(vmem(),) * 4,
        scratch_shapes=[pltpu.VMEM((1024, 1152), BF)],
        compiler_params=params(),
        name="feed_grads",
        cost_estimate=cost(5),
    )(info, *rows, *rows_two, active, grads)


def early_kernel(info, m1, o1, mg, og, grad_raw, attended, e0, e1, e2, e3, total):
    place = place_of(info)
    top, low = slice(0, RUN), slice(RUN, GROUP)
    total[:, :256] = (
        dot(m1[...], grad_raw[top, :], TN) + dot(o1[...], grad_raw[low, :], TN)
    ).astype(BF)
    total[:, 256:] = (
        dot(mg[...], attended[top, :], TN) + dot(og[...], attended[low, :], TN)
    ).astype(BF)
    for mx, out in enumerate((e0, e1, e2, e3)):
        for mz in range(4):
            row = pl.multiple_of((place ^ (mx * 4 + mz)) * 64, 64)
            out[mz * 64 : (mz + 1) * 64, :] = total[pl.ds(row, 64), :]


def early_grads(info, rows, grad_rows, grad_raw, attended):
    return pl.pallas_call(
        early_kernel,
        out_shape=(shape(256, 512, BF),) * 4,
        in_specs=[scalars()] + [vmem()] * 6,
        out_specs=(vmem(),) * 4,
        scratch_shapes=[pltpu.VMEM((1024, 512), BF)],
        compiler_params=params(),
        name="early_grads",
        cost_estimate=cost(4),
    )(info, *rows, *grad_rows, grad_raw, attended)


def last_kernel(
    info,
    m1,
    o1,
    weight,
    grad_raw,
    query_part,
    raw,
    cosine,
    sine,
    gains,
    k0,
    k1,
    k2,
    k3,
    v0,
    v1,
    v2,
    v3,
    mine_down,
    other_down,
    mine,
    other,
    l0,
    l1,
    l2,
    l3,
    grads,
    total,
):
    place = place_of(info)
    part = jnp.zeros((1, HEAD), F32)
    for half, (out, down) in enumerate(((mine, mine_down), (other, other_down))):
        here = slice(half * RUN, (half + 1) * RUN)
        out[:, 1024:] = down[...]
        key_grad = sum(k[here, :].astype(F32) for k in (k0, k1, k2, k3))
        value_grad = sum(v[here, :].astype(F32) for v in (v0, v1, v2, v3))
        grads[here, :HEAD], one = head_back(
            key_grad, raw[here, 2 * HEAD :], gains[1:2, :], cosine[here, :], sine[here, :]
        )
        grads[here, HEAD:] = value_grad.astype(BF)
        part = part + one
        out[:, :1024] = (
            dot(grad_raw[here, :], weight[:, : 2 * HEAD], NT)
            + dot(grads[here, :], weight[:, 2 * HEAD : 4 * HEAD], NT)
        ).astype(BF)
    total[...] = (
        dot(m1[...], grads[:RUN, :], TN) + dot(o1[...], grads[RUN:, :], TN)
    ).astype(BF)
    row = lax.broadcasted_iota(jnp.int32, (64, 1), 0)
    heads = jnp.where(row == 0, query_part[0:1, :], jnp.where(row == 1, part, 0.0)).astype(BF)
    for mx, out in enumerate((l0, l1, l2, l3)):
        for mz in range(4):
            row = pl.multiple_of((place ^ (mx * 4 + mz)) * 64, 64)
            here = slice(mz * 64, (mz + 1) * 64)
            out[here, : 2 * HEAD] = total[pl.ds(row, 64), :]
            out[here, 2 * HEAD :] = heads


def last_step(info, rows, weight, grad_raw, query_part, raw, cosine, sine, gains, *parts):
    return pl.pallas_call(
        last_kernel,
        out_shape=(shape(RUN, 2048, BF),) * 2 + (shape(256, 3 * HEAD, BF),) * 4,
        in_specs=[scalars()] + [vmem()] * 19,
        out_specs=(vmem(),) * 6,
        scratch_shapes=[pltpu.VMEM((GROUP, 2 * HEAD), BF), pltpu.VMEM((1024, 2 * HEAD), BF)],
        compiler_params=params(),
        name="last_step",
        cost_estimate=cost(6),
    )(info, *rows, weight, grad_raw, query_part, raw, cosine, sine, gains, *parts)


def local(
    tokens,
    positions,
    sequence_ids,
    attn_gain,
    query_weight,
    key_matrix,
    value_matrix,
    query_gain,
    key_gain,
    output_weight,
    mlp_gain,
    gate_weight,
    up_weight,
    down_weight,
    out_grad,
):
    xi, zl, co, zh, yi = (lax.axis_index(name) for name in AXES)
    place = xi * 4 + zl * 2 + zh
    start_one = jnp.sum(sequence_ids < 1, dtype=jnp.int32)
    start_two = jnp.sum(sequence_ids < 2, dtype=jnp.int32)
    info = jnp.stack([xi, zl, zh, co, yi, start_one, start_two]).astype(jnp.int32)

    gain_one = attn_gain.astype(F32)[:, None]
    gain_two = mlp_gain.astype(F32)[:, None]
    weights = prepare(
        attn_gain.reshape(1, 64),
        mlp_gain.reshape(1, 64),
        query_weight,
        key_matrix,
        value_matrix,
        output_weight.T,
        gate_weight,
        up_weight,
        down_weight.T,
    )
    both = exchange_runs(jnp.concatenate([tokens, out_grad], axis=1))
    one_own, two_own = gather_chunk(weights)
    one_own, two_own, both = lax.optimization_barrier((one_own, two_own, both))
    one_weights = [one_own] + [swap_with(one_own, "z", m) for m in (1, 2, 3)]

    resid, out_grad = both[:, :1024].astype(F32), both[:, 1024:]
    normal_one, inverse_one = rms_parts(resid)
    rows_mine = gather_along_y(normal_one.astype(BF))
    rows_mine, one_weights = lax.optimization_barrier((rows_mine, one_weights))
    rows_other = swap_with(rows_mine, "core", 1)
    out_grad, rows_other = lax.optimization_barrier((out_grad, rows_other))
    rows_one = (rows_mine, rows_other)
    cotangent = out_grad.astype(F32)
    grad_mine, grad_other = gather_rows(out_grad)

    run_places = positions.reshape(32, 4, 64)
    run_places = jnp.stack(
        [
            lax.dynamic_index_in_dim(run_places, run_of(xi * 2 + zl, co ^ half, zh), 0, False)
            for half in range(2)
        ]
    )
    run_places = jnp.where((yi & 1) == 1, run_places[:, jnp.array([1, 0, 3, 2])], run_places)
    run_places = jnp.where((yi & 2) == 2, run_places[:, jnp.array([2, 3, 0, 1])], run_places)
    half_size = HEAD // 2
    lane = jnp.arange(HEAD)
    frequency = jnp.exp(
        -jnp.log(ROPE_BASE) * 2.0 * (lane % half_size).astype(F32) / HEAD
    )
    angles = run_places.reshape(GROUP).astype(F32)[:, None] * frequency[None, :]
    cosine = jnp.cos(angles)
    sine = jnp.sin(angles) * jnp.where(lane < half_size, -1.0, 1.0)
    gains = jnp.stack([query_gain, key_gain]).astype(F32)
    query, key, value, raw, weight_full = project(
        info, *rows_one, one_weights, cosine, sine, gains
    )

    two_weights = [two_own, None, swap_with(two_own, "z", 2), None]
    two_own, two_weights[2], grad_mine, key, value = lax.optimization_barrier(
        (two_own, two_weights[2], grad_mine, key, value)
    )
    keys_x = [key] + [swap_with(key, "x", m) for m in (1, 2, 3)]
    values_z = [value] + [swap_with(value, "z", m) for m in (1, 2, 3)]
    key_own, value_own = stack(keys_x, values_z)
    key_parts = gather_steps(key_own, "z")
    value_parts = gather_steps(value_own, "x")
    two_own, key_parts, value_parts, grad_other = lax.optimization_barrier(
        (two_own, key_parts, value_parts, grad_other)
    )
    grad_rows = (grad_mine, grad_other)
    two_weights[1] = swap_with(two_own, "z", 1)
    two_weights[3] = swap_with(two_own, "z", 3)

    attended, sums, mine, other = attention_forward(
        info, query, weight_full, key_parts, value_parts
    )
    mine, other, two_weights[1] = lax.optimization_barrier((mine, other, two_weights[1]))
    hidden = resid + scatter_rows(mine, other)
    normal_two, inverse_two = rms_parts(hidden)
    rows_mine = gather_along_y(normal_two.astype(BF))
    rows_mine, two_weights[3] = lax.optimization_barrier((rows_mine, two_weights[3]))
    rows_two = (rows_mine, swap_with(rows_mine, "core", 1))

    active, grad_gate_up, mine, other, mine_down, other_down = feed(
        info, *rows_two, *grad_rows, two_weights
    )
    scaled_two = scatter_rows(mine, other)
    grad_hidden = cotangent + rms_back(scaled_two, normal_two, inverse_two)
    grad_block = grad_hidden.astype(BF)
    grad_blocks = [grad_block] + [swap_with(grad_block, "y", m) for m in (1, 2, 3)]
    two_parts = feed_grads(info, grad_rows, rows_two, active, grad_gate_up)
    grad_blocks, two_parts = lax.optimization_barrier((grad_blocks, two_parts))
    grad_rows_mine = jnp.concatenate(grad_blocks)
    grad_rows_one = (grad_rows_mine, swap_with(grad_rows_mine, "core", 1))
    two_parts = [two_parts[0]] + [swap_with(two_parts[m], "x", m) for m in (1, 2, 3)]

    grad_raw, query_part, *key_value_grads = attention_back(
        info,
        query,
        *grad_rows_one,
        weight_full,
        attended,
        sums,
        raw,
        cosine,
        sine,
        gains,
        key_parts,
        value_parts,
    )
    key_value_grads, two_parts = lax.optimization_barrier((key_value_grads, two_parts))
    key_grads, value_grads = key_value_grads[:5], key_value_grads[5:]
    forwarded = forward_parts(
        key_grads[1],
        key_grads[2],
        swap_with(key_grads[3], "z", NEIGHBOURS["z"][0]),
        swap_with(key_grads[4], "z", NEIGHBOURS["z"][1]),
        value_grads[1],
        value_grads[2],
        swap_with(value_grads[3], "x", NEIGHBOURS["x"][0]),
        swap_with(value_grads[4], "x", NEIGHBOURS["x"][1]),
    )
    early = early_grads(info, rows_one, grad_rows_one, grad_raw, attended)
    summed = sum_parts(
        key_grads[0],
        swap_with(forwarded[0], "z", NEIGHBOURS["z"][0]),
        swap_with(forwarded[1], "z", NEIGHBOURS["z"][1]),
        value_grads[0],
        swap_with(forwarded[2], "x", NEIGHBOURS["x"][0]),
        swap_with(forwarded[3], "x", NEIGHBOURS["x"][1]),
    )
    early, summed = lax.optimization_barrier((early, summed))
    key_grads = [summed[0]] + [swap_with(summed[m], "x", m) for m in (1, 2, 3)]
    value_grads = [summed[4]] + [swap_with(summed[4 + m], "z", m) for m in (1, 2, 3)]
    early = [early[0]] + [swap_with(early[m], "x", m) for m in (1, 2, 3)]

    mine, other, *late = last_step(
        info,
        rows_one,
        weight_full,
        grad_raw,
        query_part,
        raw,
        cosine,
        sine,
        gains,
        *key_grads,
        *value_grads,
        mine_down,
        other_down,
    )
    mine, other, late, early = lax.optimization_barrier((mine, other, late, early))
    late = [late[0]] + [swap_with(late[m], "x", m) for m in (1, 2, 3)]
    totals = [
        sum(part.astype(F32) for part in parts).astype(BF) for parts in (two_parts, early, late)
    ]
    received = swap_with(other, "core", 1)
    halves = [
        jnp.concatenate([v[m * 64 : (m + 1) * 64] for v in totals], axis=1) for m in range(4)
    ]
    parts = [
        mine[m * 64 : (m + 1) * 64].astype(F32) + received[m * 64 : (m + 1) * 64].astype(F32)
        for m in range(4)
    ]
    halves, parts = lax.optimization_barrier((halves, parts))
    own = sum(chunk_along_z(halves[m], m).astype(F32) for m in range(4))
    both = scatter_axis(parts, "y")
    output = hidden + both[:, 1024:]
    token_grad = grad_hidden + rms_back(both[:, :1024], normal_one, inverse_one)
    both = exchange_runs(jnp.concatenate([output.astype(BF), token_grad.astype(BF)], axis=1))
    output, token_grad = both[:, :1024], both[:, 1024:].astype(F32)

    gate_part, up_part, down_part = own[:, :384], own[:, 384:768], own[:, 768:1152]
    query_part, output_part = own[:, 1152:1408], own[:, 1408:1664]
    key_part, value_part = own[:, 1664:1792], own[:, 1792:1920]
    attn_part = (
        jnp.sum(query_part * query_weight.astype(F32), axis=1)
        + jnp.sum(key_part * key_matrix.astype(F32), axis=1)
        + jnp.sum(value_part * value_matrix.astype(F32), axis=1)
    )
    mlp_part = jnp.sum(
        gate_part * gate_weight.astype(F32) + up_part * up_weight.astype(F32), axis=1
    )
    sums_all = jnp.concatenate([attn_part, mlp_part, own[0, 1920:], own[1, 1920:]])
    received = [swap_with(sums_all, "y", m) for m in (1, 2, 3)]
    for part in received:
        sums_all = sums_all + part
    sums_all = sums_all + swap_with(sums_all, "z", 1)
    gain_parts, head_parts = sums_all[:128], sums_all[128:]
    return (
        output,
        token_grad,
        gain_parts[:64],
        query_part * gain_one,
        key_part * gain_one,
        value_part * gain_one,
        head_parts[:HEAD],
        head_parts[HEAD:],
        output_part.T,
        gain_parts[64:],
        gate_part * gain_two,
        up_part * gain_two,
        down_part.T,
    )


def solution(mesh):
    parts = Mesh(mesh.devices.reshape(4, 2, 2, 2, 4), AXES)
    ctx, tp = ("x", "zl", "core"), ("zh", "y")
    tokens, matrix, turned = P(AXES, None), P(ctx, tp), P(tp, ctx)
    return jax.shard_map(
        local,
        mesh=parts,
        in_specs=(
            tokens,
            P(),
            P(),
            P(ctx),
            matrix,
            matrix,
            matrix,
            P(),
            P(),
            turned,
            P(ctx),
            matrix,
            matrix,
            turned,
            tokens,
        ),
        out_specs=(
            tokens,
            tokens,
            P(ctx),
            matrix,
            matrix,
            matrix,
            P(),
            P(),
            turned,
            P(ctx),
            matrix,
            matrix,
            turned,
        ),
        check_vma=False,
    )
```

```python
import jax
import jax.numpy as jnp
from jax import lax
from jax.experimental import pallas as pl
from jax.experimental.pallas import tpu as pltpu
from jax.sharding import Mesh, PartitionSpec as P

AXES = ("x", "zl", "core", "zh", "y")
EPS = 1e-06
ROPE_BASE = 1000000.0
HEAD = 128
RUN = 256
GROUP = 512
KEYS = 512
N_BLOCKS = 16
LOG2E = 1.4426950408889634
LN2 = 0.6931471805599453
Q_SCALE = LOG2E * HEAD ** (-0.5)
BF = jnp.bfloat16
F32 = jnp.float32
VMEM_LIMIT = 60 * 1024 * 1024


NEIGHBOURS = {"x": (1, 3), "z": (2, 3)}


def swap_with(value, axis, mask):
    if axis == "z":
        return lax.ppermute(value, ("zl", "zh"), [(i, i ^ mask) for i in range(4)])
    size = 2 if axis == "core" else 4
    return lax.ppermute(value, axis, [(i, i ^ mask) for i in range(size)])


def chunk_along_x(value, mask):
    moves = [
        ((x * 2 + core) * 2 + zh, ((x ^ mask) * 2 + zh) * 2 + core)
        for x in range(4)
        for core in range(2)
        for zh in range(2)
    ]
    return lax.ppermute(value, ("x", "core", "zh"), moves)


def chunk_along_z(value, mask):
    moves = [
        ((zl * 2 + core) * 2 + zh, ((zl ^ (mask >> 1)) * 2 + (zh ^ (mask & 1))) * 2 + core)
        for zl in range(2)
        for core in range(2)
        for zh in range(2)
    ]
    return lax.ppermute(value, ("zl", "core", "zh"), moves)


def exchange_runs(value):
    mirror = [(i, i ^ 14 if i % 2 else i) for i in range(16)]
    return lax.ppermute(value, ("x", "zl", "core"), mirror)


def gather_chunk(value):
    parts = [chunk_along_x(value, m) for m in range(4)]
    return [jnp.concatenate([p[:, c] for p in parts]) for c in (slice(0, 768), slice(768, 1920))]


def scatter_axis(parts, axis):
    total = parts[0].astype(F32)
    for m in (1, 2, 3):
        total = total + swap_with(parts[m].astype(BF), axis, m).astype(F32)
    return total


def gather_steps(value, axis):
    near, far = NEIGHBOURS[axis]
    half = value.shape[0] // 2
    one, two = swap_with(value, axis, near), swap_with(value, axis, far)
    return [value, one, two, swap_with(two[:half], axis, near), swap_with(one[half:], axis, far)]


def gather_along_y(block):
    return jnp.concatenate([block] + [swap_with(block, "y", m) for m in (1, 2, 3)], axis=0)


def gather_rows(block):
    half = gather_along_y(block)
    return half, swap_with(half, "core", 1)


def scatter_rows(mine, other):
    received = swap_with(other, "core", 1)
    parts = [
        mine[m * 64 : (m + 1) * 64].astype(F32) + received[m * 64 : (m + 1) * 64].astype(F32)
        for m in range(4)
    ]
    return scatter_axis(parts, "y")


def rms_parts(value):
    inverse = lax.rsqrt(jnp.mean(value * value, axis=-1, keepdims=True) + EPS)
    return value * inverse, inverse


def rms_back(scaled, normal, inverse):
    return inverse * (scaled - normal * jnp.mean(scaled * normal, axis=-1, keepdims=True))


def dot(left, right, contract):
    return lax.dot_general(left, right, (contract, ((), ())), preferred_element_type=F32)


NN = ((1,), (0,))
NT = ((1,), (1,))
TN = ((0,), (0,))


def stream_index(spot, yi):
    return (((spot >> 6) ^ yi) << 6) | (spot & 63)


def vmem():
    return pl.BlockSpec(memory_space=pltpu.VMEM)


def anywhere():
    return pl.BlockSpec(memory_space=pl.ANY)


def scalars():
    return pl.BlockSpec(memory_space=pltpu.SMEM)


def params():
    return pltpu.CompilerParams(vmem_limit_bytes=VMEM_LIMIT)


def cost(microseconds):
    return pl.CostEstimate(
        flops=int(microseconds * 1.15e9), transcendentals=0, bytes_accessed=1 << 20
    )


def shape(rows, columns, kind):
    return jax.ShapeDtypeStruct((rows, columns), kind)


def place_of(info):
    return info[0] * 4 + info[1] * 2 + info[2]


def rotate_lanes(value, cosine, sine):
    return value * cosine + pltpu.roll(value, HEAD // 2, 1) * sine


def normed(value):
    inverse = lax.rsqrt(jnp.mean(value * value, axis=-1, keepdims=True) + EPS)
    return value * inverse, inverse


def column_of(row):
    diagonal = lax.broadcasted_iota(jnp.int32, (64, 64), 0) == lax.broadcasted_iota(
        jnp.int32, (64, 64), 1
    )
    return jnp.sum(jnp.where(diagonal, row, 0.0), axis=1, keepdims=True)


def prepare_kernel(gain_one, gain_two, query, key, value, output, gate, up, down, out):
    first = column_of(gain_one[...].astype(F32))
    second = column_of(gain_two[...].astype(F32))
    out[:, :256] = (query[...].astype(F32) * first).astype(BF)
    out[:, 256:384] = (key[...].astype(F32) * first).astype(BF)
    out[:, 384:512] = (value[...].astype(F32) * first).astype(BF)
    out[:, 512:768] = output[...]
    out[:, 768:1152] = (gate[...].astype(F32) * second).astype(BF)
    out[:, 1152:1536] = (up[...].astype(F32) * second).astype(BF)
    out[:, 1536:] = down[...]


def prepare(*arrays):
    return pl.pallas_call(
        prepare_kernel,
        out_shape=shape(64, 1920, BF),
        in_specs=[vmem()] * 9,
        out_specs=vmem(),
        compiler_params=params(),
        name="prepare_weights",
        cost_estimate=cost(2),
    )(*arrays)


def weight_copies(info, parts, weight, sems):
    place = place_of(info)
    copies = []
    for mz, part in enumerate(parts):
        for mx in range(4):
            row = pl.multiple_of((place ^ (mx * 4 + mz)) * 64, 64)
            copies.append(
                pltpu.make_async_copy(
                    part.at[pl.ds(mx * 64, 64)], weight.at[pl.ds(row, 64)], sems.at[mz * 4 + mx]
                )
            )
    return copies


def project_kernel(
    info, mine, other, w0, w1, w2, w3, cosine, sine, gains, query, key, value, raw, weight, sems
):
    copies = weight_copies(info, (w0, w1, w2, w3), weight, sems)
    for copy in copies:
        copy.start()
    for copy in copies:
        copy.wait()
    for half, rows in enumerate((mine, other)):
        here = slice(half * RUN, (half + 1) * RUN)
        product = dot(rows[...], weight[:, : 4 * HEAD], NN)
        raw[here, :] = product[:, : 3 * HEAD]
        value[here, :] = product[:, 3 * HEAD :].astype(BF)
        for head in range(3):
            normal, _ = normed(product[:, head * HEAD : (head + 1) * HEAD])
            gain = gains[0:1, :] if head < 2 else gains[1:2, :]
            turned = rotate_lanes(normal * gain, cosine[here, :], sine[here, :])
            if head < 2:
                query[here, head * HEAD : (head + 1) * HEAD] = (turned * Q_SCALE).astype(BF)
            else:
                key[here, :] = turned.astype(BF)


def project(info, mine, other, parts, cosine, sine, gains):
    return pl.pallas_call(
        project_kernel,
        out_shape=(
            shape(GROUP, 2 * HEAD, BF),
            shape(GROUP, HEAD, BF),
            shape(GROUP, HEAD, BF),
            shape(GROUP, 3 * HEAD, F32),
            shape(1024, 6 * HEAD, BF),
        ),
        in_specs=[scalars(), vmem(), vmem()] + [anywhere()] * 4 + [vmem()] * 3,
        out_specs=(vmem(),) * 5,
        scratch_shapes=[pltpu.SemaphoreType.DMA((16,))],
        compiler_params=params(),
        name="project",
        cost_estimate=cost(5.5),
    )(info, mine, other, *parts, cosine, sine, gains)


def run_of(group, core, zh):
    return ((group ^ (7 * core)) * 2 + core) * 2 + zh


def key_copies(info, key_parts, value_parts, key_all, value_all, sems):
    xi, zl, zh, co = info[0], info[1], info[2], info[3]
    copies = []
    for kind, (parts, target, axis) in enumerate(
        ((key_parts, key_all, "z"), (value_parts, value_all, "x"))
    ):
        near, far = NEIGHBOURS[axis]
        pieces = [(0, parts[0], 0), (near, parts[1], 0), (far, parts[2], 0)]
        pieces += [(near ^ far, parts[3], 0), (near ^ far, parts[4], 2)]
        for turn, source, first in pieces:
            for sub in range(first, min(first + source.shape[0] // GROUP, 4)):
                mx, mz = (sub, turn) if kind == 0 else (turn, sub)
                group = (xi ^ mx) * 2 + (zl ^ (mz >> 1))
                for half in range(2):
                    row = run_of(group, co ^ half, zh ^ (mz & 1)) * RUN
                    copies.append(
                        pltpu.make_async_copy(
                            source.at[pl.ds((sub - first) * GROUP + half * RUN, RUN)],
                            target.at[pl.ds(pl.multiple_of(row, RUN), RUN)],
                            sems.at[len(copies)],
                        )
                    )
    return copies


def first_of(token, start_one, start_two):
    return jnp.where(
        token >= start_two, start_two, jnp.where(token >= start_one, start_one, 0)
    )


def spans(group, core):
    mine = (group ^ (7 * core)) * 2 + core
    theirs = (group ^ (7 * (1 - core))) * 2 + 1 - core
    big = jnp.where(theirs > mine, 1, 0)
    return jnp.minimum(mine, theirs), jnp.maximum(mine, theirs), big


def attention_kernel(
    info,
    query,
    out_weight,
    k0,
    k1,
    k2,
    k3,
    k4,
    v0,
    v1,
    v2,
    v3,
    v4,
    out,
    sums,
    mine,
    other,
    key_all,
    value_all,
    totals,
    sems,
):
    copies = key_copies(info, (k0, k1, k2, k3, k4), (v0, v1, v2, v3, v4), key_all, value_all, sems)
    for copy in copies:
        copy.start()
    for copy in copies:
        copy.wait()
    xi, zl, zh, co, yi = (info[i] for i in range(5))
    start_one, start_two = info[5], info[6]
    group = xi * 2 + zl
    low, high, big = spans(group, co)
    ones = jnp.ones((KEYS, HEAD), BF)
    row_spot = stream_index(lax.broadcasted_iota(jnp.int32, (RUN, 1), 0), yi)
    totals[...] = jnp.zeros_like(totals)

    def tokens_of(half):
        token = run_of(group, co ^ half, zh) * RUN + row_spot
        return token, first_of(token, start_one, start_two)

    def block(index, masked, halves):
        rows = pl.ds(pl.multiple_of(index * KEYS, KEYS), KEYS)
        keys = key_all[rows, :]
        values = jnp.concatenate([value_all[rows, :], ones], axis=1)
        spot = lax.broadcasted_iota(jnp.int32, (1, KEYS), 1)
        key_tokens = index * KEYS + (spot & ~(RUN - 1)) + stream_index(spot & (RUN - 1), yi)
        for half in halves:
            rows_here = pl.ds(pl.multiple_of(half * RUN, RUN), RUN)
            if masked:
                token, start = tokens_of(half)
                allowed = (key_tokens <= token) & (key_tokens >= start)
            for head in range(2):
                scores = dot(query[rows_here, head * HEAD : (head + 1) * HEAD], keys, NT)
                weights = jnp.exp2(scores)
                if masked:
                    weights = jnp.where(allowed, weights, 0.0)
                totals[half * 2 + head] += dot(weights.astype(BF), values, NN)

    def full_both(index, carry):
        block(index, False, (0, 1))
        return carry

    def full_big(step, carry):
        block(low + 1 + 2 * step, False, (big,))
        block(low + 2 + 2 * step, False, (big,))
        return carry

    lax.fori_loop(1, low, full_both, 0)
    lax.fori_loop(0, (high - 1 - low) // 2, full_big, 0)
    for half in range(2):
        keep = tokens_of(half)[1] <= KEYS
        for head in range(2):
            totals[half * 2 + head] = jnp.where(keep, totals[half * 2 + head], 0.0)
    block(jnp.int32(0), True, (0, 1))

    @pl.when(low > 0)
    def _():
        block(low, True, (0, 1))

    block(high, True, (big,))
    for half in range(2):
        for head in range(2):
            total = totals[half * 2 + head]
            weight_sum = total[:, HEAD:]
            out[half * RUN : (half + 1) * RUN, head * HEAD : (head + 1) * HEAD] = (
                total[:, :HEAD] / weight_sum
            ).astype(BF)
            sums[half * 2 + head] = jnp.log2(weight_sum).T[:8]
    mine[...] = dot(out[:RUN, :], out_weight[:, 4 * HEAD :], NT).astype(BF)
    other[...] = dot(out[RUN:, :], out_weight[:, 4 * HEAD :], NT).astype(BF)


def attention_forward(info, query, out_weight, key_parts, value_parts):
    return pl.pallas_call(
        attention_kernel,
        out_shape=(
            shape(GROUP, 2 * HEAD, BF),
            jax.ShapeDtypeStruct((4, 8, RUN), F32),
            shape(RUN, 1024, BF),
            shape(RUN, 1024, BF),
        ),
        in_specs=[scalars(), vmem(), vmem()] + [anywhere()] * 10,
        out_specs=(vmem(),) * 4,
        scratch_shapes=[
            pltpu.VMEM((N_BLOCKS * KEYS, HEAD), BF),
            pltpu.VMEM((N_BLOCKS * KEYS, HEAD), BF),
            pltpu.VMEM((4, RUN, 2 * HEAD), F32),
            pltpu.SemaphoreType.DMA((64,)),
        ],
        compiler_params=params(),
        name="attention_forward",
        cost_estimate=cost(13),
    )(info, query, out_weight, *key_parts, *value_parts)


def feed_kernel(
    info,
    mine,
    other,
    mine_grad,
    other_grad,
    w0,
    w1,
    w2,
    w3,
    active,
    grads,
    mine_out,
    other_out,
    mine_down,
    other_down,
    weight,
    sems,
):
    copies = weight_copies(info, (w0, w1, w2, w3), weight, sems)
    for copy in copies:
        copy.start()
    for copy in copies:
        copy.wait()
    for half, (rows, rows_grad, out) in enumerate(
        ((mine, mine_grad, mine_out), (other, other_grad, other_out))
    ):
        here = slice(half * RUN, (half + 1) * RUN)
        gate_up = dot(rows[...], weight[:, :768], NN)
        gate, up = gate_up[:, :384], gate_up[:, 384:]
        sigmoid = 1.0 / (1.0 + jnp.exp(-gate))
        swish = gate * sigmoid
        active[here, :] = (swish * up).astype(BF)
        grad_active = dot(rows_grad[...], weight[:, 768:], NN)
        slope = sigmoid * (1.0 + gate * (1.0 - sigmoid))
        grads[here, :384] = (grad_active * up * slope).astype(BF)
        grads[here, 384:] = (grad_active * swish).astype(BF)
        out[...] = dot(grads[here, :], weight[:, :768], NT).astype(BF)
    mine_down[...] = dot(active[:RUN, :], weight[:, 768:], NT).astype(BF)
    other_down[...] = dot(active[RUN:, :], weight[:, 768:], NT).astype(BF)


def feed(info, mine, other, mine_grad, other_grad, parts):
    return pl.pallas_call(
        feed_kernel,
        out_shape=(shape(GROUP, 384, BF), shape(GROUP, 768, BF)) + (shape(RUN, 1024, BF),) * 4,
        in_specs=[scalars()] + [vmem()] * 4 + [anywhere()] * 4,
        out_specs=(vmem(),) * 6,
        scratch_shapes=[pltpu.VMEM((1024, 1152), BF), pltpu.SemaphoreType.DMA((16,))],
        compiler_params=params(),
        name="feed",
        cost_estimate=cost(7.5),
    )(info, mine, other, mine_grad, other_grad, *parts)


def head_back(gradient, raw, gain, cosine, sine):
    normal, inverse = normed(raw)
    turned = rotate_lanes(gradient, cosine, -sine)
    part = jnp.sum(turned * normal, axis=0, keepdims=True)
    scaled = turned * gain
    mean = jnp.mean(scaled * normal, axis=-1, keepdims=True)
    return (inverse * (scaled - normal * mean)).astype(BF), part


def attention_back_kernel(
    info,
    query,
    mine,
    other,
    out_weight,
    attended,
    sums,
    raw,
    cosine,
    sine,
    gains,
    k0,
    k1,
    k2,
    k3,
    k4,
    v0,
    v1,
    v2,
    v3,
    v4,
    grad_raw,
    gain_part,
    gk0,
    gk1,
    gk2,
    gk3,
    gk4,
    gv0,
    gv1,
    gv2,
    gv3,
    gv4,
    key_all,
    value_all,
    totals,
    grad,
    deltas,
    grad_key,
    grad_value,
    sems,
):
    copies = key_copies(info, (k0, k1, k2, k3, k4), (v0, v1, v2, v3, v4), key_all, value_all, sems)
    for copy in copies:
        copy.start()
    for half, rows_in in enumerate((mine, other)):
        here = slice(half * RUN, (half + 1) * RUN)
        rows_grad = dot(rows_in[...], out_weight[:, 4 * HEAD :], NN).astype(BF)
        grad[here, :] = rows_grad
        products = rows_grad.astype(F32) * attended[here, :].astype(F32)
        for head in range(2):
            turned = products[:, head * HEAD : (head + 1) * HEAD].T
            deltas[half * 2 + head] = jnp.broadcast_to(
                jnp.sum(turned, axis=0, keepdims=True), (8, RUN)
            )
    for copy in copies:
        copy.wait()
    xi, zl, zh, co, yi = (info[i] for i in range(5))
    start_one, start_two = info[5], info[6]
    group = xi * 2 + zl
    low, high, big = spans(group, co)
    column_spot = stream_index(lax.broadcasted_iota(jnp.int32, (1, RUN), 1), yi)

    def tokens_of(half):
        token = run_of(group, co ^ half, zh) * RUN + column_spot
        return token, first_of(token, start_one, start_two)

    totals[...] = jnp.zeros_like(totals)

    def places(index):
        owner_core = index % 2
        owner = (index // 2) ^ (7 * owner_core)
        mx = (owner // 2) ^ xi
        half = owner_core ^ co
        spots = []
        for run in range(2):
            mz = ((owner % 2) ^ zl) * 2 + (run ^ zh)
            spots.append((mx, mz, half))
        return spots

    def store(index, key_grad, value_grad):
        for run, (mx, mz, half) in enumerate(places(index)):
            rows = slice(run * RUN, (run + 1) * RUN)
            key_row = (mz * 4 + mx) * GROUP + half * RUN
            value_row = (mx * 4 + mz) * GROUP + half * RUN
            grad_key[pl.ds(pl.multiple_of(key_row, RUN), RUN), :] = key_grad[rows]
            grad_value[pl.ds(pl.multiple_of(value_row, RUN), RUN), :] = value_grad[rows]

    def block(index, masked, halves):
        rows = pl.ds(pl.multiple_of(index * KEYS, KEYS), KEYS)
        keys = key_all[rows, :]
        values = value_all[rows, :]
        spot = lax.broadcasted_iota(jnp.int32, (KEYS, 1), 0)
        key_tokens = index * KEYS + (spot & ~(RUN - 1)) + stream_index(spot & (RUN - 1), yi)
        key_grad = jnp.zeros((KEYS, HEAD), F32)
        value_grad = jnp.zeros((KEYS, HEAD), F32)
        for half in halves:
            rows_here = pl.ds(pl.multiple_of(half * RUN, RUN), RUN)
            token, start = tokens_of(half)
            if masked:
                allowed = (key_tokens <= token) & (key_tokens >= start)
            for head in range(2):
                lanes = slice(head * HEAD, (head + 1) * HEAD)
                queries = query[rows_here, lanes]
                grads = grad[rows_here, lanes]
                level = sums[half * 2 + head][0:1, :]
                if not masked:
                    level = jnp.where(start <= KEYS, level, 1e30)
                probs = jnp.exp2(dot(keys, queries, NT) - level)
                if masked:
                    probs = jnp.where(allowed, probs, 0.0)
                grad_probs = dot(values, grads, NT)
                grad_scores = (probs * (grad_probs - deltas[half * 2 + head][0:1, :])).astype(BF)
                value_grad = value_grad + dot(probs.astype(BF), grads, NN)
                key_grad = key_grad + dot(grad_scores, queries, NN)
                totals[half * 2 + head] += dot(grad_scores, keys, TN)
        store(index, (key_grad * LN2).astype(BF), value_grad.astype(BF))

    def full_both(index, carry):
        block(index, False, (0, 1))
        return carry

    def full_big(step, carry):
        block(low + 1 + 2 * step, False, (big,))
        block(low + 2 + 2 * step, False, (big,))
        return carry

    lax.fori_loop(1, low, full_both, 0)
    lax.fori_loop(0, (high - 1 - low) // 2, full_big, 0)
    block(jnp.int32(0), True, (0, 1))

    @pl.when(low > 0)
    def _():
        block(low, True, (0, 1))

    block(high, True, (big,))

    def empty(index, carry):
        nothing = jnp.zeros((KEYS, HEAD), BF)
        store(index, nothing, nothing)
        return carry

    lax.fori_loop(high + 1, N_BLOCKS, empty, 0)
    outs = []
    for source, targets, axis in (
        (grad_key, (gk0, gk1, gk2, gk3, gk4), "z"),
        (grad_value, (gv0, gv1, gv2, gv3, gv4), "x"),
    ):
        near, far = NEIGHBOURS[axis]
        block = 4 * GROUP
        starts = (0, near * block, far * block, (near ^ far) * block, (near ^ far) * block + block // 2)
        for start, target in zip(starts, targets):
            outs.append(
                pltpu.make_async_copy(
                    source.at[pl.ds(start, target.shape[0])], target, sems.at[len(outs)]
                )
            )
    for copy in outs:
        copy.start()
    part = jnp.zeros((1, HEAD), F32)
    for half in range(2):
        here = slice(half * RUN, (half + 1) * RUN)
        for head in range(2):
            lanes = slice(head * HEAD, (head + 1) * HEAD)
            grad_raw[here, lanes], one = head_back(
                totals[half * 2 + head] * HEAD ** (-0.5),
                raw[here, lanes],
                gains[0:1, :],
                cosine[here, :],
                sine[here, :],
            )
            part = part + one
    gain_part[...] = jnp.broadcast_to(part, (8, HEAD))
    for copy in outs:
        copy.wait()


def attention_back(
    info, query, mine, other, out_weight, attended, sums, raw, cosine, sine, gains, keys, values
):
    return pl.pallas_call(
        attention_back_kernel,
        out_shape=(shape(GROUP, 2 * HEAD, BF), shape(8, HEAD, F32))
        + ((shape(4 * GROUP, HEAD, BF),) * 3 + (shape(2 * GROUP, HEAD, BF),) * 2) * 2,
        in_specs=[scalars()] + [vmem()] * 10 + [anywhere()] * 10,
        out_specs=(vmem(), vmem()) + (anywhere(),) * 10,
        scratch_shapes=[
            pltpu.VMEM((N_BLOCKS * KEYS, HEAD), BF),
            pltpu.VMEM((N_BLOCKS * KEYS, HEAD), BF),
            pltpu.VMEM((4, RUN, HEAD), F32),
            pltpu.VMEM((GROUP, 2 * HEAD), BF),
            pltpu.VMEM((4, 8, RUN), F32),
            pltpu.VMEM((N_BLOCKS * KEYS, HEAD), BF),
            pltpu.VMEM((N_BLOCKS * KEYS, HEAD), BF),
            pltpu.SemaphoreType.DMA((64,)),
        ],
        compiler_params=params(),
        name="attention_back",
        cost_estimate=cost(24),
    )(
        info,
        query,
        mine,
        other,
        out_weight,
        attended,
        sums,
        raw,
        cosine,
        sine,
        gains,
        *keys,
        *values,
    )


def stack_kernel(k0, k1, k2, k3, v0, v1, v2, v3, keys, values):
    for m, (key, value) in enumerate(((k0, v0), (k1, v1), (k2, v2), (k3, v3))):
        rows = slice(m * GROUP, (m + 1) * GROUP)
        keys[rows, :] = key[...]
        values[rows, :] = value[...]


def stack(keys, values):
    return pl.pallas_call(
        stack_kernel,
        out_shape=(shape(4 * GROUP, HEAD, BF),) * 2,
        in_specs=[vmem()] * 8,
        out_specs=(vmem(),) * 2,
        compiler_params=params(),
        name="stack_keys_values",
        cost_estimate=cost(2.3),
    )(*keys, *values)


def forward_kernel(*refs):
    half = 2 * GROUP
    for kind in range(2):
        near, far, for_far, for_near = refs[kind * 4 : kind * 4 + 4]
        out_near, out_far = refs[8 + kind * 2 : 10 + kind * 2]
        out_near[:half, :] = near[:half, :]
        out_near[half:, :] = (near[half:, :].astype(F32) + for_near[...].astype(F32)).astype(BF)
        out_far[:half, :] = (far[:half, :].astype(F32) + for_far[...].astype(F32)).astype(BF)
        out_far[half:, :] = far[half:, :]


def forward_parts(*arrays):
    return pl.pallas_call(
        forward_kernel,
        out_shape=(shape(4 * GROUP, HEAD, BF),) * 4,
        in_specs=[vmem()] * 8,
        out_specs=(vmem(),) * 4,
        compiler_params=params(),
        name="forward_key_value_grads",
        cost_estimate=cost(2),
    )(*arrays)


def sum_kernel(k0, k1, k2, v0, v1, v2, *outs):
    for kind, parts in enumerate(((k0, k1, k2), (v0, v1, v2))):
        for m in range(4):
            rows = slice(m * GROUP, (m + 1) * GROUP)
            total = sum(part[rows, :].astype(F32) for part in parts)
            outs[kind * 4 + m][...] = total.astype(BF)


def sum_parts(*arrays):
    return pl.pallas_call(
        sum_kernel,
        out_shape=(shape(GROUP, HEAD, BF),) * 8,
        in_specs=[vmem()] * 6,
        out_specs=(vmem(),) * 8,
        compiler_params=params(),
        name="sum_key_value_grads",
        cost_estimate=cost(3),
    )(*arrays)


def feed_grads_kernel(info, m1, o1, m2, o2, active, grads, f0, f1, f2, f3, total):
    place = place_of(info)
    top, low = slice(0, RUN), slice(RUN, GROUP)
    total[:, :768] = (
        dot(m2[...], grads[top, :], TN) + dot(o2[...], grads[low, :], TN)
    ).astype(BF)
    total[:, 768:] = (
        dot(m1[...], active[top, :], TN) + dot(o1[...], active[low, :], TN)
    ).astype(BF)
    for mx, out in enumerate((f0, f1, f2, f3)):
        for mz in range(4):
            row = pl.multiple_of((place ^ (mx * 4 + mz)) * 64, 64)
            out[mz * 64 : (mz + 1) * 64, :] = total[pl.ds(row, 64), :]


def feed_grads(info, rows, rows_two, active, grads):
    return pl.pallas_call(
        feed_grads_kernel,
        out_shape=(shape(256, 1152, BF),) * 4,
        in_specs=[scalars()] + [vmem()] * 6,
        out_specs=(vmem(),) * 4,
        scratch_shapes=[pltpu.VMEM((1024, 1152), BF)],
        compiler_params=params(),
        name="feed_grads",
        cost_estimate=cost(5),
    )(info, *rows, *rows_two, active, grads)


def early_kernel(info, m1, o1, mg, og, grad_raw, attended, e0, e1, e2, e3, total):
    place = place_of(info)
    top, low = slice(0, RUN), slice(RUN, GROUP)
    total[:, :256] = (
        dot(m1[...], grad_raw[top, :], TN) + dot(o1[...], grad_raw[low, :], TN)
    ).astype(BF)
    total[:, 256:] = (
        dot(mg[...], attended[top, :], TN) + dot(og[...], attended[low, :], TN)
    ).astype(BF)
    for mx, out in enumerate((e0, e1, e2, e3)):
        for mz in range(4):
            row = pl.multiple_of((place ^ (mx * 4 + mz)) * 64, 64)
            out[mz * 64 : (mz + 1) * 64, :] = total[pl.ds(row, 64), :]


def early_grads(info, rows, grad_rows, grad_raw, attended):
    return pl.pallas_call(
        early_kernel,
        out_shape=(shape(256, 512, BF),) * 4,
        in_specs=[scalars()] + [vmem()] * 6,
        out_specs=(vmem(),) * 4,
        scratch_shapes=[pltpu.VMEM((1024, 512), BF)],
        compiler_params=params(),
        name="early_grads",
        cost_estimate=cost(4),
    )(info, *rows, *grad_rows, grad_raw, attended)


def last_kernel(
    info,
    m1,
    o1,
    weight,
    grad_raw,
    query_part,
    raw,
    cosine,
    sine,
    gains,
    k0,
    k1,
    k2,
    k3,
    v0,
    v1,
    v2,
    v3,
    mine_down,
    other_down,
    mine,
    other,
    l0,
    l1,
    l2,
    l3,
    grads,
    total,
):
    place = place_of(info)
    part = jnp.zeros((1, HEAD), F32)
    for half, (out, down) in enumerate(((mine, mine_down), (other, other_down))):
        here = slice(half * RUN, (half + 1) * RUN)
        out[:, 1024:] = down[...]
        key_grad = sum(k[here, :].astype(F32) for k in (k0, k1, k2, k3))
        value_grad = sum(v[here, :].astype(F32) for v in (v0, v1, v2, v3))
        grads[here, :HEAD], one = head_back(
            key_grad, raw[here, 2 * HEAD :], gains[1:2, :], cosine[here, :], sine[here, :]
        )
        grads[here, HEAD:] = value_grad.astype(BF)
        part = part + one
        out[:, :1024] = (
            dot(grad_raw[here, :], weight[:, : 2 * HEAD], NT)
            + dot(grads[here, :], weight[:, 2 * HEAD : 4 * HEAD], NT)
        ).astype(BF)
    total[...] = (
        dot(m1[...], grads[:RUN, :], TN) + dot(o1[...], grads[RUN:, :], TN)
    ).astype(BF)
    row = lax.broadcasted_iota(jnp.int32, (64, 1), 0)
    heads = jnp.where(row == 0, query_part[0:1, :], jnp.where(row == 1, part, 0.0)).astype(BF)
    for mx, out in enumerate((l0, l1, l2, l3)):
        for mz in range(4):
            row = pl.multiple_of((place ^ (mx * 4 + mz)) * 64, 64)
            here = slice(mz * 64, (mz + 1) * 64)
            out[here, : 2 * HEAD] = total[pl.ds(row, 64), :]
            out[here, 2 * HEAD :] = heads


def last_step(info, rows, weight, grad_raw, query_part, raw, cosine, sine, gains, *parts):
    return pl.pallas_call(
        last_kernel,
        out_shape=(shape(RUN, 2048, BF),) * 2 + (shape(256, 3 * HEAD, BF),) * 4,
        in_specs=[scalars()] + [vmem()] * 19,
        out_specs=(vmem(),) * 6,
        scratch_shapes=[pltpu.VMEM((GROUP, 2 * HEAD), BF), pltpu.VMEM((1024, 2 * HEAD), BF)],
        compiler_params=params(),
        name="last_step",
        cost_estimate=cost(6),
    )(info, *rows, weight, grad_raw, query_part, raw, cosine, sine, gains, *parts)


def local(
    tokens,
    positions,
    sequence_ids,
    attn_gain,
    query_weight,
    key_matrix,
    value_matrix,
    query_gain,
    key_gain,
    output_weight,
    mlp_gain,
    gate_weight,
    up_weight,
    down_weight,
    out_grad,
):
    xi, zl, co, zh, yi = (lax.axis_index(name) for name in AXES)
    place = xi * 4 + zl * 2 + zh
    start_one = jnp.sum(sequence_ids < 1, dtype=jnp.int32)
    start_two = jnp.sum(sequence_ids < 2, dtype=jnp.int32)
    info = jnp.stack([xi, zl, zh, co, yi, start_one, start_two]).astype(jnp.int32)

    gain_one = attn_gain.astype(F32)[:, None]
    gain_two = mlp_gain.astype(F32)[:, None]
    weights = prepare(
        attn_gain.reshape(1, 64),
        mlp_gain.reshape(1, 64),
        query_weight,
        key_matrix,
        value_matrix,
        output_weight.T,
        gate_weight,
        up_weight,
        down_weight.T,
    )
    both = exchange_runs(jnp.concatenate([tokens, out_grad], axis=1))
    one_own, two_own = gather_chunk(weights)
    run_places = positions.reshape(32, 4, 64)
    run_places = jnp.stack(
        [
            lax.dynamic_index_in_dim(run_places, run_of(xi * 2 + zl, co ^ half, zh), 0, False)
            for half in range(2)
        ]
    )
    run_places = jnp.where((yi & 1) == 1, run_places[:, jnp.array([1, 0, 3, 2])], run_places)
    run_places = jnp.where((yi & 2) == 2, run_places[:, jnp.array([2, 3, 0, 1])], run_places)
    half_size = HEAD // 2
    lane = jnp.arange(HEAD)
    frequency = jnp.exp(
        -jnp.log(ROPE_BASE) * 2.0 * (lane % half_size).astype(F32) / HEAD
    )
    angles = run_places.reshape(GROUP).astype(F32)[:, None] * frequency[None, :]
    cosine = jnp.cos(angles)
    sine = jnp.sin(angles) * jnp.where(lane < half_size, -1.0, 1.0)
    gains = jnp.stack([query_gain, key_gain]).astype(F32)
    one_own, two_own, both, info, cosine, sine, gains = lax.optimization_barrier(
        (one_own, two_own, both, info, cosine, sine, gains)
    )
    one_weights = [one_own] + [swap_with(one_own, "z", m) for m in (1, 2, 3)]

    resid, out_grad = both[:, :1024].astype(F32), both[:, 1024:]
    normal_one, inverse_one = rms_parts(resid)
    rows_mine = gather_along_y(normal_one.astype(BF))
    rows_mine, one_weights = lax.optimization_barrier((rows_mine, one_weights))
    rows_other = swap_with(rows_mine, "core", 1)
    out_grad, rows_other = lax.optimization_barrier((out_grad, rows_other))
    rows_one = (rows_mine, rows_other)
    cotangent = out_grad.astype(F32)
    grad_mine, grad_other = gather_rows(out_grad)

    query, key, value, raw, weight_full = project(
        info, *rows_one, one_weights, cosine, sine, gains
    )

    two_weights = [two_own, None, swap_with(two_own, "z", 2), None]
    two_own, two_weights[2], grad_mine, key, value = lax.optimization_barrier(
        (two_own, two_weights[2], grad_mine, key, value)
    )
    keys_x = [key] + [swap_with(key, "x", m) for m in (1, 2, 3)]
    values_z = [value] + [swap_with(value, "z", m) for m in (1, 2, 3)]
    key_own, value_own = stack(keys_x, values_z)
    key_parts = gather_steps(key_own, "z")
    value_parts = gather_steps(value_own, "x")
    two_own, key_parts, value_parts, grad_other = lax.optimization_barrier(
        (two_own, key_parts, value_parts, grad_other)
    )
    grad_rows = (grad_mine, grad_other)
    two_weights[1] = swap_with(two_own, "z", 1)
    two_weights[3] = swap_with(two_own, "z", 3)

    attended, sums, mine, other = attention_forward(
        info, query, weight_full, key_parts, value_parts
    )
    mine, other, two_weights[1] = lax.optimization_barrier((mine, other, two_weights[1]))
    hidden = resid + scatter_rows(mine, other)
    normal_two, inverse_two = rms_parts(hidden)
    rows_mine = gather_along_y(normal_two.astype(BF))
    rows_mine, two_weights[3] = lax.optimization_barrier((rows_mine, two_weights[3]))
    rows_two = (rows_mine, swap_with(rows_mine, "core", 1))

    active, grad_gate_up, mine, other, mine_down, other_down = feed(
        info, *rows_two, *grad_rows, two_weights
    )
    scaled_two = scatter_rows(mine, other)
    grad_hidden = cotangent + rms_back(scaled_two, normal_two, inverse_two)
    grad_block = grad_hidden.astype(BF)
    grad_blocks = [grad_block] + [swap_with(grad_block, "y", m) for m in (1, 2, 3)]
    two_parts = feed_grads(info, grad_rows, rows_two, active, grad_gate_up)
    grad_blocks, two_parts = lax.optimization_barrier((grad_blocks, two_parts))
    grad_rows_mine = jnp.concatenate(grad_blocks)
    grad_rows_one = (grad_rows_mine, swap_with(grad_rows_mine, "core", 1))
    two_parts = [two_parts[0]] + [swap_with(two_parts[m], "x", m) for m in (1, 2, 3)]

    grad_raw, query_part, *key_value_grads = attention_back(
        info,
        query,
        *grad_rows_one,
        weight_full,
        attended,
        sums,
        raw,
        cosine,
        sine,
        gains,
        key_parts,
        value_parts,
    )
    key_value_grads, two_parts = lax.optimization_barrier((key_value_grads, two_parts))
    key_grads, value_grads = key_value_grads[:5], key_value_grads[5:]
    forwarded = forward_parts(
        key_grads[1],
        key_grads[2],
        swap_with(key_grads[3], "z", NEIGHBOURS["z"][0]),
        swap_with(key_grads[4], "z", NEIGHBOURS["z"][1]),
        value_grads[1],
        value_grads[2],
        swap_with(value_grads[3], "x", NEIGHBOURS["x"][0]),
        swap_with(value_grads[4], "x", NEIGHBOURS["x"][1]),
    )
    early = early_grads(info, rows_one, grad_rows_one, grad_raw, attended)
    summed = sum_parts(
        key_grads[0],
        swap_with(forwarded[0], "z", NEIGHBOURS["z"][0]),
        swap_with(forwarded[1], "z", NEIGHBOURS["z"][1]),
        value_grads[0],
        swap_with(forwarded[2], "x", NEIGHBOURS["x"][0]),
        swap_with(forwarded[3], "x", NEIGHBOURS["x"][1]),
    )
    early, summed = lax.optimization_barrier((early, summed))
    key_grads = [summed[0]] + [swap_with(summed[m], "x", m) for m in (1, 2, 3)]
    value_grads = [summed[4]] + [swap_with(summed[4 + m], "z", m) for m in (1, 2, 3)]
    early = [early[0]] + [swap_with(early[m], "x", m) for m in (1, 2, 3)]

    mine, other, *late = last_step(
        info,
        rows_one,
        weight_full,
        grad_raw,
        query_part,
        raw,
        cosine,
        sine,
        gains,
        *key_grads,
        *value_grads,
        mine_down,
        other_down,
    )
    mine, other, late, early = lax.optimization_barrier((mine, other, late, early))
    late = [late[0]] + [swap_with(late[m], "x", m) for m in (1, 2, 3)]
    totals = [
        sum(part.astype(F32) for part in parts).astype(BF) for parts in (two_parts, early, late)
    ]
    received = swap_with(other, "core", 1)
    halves = [
        jnp.concatenate([v[m * 64 : (m + 1) * 64] for v in totals], axis=1) for m in range(4)
    ]
    parts = [
        mine[m * 64 : (m + 1) * 64].astype(F32) + received[m * 64 : (m + 1) * 64].astype(F32)
        for m in range(4)
    ]
    halves, parts = lax.optimization_barrier((halves, parts))
    own = sum(chunk_along_z(halves[m], m).astype(F32) for m in range(4))
    both = scatter_axis(parts, "y")
    output = hidden + both[:, 1024:]
    token_grad = grad_hidden + rms_back(both[:, :1024], normal_one, inverse_one)
    both = exchange_runs(jnp.concatenate([output.astype(BF), token_grad.astype(BF)], axis=1))
    output, token_grad = both[:, :1024], both[:, 1024:].astype(F32)

    gate_part, up_part, down_part = own[:, :384], own[:, 384:768], own[:, 768:1152]
    query_part, output_part = own[:, 1152:1408], own[:, 1408:1664]
    key_part, value_part = own[:, 1664:1792], own[:, 1792:1920]
    attn_part = (
        jnp.sum(query_part * query_weight.astype(F32), axis=1)
        + jnp.sum(key_part * key_matrix.astype(F32), axis=1)
        + jnp.sum(value_part * value_matrix.astype(F32), axis=1)
    )
    mlp_part = jnp.sum(
        gate_part * gate_weight.astype(F32) + up_part * up_weight.astype(F32), axis=1
    )
    sums_all = jnp.concatenate([attn_part, mlp_part, own[0, 1920:], own[1, 1920:]])
    received = [swap_with(sums_all, "y", m) for m in (1, 2, 3)]
    for part in received:
        sums_all = sums_all + part
    sums_all = sums_all + swap_with(sums_all, "z", 1)
    gain_parts, head_parts = sums_all[:128], sums_all[128:]
    return (
        output,
        token_grad,
        gain_parts[:64],
        query_part * gain_one,
        key_part * gain_one,
        value_part * gain_one,
        head_parts[:HEAD],
        head_parts[HEAD:],
        output_part.T,
        gain_parts[64:],
        gate_part * gain_two,
        up_part * gain_two,
        down_part.T,
    )


def solution(mesh):
    parts = Mesh(mesh.devices.reshape(4, 2, 2, 2, 4), AXES)
    ctx, tp = ("x", "zl", "core"), ("zh", "y")
    tokens, matrix, turned = P(AXES, None), P(ctx, tp), P(tp, ctx)
    return jax.shard_map(
        local,
        mesh=parts,
        in_specs=(
            tokens,
            P(),
            P(),
            P(ctx),
            matrix,
            matrix,
            matrix,
            P(),
            P(),
            turned,
            P(ctx),
            matrix,
            matrix,
            turned,
            tokens,
        ),
        out_specs=(
            tokens,
            tokens,
            P(ctx),
            matrix,
            matrix,
            matrix,
            P(),
            P(),
            turned,
            P(ctx),
            matrix,
            matrix,
            turned,
        ),
        check_vma=False,
    )
```
